256 devices in a mesh: dp: 8 (over z), seq: 32 (over x, y, core).
Axes of the slice: x: 4, y: 4, z: 8, core: 2. Of those that a mesh axis runs over, the one named last changes fastest.
Arguments:
- tokens: bfloat16 [16, 2048, 768], P('dp', 'seq'), may hold values from -6 to 6
- lengths: int32 [16], P('dp'), may hold values from 128 to 2048, as said below
- w_value: bfloat16 [768, 768], P('seq'), may hold values from -0.21875 to 0.21875
- w_out: bfloat16 [768, 768], P('seq'), may hold values from -0.625 to 0.625
- w_up: bfloat16 [768, 3072], P('seq'), may hold values from -0.21875 to 0.21875
- w_down: bfloat16 [3072, 768], P('seq'), may hold values from -0.109375 to 0.109375
- gain_mix: float32 [768], replicated, may hold values from 0.1 to 1.9
- gain_ffn: float32 [768], replicated, may hold values from 0.1 to 1.9
- mix_table: bfloat16 [12, 2048, 2048], P(None, 'seq'), may hold values from -9 to 9
- out_grad: bfloat16 [16, 2048, 768], P('dp', 'seq'), may hold values from -6 to 6
Outputs:
- output: bfloat16 [16, 2048, 768], P('dp', 'seq')
- input_grad: float32 [16, 2048, 768], P('dp', 'seq')
- value_weight_grad: float32 [768, 768], P('seq')
- out_weight_grad: float32 [768, 768], P('seq')
- up_weight_grad: float32 [768, 3072], P('seq')
- down_weight_grad: float32 [3072, 768], P('seq')
- mix_gain_grad: float32 [768], P('seq')
- ffn_gain_grad: float32 [768], P('seq')
- table_grad: float32 [12, 2048, 2048], P(None, 'seq', 'dp')
The draws below stay inside these ranges and needn't reach their ends.
Inputs may be any that keep to these rules, and one draw needn't show every extreme that they name: `lengths`: within each group of 2 items held by one index of dp, one item, which one drawn from the seed, has length 2048.
All inputs are finite; a program needn't handle non-finite values.
Results may differ from the reference program's by a relative error of at most 0.0095.
Values may be sent and summed in bfloat16 or wider, within the bound.
A program may use at most 128 MiB of HBM per device.

```python
import math
import jax
import jax.numpy as jnp
from jax import lax

D = 768
HEADS = 12
HEAD_DIM = 64
FF = 3072
B_DEV = 2
LEN = 2048
BATCH = 16


def draw_lengths(key, part):
    key = jax.random.fold_in(key, 7)
    short_key, pick_key = jax.random.split(key)
    drawn = jax.random.randint(short_key, (BATCH,), LEN // 16, LEN + 1)
    group_count = BATCH // B_DEV
    chosen = jax.random.randint(pick_key, (group_count,), 0, B_DEV)
    slots = jnp.arange(BATCH)
    full_mask = slots % B_DEV == jnp.repeat(chosen, B_DEV, total_repeat_length=BATCH)
    return jnp.where(full_mask, LEN, drawn).astype(jnp.int32)


def shard_levels(key, dims, cuts, low, high):
    loudness = 1.0
    for axis_at, parts in cuts:
        draws = jax.random.uniform(jax.random.fold_in(jax.random.fold_in(key, 6), axis_at), (parts,), jnp.float32, low / len(cuts), high / len(cuts))
        loudness = loudness * jnp.repeat(jnp.exp(draws), dims[axis_at] // parts).reshape((-1,) + (1,) * (len(dims) - 1 - axis_at))
    return loudness


def normal_values(own_key, extent, scale, reach, shards=(), kind=jnp.bfloat16):
    values = jax.random.normal(own_key, extent, jnp.float32) * scale
    if len(shards) > 0:
        values = shard_levels(own_key, extent, shards, -0.22, 0.18) * values
    return jnp.clip(values, min=-reach, max=reach).astype(kind)


def setup_inputs(seed: int = 0) -> dict:
    keys = jax.random.split(jax.random.key(seed), 11)
    return {
        "tokens": normal_values(keys[0], (BATCH, LEN, D), 1.0, 6.0, ((0, 8), (1, 32))),
        "lengths": draw_lengths(jax.random.fold_in(keys[10], 71), 0),
        "w_value": normal_values(keys[2], (D, D), D ** -0.5, 0.21875, ((0, 32),)),
        "w_out": normal_values(keys[3], (D, D), (D // 8) ** -0.5, 0.625, ((0, 32),)),
        "w_up": normal_values(keys[4], (D, FF), D ** -0.5, 0.21875, ((0, 32),)),
        "w_down": normal_values(keys[5], (FF, D), FF ** -0.5, 0.109375, ((0, 32),)),
        "gain_mix": jnp.clip(1.0 + 0.18 * jax.random.normal(keys[6], (D,), jnp.float32), 0.1, 1.9),
        "gain_ffn": jnp.clip(1.0 + 0.18 * jax.random.normal(keys[7], (D,), jnp.float32), 0.1, 1.9),
        "mix_table": normal_values(keys[8], (HEADS, LEN, LEN), 1.5, 9.0, ((1, 32),)),
        "out_grad": normal_values(keys[9], (BATCH, LEN, D), 1.0, 6.0, ((0, 8), (1, 32))),
    }


@jax.custom_vjp
def low(v):
    return lax.optimization_barrier(v.astype(jnp.bfloat16)).astype(jnp.float32)

@jax.custom_vjp
def low_back(v):
    return v

def low_keep(v):
    return (low(v), None)

def low_pass(kept, grad):
    return (grad,)

def back_keep(v):
    return (v, None)

def back_low(kept, grad):
    return (low(grad),)
low.defvjp(low_keep, low_pass)
low_back.defvjp(back_keep, back_low)
EPS = 1e-06
HIGH = lax.Precision.HIGHEST

def rms_norm(value, gain):
    scale = lax.rsqrt(lax.optimization_barrier(jnp.mean(value * value, axis=-1, keepdims=True)) + EPS)
    return value * scale * gain

def project(value, weight):
    return jnp.einsum('gld,de->gle', value, weight, precision=HIGH)

def mix_item(mix_table, values, length):
    places = jnp.arange(LEN)
    valid_pos = places < length
    valid_pair = valid_pos[:, None] & valid_pos[None, :]
    head_values = jnp.transpose(values.reshape(LEN, HEADS, HEAD_DIM), (1, 0, 2))

    def one_head(operands):
        table_block, head_vals = operands
        scores = jnp.transpose(table_block)
        masked = jnp.where(valid_pos[None, :], scores, -1e+30)
        row_top = lax.optimization_barrier(jnp.max(masked, axis=1, keepdims=True))
        exponent = jnp.where(valid_pos[None, :], jnp.exp(masked - row_top), 0.0)
        row_total = lax.optimization_barrier(jnp.sum(exponent, axis=1, keepdims=True))
        weights = low(jnp.where(valid_pair, exponent / row_total, 0.0))
        return jnp.dot(weights, head_vals, precision=HIGH)
    per_head = lax.map(jax.checkpoint(one_head), (mix_table, head_values))
    return jnp.transpose(per_head, (1, 0, 2)).reshape(LEN, HEADS * HEAD_DIM)

def layer(params, tokens, lengths):
    w_value, w_out, w_up, w_down, gain_mix, gain_ffn, mix_table = params
    normed = low(rms_norm(tokens, gain_mix))
    values = low_back(low(project(normed, w_value)))
    mixed = jax.vmap(lambda item_vals, item_len: mix_item(mix_table, item_vals, item_len))(values, lengths)
    mixed = low_back(low(mixed))
    middle = tokens + low_back(project(mixed, w_out))
    normed_ffn = low(rms_norm(middle, gain_ffn))
    hidden_pre = low_back(project(normed_ffn, w_up))
    hidden = low(jax.nn.gelu(hidden_pre))
    return low(middle + project(hidden, w_down))

def reference(tokens, lengths, w_value, w_out, w_up, w_down, gain_mix, gain_ffn, mix_table, out_grad):
    params = tuple((member.astype(jnp.float32) for member in (w_value, w_out, w_up, w_down, gain_mix, gain_ffn, mix_table)))
    group_size = math.gcd(BATCH, max(1, 4096 // LEN))
    step_count = BATCH // group_size
    block_data = (tokens.astype(jnp.float32).reshape(step_count, group_size, LEN, D), lengths.reshape(step_count, group_size), out_grad.astype(jnp.float32).reshape(step_count, group_size, LEN, D))
    zero_grads = jax.tree.map(jnp.zeros_like, params)

    def advance(running, block_in):
        block_tokens, block_len, block_grad = block_in
        result, pullback = jax.vjp(lambda weights, inputs: layer(weights, inputs, block_len), params, block_tokens)
        weight_grads, input_grad = pullback(block_grad)
        return (jax.tree.map(jnp.add, running, weight_grads), (result, input_grad))
    sums, (results, input_grads) = lax.scan(advance, zero_grads, block_data)
    output = results.reshape(BATCH, LEN, D).astype(jnp.bfloat16)
    input_grad = input_grads.reshape(BATCH, LEN, D)
    return (output, input_grad, sums[0], sums[1], sums[2], sums[3], sums[4], sums[5], sums[6])
```

```python
import jax
import jax.numpy as jnp
from jax import lax
from jax.experimental import pallas as pl
from jax.experimental.pallas import tpu as pltpu
from jax.sharding import PartitionSpec as P

D = 768
HALF = 384
HEADS = 12
HH = 6
EPS = 1e-06
MESH = pl.DeviceIdType.MESH
BF = jnp.bfloat16
F32 = jnp.float32
OFFS = (1, 3, 2)
ROWS = 144
GELU_C = 0.7978845608028654
GELU_A = 0.044715


def here():
    s = lax.axis_index("seq")
    return lax.axis_index("dp"), s // 8, (s // 2) % 4, s % 2


def at(z, x, y, c):
    return (z, (x * 4 + y) * 2 + c)


def remote(src, dst, sems, idx, device):
    return pltpu.make_async_remote_copy(
        src_ref=src,
        dst_ref=dst,
        send_sem=sems.at[(0,) + idx],
        recv_sem=sems.at[(1,) + idx],
        device_id=device,
        device_id_type=MESH,
    )


def along(first, k):
    z, x, y, c = here()
    if first == "x":
        return at(z, lax.rem(x + k, 4), y, c)
    return at(z, x, lax.rem(y + k, 4), c)


OTHER = {"x": "y", "y": "x"}


def own_at(first):
    _, x, y, _ = here()
    return x if first == "x" else y


def gather_one(buf, first, sems):
    _, x, y, _ = here()
    return [
        remote(buf.at[x, y], buf.at[x, y], sems, (0, i), along(first, k))
        for i, k in enumerate(OFFS)
    ]


def gather_two(buf, first, sems):
    _, x, y, _ = here()
    view = buf.at[:, y] if first == "x" else buf.at[x]
    return [
        remote(view, view, sems, (1, i), along(OTHER[first], k)) for i, k in enumerate(OFFS)
    ]


def scatter_one(src, rcv, first, sems):
    mine = own_at(first)
    out = []
    for i, k in enumerate(OFFS):
        to = lax.rem(mine + k, 4)
        part = src.at[to] if first == "x" else src.at[:, to]
        out.append(remote(part, rcv.at[mine], sems, (0, i), along(first, k)))
    return out


def scatter_sum(src, rcv, mid, first):
    mine = own_at(first)
    for j in range(4):
        own = src[mine, j] if first == "x" else src[j, mine]
        total = own.astype(F32)
        for k in OFFS:
            total = total + rcv[lax.rem(mine + k, 4), j].astype(F32)
        mid[j] = total.astype(BF)


def scatter_two(mid, rcv, first, sems):
    second = OTHER[first]
    mine = own_at(second)
    return [
        remote(mid.at[lax.rem(mine + k, 4)], rcv.at[mine], sems, (1, i), along(second, k))
        for i, k in enumerate(OFFS)
    ]


def scatter_end(mid, rcv, first):
    mine = own_at(OTHER[first])
    total = mid[mine].astype(F32)
    for k in OFFS:
        total = total + rcv[lax.rem(mine + k, 4)].astype(F32)
    return total


def start(copies):
    for copy in copies:
        copy.start()


def wait_recv(copies):
    for copy in copies:
        copy.wait_recv()


def wait_send(copies):
    for copy in copies:
        copy.wait_send()


def signal(device):
    pl.semaphore_signal(
        pltpu.get_barrier_semaphore(), inc=1, device_id=device, device_id_type=MESH
    )


def meet(with_z):
    z, x, y, c = here()
    count = 0
    for k in range(1, 4):
        signal(at(z, lax.rem(x + k, 4), y, c))
        signal(at(z, x, lax.rem(y + k, 4), c))
        count += 2
    signal(at(z, x, y, 1 - c))
    count += 1
    if with_z:
        for k in range(1, 8):
            signal(at(lax.rem(z + k, 8), x, y, c))
            count += 1
    pl.semaphore_wait(pltpu.get_barrier_semaphore(), count)


def dot(a, b):
    return jnp.dot(a, b, preferred_element_type=F32)


def dot_nt(a, b):
    return lax.dot_general(a, b, (((1,), (1,)), ((), ())), preferred_element_type=F32)


def flip(a):
    return jnp.transpose(a)


def rms_of(v):
    return lax.rsqrt(jnp.mean(v * v, axis=-1, keepdims=True) + EPS)


def front(
    tokens, out_grad, pre, w_down, table, mask, gain_mix, gain_ffn,
    out, mgrad, gch, vals, e_out, normed, tok_o, wv_o, dwu, dwd, dwo, gain_o,
    pre_s, tok, og, tab, wv, wo_all, wu0, wu1, wd0, wd1,
    ux, uy, rx, ry, mx, my, rx2, ry2, mt, rr, mix, vt, middle, nf, hid, pgr, act, part, part_r, fng, fng_r,
    s_sib, s_ag, s_u, s_loc,
):
    z, x, y, c = here()
    sib = at(z, x, y, 1 - c)
    wo = wo_all.at[c]
    meet(False)

    def to_sib(src, dst, i):
        return remote(src, dst, s_sib, (i,), sib)

    swap_pre = to_sib(pre.at[1 - c], pre_s.at[c], 0)
    swap_tok = to_sib(tokens, tok.at[:, c], 1)
    swap_tab = to_sib(table.at[pl.ds(6 * (1 - c), 6)], tab.at[:, c], 2)
    swap_og = to_sib(out_grad, og.at[:, c], 3)
    own_tab = pltpu.make_async_copy(table.at[pl.ds(6 * c, 6)], tab.at[:, c], s_loc)
    start([swap_pre, swap_tok, swap_tab, own_tab, swap_og])
    pre_s[c] = pre[c]
    tok[:, c] = tokens[...]
    og[:, c] = out_grad[...]
    wd0[x, y] = w_down[0:48]
    wd1[x, y] = w_down[48:96]
    swap_pre.wait_recv()
    shard = pre_s[...].reshape(48, 2304).astype(BF)
    wv[x, y] = shard[:, 0:HALF]
    wo[x, y] = shard[:, HALF:D]
    wu0[x, y] = shard[:, D : 2 * D]
    wu1[x, y] = shard[:, 2 * D : 3 * D]
    bufs = ((wv, "x"), (wo, "y"), (wu0, "x"), (wu1, "y"), (wd0, "x"), (wd1, "y"))
    g1 = [gather_one(buf, first, s_ag.at[:, i]) for i, (buf, first) in enumerate(bufs)]
    g2 = [gather_two(buf, first, s_ag.at[:, i]) for i, (buf, first) in enumerate(bufs)]
    for i in range(6):
        start(g1[i])
    swap_tok.wait_recv()
    values = tok[...].reshape(256, D).astype(F32)
    normed[...] = (values * rms_of(values) * gain_mix[...]).astype(BF)
    tok_o[...] = tok[...]
    for i in range(2):
        wait_recv(g1[i])
        start(g2[i])
    swap_tab.wait_recv()
    own_tab.wait()

    def exps(h, carry):
        e_out[h] = jnp.exp(tab[h].reshape(128, 2048).astype(F32)).astype(BF)
        return carry

    lax.fori_loop(0, HH, exps, 0)
    wait_recv(g2[0])
    wv_o[...] = wv[...].reshape(D, HALF)
    v = dot(normed[...], wv_o[...]).astype(BF).astype(F32)
    lane_mask = jnp.concatenate([mask[0:1], mask[1:2]], axis=1)
    vall = flip(v) * lane_mask
    ones = jnp.concatenate([mask[...], jnp.zeros((8, 128), F32)], axis=0)
    for h in range(HH):
        block = jnp.concatenate(
            [vall[64 * h : 64 * h + 64, 0:128], vall[64 * h : 64 * h + 64, 128:256]], axis=0
        )
        vt[h] = jnp.concatenate([block, ones], axis=0).astype(BF)
        vals[h] = flip(block).astype(BF)

    s1x = scatter_one(ux, rx, "x", s_u.at[:, 0])
    s1y = scatter_one(uy, ry, "y", s_u.at[:, 1])
    for i, k in enumerate(OFFS + (0,)):
        xx = lax.rem(x + k, 4)
        yy = lax.rem(y + k, 4)

        def head_x(h, carry, xx=xx):
            u = dot(vt[h], e_out[h, :, pl.ds(pl.multiple_of(512 * xx, 512), 512)])
            for j in range(4):
                ux[xx, j, h] = u[:, 128 * j : 128 * j + 128].astype(BF)
            return carry

        def head_y(h, carry, yy=yy):
            for j in range(4):
                cols = pl.ds(pl.multiple_of(512 * j + 128 * yy, 128), 128)
                uy[j, yy, h] = dot(vt[h + 3], e_out[h + 3, :, cols]).astype(BF)
            return carry

        lax.fori_loop(0, 3, head_x, 0)
        if i < 3:
            s1x[i].start()
        lax.fori_loop(0, 3, head_y, 0)
        if i < 3:
            s1y[i].start()
    for i in (2, 3):
        wait_recv(g1[i])
        start(g2[i])
    wait_recv(g2[1])
    swap_wo = to_sib(wo, wo, 4)
    swap_wo.start()
    s2x = scatter_two(mx, rx2, "x", s_u.at[:, 0])
    s2y = scatter_two(my, ry2, "y", s_u.at[:, 1])
    wait_recv(s1x)
    scatter_sum(ux, rx, mx, "x")
    start(s2x)
    wait_recv(s1y)
    scatter_sum(uy, ry, my, "y")
    start(s2y)
    for i in (4, 5):
        wait_recv(g1[i])
        start(g2[i])

    for half, (copies, mid, rcv, first) in enumerate(((s2x, mx, rx2, "x"), (s2y, my, ry2, "y"))):
        wait_recv(copies)
        total = scatter_end(mid, rcv, first)
        for hh in range(3):
            h = half * 3 + hh
            for b in range(2):
                r = mask[b : b + 1] / total[hh, 128 + b : 129 + b]
                rr[b, h : h + 1] = r
                mt[b, 64 * h : 64 * h + 64] = total[hh, 64 * b : 64 * b + 64] * r
    for b in range(2):
        mix[c, b] = flip(mt[b]).astype(BF)
    swap_mix = to_sib(mix.at[c], mix.at[c], 5)
    swap_mix.start()
    swap_wo.wait_recv()
    swap_mix.wait_recv()
    mixed = [mix[i].reshape(256, HALF) for i in range(2)]
    for cc in range(2):
        w = wo_all[cc].reshape(D, HALF)
        cols = slice(HALF * cc, HALF * cc + HALF)
        middle[:, cols] = (
            tok[...].reshape(256, D)[:, cols].astype(F32)
            + dot(mixed[0], w[0:HALF])
            + dot(mixed[1], w[HALF:D])
        )
    mid_v = middle[...]
    rms = rms_of(mid_v)
    nf[...] = (mid_v * rms * gain_ffn[...]).astype(BF)
    nft = flip(nf[...])
    swap_og.wait_recv()
    grad = og[...].reshape(256, D)
    for hf, (up, down) in enumerate(((wu0, wd0), (wu1, wd1))):
        wait_recv(g2[2 + hf])
        hp = dot(nf[...], up[...].reshape(D, D))
        t = jnp.tanh(GELU_C * (hp + GELU_A * hp * hp * hp))
        hid[hf] = (0.5 * hp * (1.0 + t)).astype(BF)
        act[hf] = 0.5 * (1.0 + t) + 0.5 * hp * (1.0 - t * t) * (
            GELU_C * (1.0 + 3.0 * GELU_A * hp * hp)
        )
    for hf, (up, down) in enumerate(((wu0, wd0), (wu1, wd1))):
        wait_recv(g2[4 + hf])
        w = down[...].reshape(D, D)
        pgr[hf] = (act[hf] * dot_nt(grad, w)).astype(BF)
        more = dot_nt(pgr[hf], up[...].reshape(D, D)).reshape(2, 2, 64, D)
        fng[...] = more if hf == 0 else fng[...] + more
    swap_fng = to_sib(fng, fng_r, 6)
    swap_fng.start()
    for hf, (up, down) in enumerate(((wu0, wd0), (wu1, wd1))):
        more = dot(hid[hf], down[...].reshape(D, D)).reshape(2, 2, 64, D)
        part[...] = more if hf == 0 else part[...] + more
    swap_part = to_sib(part.at[:, 1 - c], part_r, 7)
    swap_part.start()
    for hf in range(2):
        dwu[hf] = dot(nft, pgr[hf]).astype(BF).reshape(4, 4, 48, D)
        dwd[hf] = dot(flip(hid[hf]), grad).astype(BF).reshape(4, 4, 48, D)
    swap_fng.wait_recv()
    full = (fng[...] + fng_r[...]).reshape(256, D)
    mid_v = middle[...]
    rms = rms_of(mid_v)
    gain_o[...] = jnp.sum(full * mid_v * rms, axis=0, keepdims=True)
    weighted = full * gain_ffn[...]
    inner = jnp.mean(weighted * mid_v, axis=-1, keepdims=True)
    mg = grad.astype(F32) + rms * weighted - mid_v * (rms * rms * rms) * inner
    swap_fng.wait_send()
    fng[...] = mg.reshape(2, 2, 64, D)
    bg = mg.astype(BF)
    nf[...] = bg
    mgrad[...] = fng[:, c]
    swap_part.wait_recv()
    fng_r[...] = middle[...].reshape(2, 2, 64, D)
    out[...] = (fng_r[:, c] + (part[:, c] + part_r[...])).astype(BF)
    cols = pl.ds(pl.multiple_of(HALF * c, 128), HALF)
    bg_c = nf[:, cols]
    for i in range(2):
        dwo[i] = dot(flip(mixed[i]), bg_c).astype(BF).reshape(2, 4, 48, HALF)
    xg = jnp.zeros((256, HALF), F32)
    for cc in range(2):
        w = wo_all[cc, pl.ds(2 * c, 2)].reshape(HALF, HALF)
        xg = xg + dot_nt(bg[:, HALF * cc : HALF * cc + HALF], w)
    for b in range(2):
        xgt = flip(xg[128 * b : 128 * b + 128])
        for h in range(HH):
            rows = xgt[64 * h : 64 * h + 64]
            r = rr[b, h : h + 1]
            delta = jnp.sum(rows * mt[b, 64 * h : 64 * h + 64], axis=0, keepdims=True) * r
            gch[h, 64 * b : 64 * b + 64] = (rows * r).astype(BF)
            mt[b, 64 * h : 64 * h + 1] = delta
    for h in range(HH):
        d0 = mt[0, 64 * h : 64 * h + 1]
        d1 = mt[1, 64 * h : 64 * h + 1]
        h0 = d0.astype(BF).astype(F32)
        h1 = d1.astype(BF).astype(F32)
        gch[h, 128:144] = jnp.concatenate(
            [h0, h1, d0 - h0, d1 - h1, jnp.zeros((12, 128), F32)], axis=0
        ).astype(BF)
    swap_pre.wait_send()
    swap_tok.wait_send()
    swap_tab.wait_send()
    swap_og.wait_send()
    swap_wo.wait_send()
    swap_mix.wait_send()
    swap_part.wait_send()
    for group in g1 + g2 + [s1x, s1y, s2x, s2y]:
        wait_send(group)


def back(
    gch, vals, e, mask, mask_cols, normed, tok, wv, dwu, dwd, dwo, gain_f, gain_mix, mgrad,
    tg, input_grad, res,
    gx, gy, ru, ru2, mu, rl, rl2, ml, dwv, gs, gr, up_s, up_r, dn_s, dn_r, tgf, tg_r, vgt, ng, ng_r, ig, sums, zr, zs, zf,
    s_g, s_w, s_l, s_gain, s_up, s_dn, s_sib, s_z,
):
    z, x, y, c = here()
    sib = at(z, x, y, 1 - c)
    up = at(lax.rem(z + 1, 8), x, y, c)
    down = at(lax.rem(z + 7, 8), x, y, c)
    meet(True)
    gx[x, y] = gch[0:3]
    gy[x, y] = gch[3:6]
    a1x = gather_one(gx, "x", s_g.at[:, 0])
    a1y = gather_one(gy, "y", s_g.at[:, 1])
    a2x = gather_two(gx, "x", s_g.at[:, 0])
    a2y = gather_two(gy, "y", s_g.at[:, 1])
    start(a1x)
    start(a1y)
    wait_recv(a1x)
    start(a2x)
    wait_recv(a1y)
    start(a2y)
    lots = ((dwu.at[0], "x"), (dwu.at[1], "y"), (dwd.at[0], "x"), (dwd.at[1], "y"))
    w1 = [scatter_one(src, ru.at[i], first, s_w.at[:, i]) for i, (src, first) in enumerate(lots)]
    w2 = [scatter_two(mu.at[i], ru2.at[i], first, s_w.at[:, i]) for i, (_, first) in enumerate(lots)]
    l1o = scatter_one(dwo, rl.at[0], "x", s_l.at[:, 0])
    for group in w1:
        start(group)
    start(l1o)
    wait_recv(a2x)
    wait_recv(a2y)

    def table_part(d, hf):
        buf = gx if hf == 0 else gy
        out = []
        for hh in range(3):
            h = 3 * hf + hh
            row = []
            for i in range(2):
                k = 2 * d + i
                g = buf[k // 4, lax.rem(k, 4), hh]
                cols = pl.ds(pl.multiple_of(256 * d + 128 * i, 128), 128)
                extra = g[128:144].astype(F32)
                s = dot(vals[h], g[0:128])
                s = s - mask_cols[0] * (extra[0:1] + extra[2:3])
                s = s - mask_cols[1] * (extra[1:2] + extra[3:4])
                row.append(s * e[h, :, cols].astype(F32))
            out.append(jnp.concatenate(row, axis=1))
        return out

    def ring(send, recv, sems, t, hf, device):
        return remote(send.at[t, hf], recv.at[t, hf], sems, (t, hf), device)

    ups = [[ring(up_s, up_r, s_up, t, hf, up) for hf in range(2)] for t in range(4)]
    dns = [[ring(dn_s, dn_r, s_dn, t, hf, down) for hf in range(2)] for t in range(3)]

    def step(t):
        for copies, send, recv, d in (
            (ups, up_s, up_r, lax.rem(z + 4 - t, 8)),
            (dns, dn_s, dn_r, lax.rem(z + 5 + t, 8)),
        ):
            if t == 3 and copies is dns:
                continue
            for hf in range(2):
                if t > 0:
                    copies[t - 1][hf].wait_recv()
                parts = table_part(d, hf)
                for hh in range(3):
                    p = parts[hh]
                    if t > 0:
                        p = p + recv[t - 1, hf, hh].astype(F32)
                    send[t, hf, hh] = p.astype(BF)
                copies[t][hf].start()

    step(0)
    for h in range(HH):
        buf = gx if h < 3 else gy
        total = jnp.zeros((128, 128), F32)
        for k in range(16):
            total = total + dot_nt(buf[k // 4, k % 4, h % 3, 0:128], e[h, :, 128 * k : 128 * k + 128])
        for b in range(2):
            vgt[b, 64 * h : 64 * h + 64] = total[64 * b : 64 * b + 64] * mask[b : b + 1]
    vg = jnp.concatenate([flip(vgt[b]) for b in range(2)], axis=0).astype(BF)
    dwv[...] = dot(flip(normed[...]), vg).astype(BF).reshape(4, 4, 48, HALF)
    l1v = scatter_one(dwv, rl.at[1], "y", s_l.at[:, 1])
    start(l1v)
    part = dot_nt(vg, wv[...])
    ig[...] = part
    swap_ng = remote(ig, ng_r, s_sib, (0,), sib)
    swap_ng.start()
    step(1)
    swap_ng.wait_recv()
    full = ig[...] + ng_r[...]
    xv = tok[...].reshape(256, D).astype(F32)
    rms = rms_of(xv)
    gain_m = jnp.sum(full * xv * rms, axis=0, keepdims=True)
    weighted = full * gain_mix[...]
    inner = jnp.mean(weighted * xv, axis=-1, keepdims=True)
    ng[...] = (rms * weighted - xv * (rms * rms * rms) * inner).reshape(2, 2 * 64, D)
    input_grad[...] = mgrad[...] + ng[:, pl.ds(pl.multiple_of(64 * c, 64), 64)]
    gains = jnp.concatenate([gain_f[...], gain_m], axis=0)
    high = gains.astype(BF).astype(F32)
    gs[...] = jnp.concatenate([high, gains - high, jnp.zeros((12, D), F32)], axis=0).astype(BF)
    gr[x, y] = gs[...]
    gain1 = gather_one(gr, "x", s_gain)
    gain2 = gather_two(gr, "x", s_gain)
    start(gain1)
    for i, (src, first) in enumerate(lots):
        wait_recv(w1[i])
        scatter_sum(src, ru.at[i], mu.at[i], first)
        start(w2[i])
    step(2)
    l2 = [
        scatter_two(ml.at[0], rl2.at[0], "x", s_l.at[:, 0]),
        scatter_two(ml.at[1], rl2.at[1], "y", s_l.at[:, 1]),
    ]
    wait_recv(l1o)
    scatter_sum(dwo, rl.at[0], ml.at[0], "x")
    start(l2[0])
    wait_recv(l1v)
    scatter_sum(dwv, rl.at[1], ml.at[1], "y")
    start(l2[1])
    wait_recv(gain1)
    start(gain2)
    step(3)
    for i, (src, first) in enumerate(lots):
        wait_recv(w2[i])
        sums[48 * i : 48 * i + 48] = scatter_end(mu.at[i], ru2.at[i], first).astype(BF)
    wait_recv(l2[0])
    sums[192:240, 0:HALF] = scatter_end(ml.at[0], rl2.at[0], "x").astype(BF)
    wait_recv(l2[1])
    sums[192:240, HALF:D] = scatter_end(ml.at[1], rl2.at[1], "y").astype(BF)
    wait_recv(gain2)
    gsum = gr[...].reshape(16, 16, D).astype(F32)
    gtot = jnp.sum(gsum, axis=0)
    gains = gtot[0:2] + gtot[2:4]
    high = gains.astype(BF).astype(F32)
    sums[240:256] = jnp.concatenate([high, gains - high, jnp.zeros((12, D), F32)], axis=0).astype(BF)
    z1 = [
        remote(
            sums.at[pl.ds(pl.multiple_of(32 * lax.rem(z + k, 8), 32), 32)],
            zr.at[z], s_z, (0, k), at(lax.rem(z + k, 8), x, y, c),
        )
        for k in range(1, 8)
    ]
    start(z1)
    own = table_part(z, 0) + table_part(z, 1)
    for hf in range(2):
        ups[3][hf].wait_recv()
        dns[2][hf].wait_recv()
        for hh in range(3):
            p = own[3 * hf + hh] + (
                up_r[3, hf, hh].astype(F32) + dn_r[2, hf, hh].astype(F32)
            )
            tgf[3 * hf + hh] = p.reshape(2, 64, 256)
    swap_tg = remote(tgf.at[:, 1 - c], tg_r, s_sib, (1,), sib)
    swap_tg.start()
    mine = sums[pl.ds(pl.multiple_of(32 * z, 32), 32)].astype(F32)
    wait_recv(z1)
    for k in range(1, 8):
        mine = mine + zr[lax.rem(z + k, 8)].astype(F32)
    zs[z] = mine.astype(BF)
    z2 = [
        remote(zs.at[z], zs.at[z], s_z, (1, k), at(lax.rem(z + k, 8), x, y, c))
        for k in range(1, 8)
    ]
    start(z2)
    tg[c] = tgf[:, c]
    swap_tg.wait_recv()
    tg[1 - c] = tg_r[...]
    wait_recv(z2)
    zf[c] = zs[...]
    swap_res = remote(zs, zf.at[c], s_sib, (2,), sib)
    swap_res.start()
    swap_res.wait_recv()
    res[...] = zf[...].reshape(2, 256, D)
    for group in [a1x, a1y, a2x, a2y, l1o, l1v, gain1, gain2, z1, z2] + w1 + w2 + l2 + ups + dns:
        wait_send(group)
    swap_ng.wait_send()
    swap_tg.wait_send()
    swap_res.wait_send()


def vmem(shape, kind=BF):
    return pltpu.VMEM(shape, kind)


def dma(*shape):
    return pltpu.SemaphoreType.DMA(shape)


IN_VMEM = pl.BlockSpec(memory_space=pltpu.VMEM)


def per_device(tokens, lengths, w_value, w_out, w_up, w_down, gain_mix, gain_ffn, mix_table, out_grad):
    s = lax.axis_index("seq")
    c = s % 2
    positions = (s // 2) * 128 + jnp.arange(128)
    ok = (positions[None, :] < lengths[:, None]).astype(F32)
    mask = jnp.concatenate([ok, jnp.zeros((6, 128), F32)], axis=0)
    mask_cols = jnp.broadcast_to(ok[:, :, None], (2, 128, 128))
    pre = jnp.concatenate(
        [
            w_value.reshape(24, 2, HALF).transpose(1, 0, 2),
            w_out.reshape(24, 2, HALF).transpose(1, 0, 2),
            w_up.reshape(24, 16, 2, 2, 48).transpose(2, 0, 3, 1, 4).reshape(2, 24, 1536),
        ],
        axis=2,
    ).astype(F32)
    sd = jax.ShapeDtypeStruct
    outs = pl.pallas_call(
        front,
        name="front",
        out_shape=[
            sd((2, 64, D), BF), sd((2, 64, D), F32), sd((HH, ROWS, 128), BF), sd((HH, 128, 128), BF),
            sd((HH, 128, 2048), BF), sd((256, D), BF), sd((2, 2, 64, D), BF), sd((D, HALF), BF),
            sd((2, 4, 4, 48, D), BF), sd((2, 4, 4, 48, D), BF), sd((2, 2, 4, 48, HALF), BF), sd((1, D), F32),
        ],
        in_specs=[IN_VMEM] * 4 + [pl.BlockSpec(memory_space=pl.ANY)] + [IN_VMEM] * 3,
        out_specs=[IN_VMEM] * 12,
        scratch_shapes=[
            vmem((2, 24, 2304), F32), vmem((2, 2, 64, D)), vmem((2, 2, 64, D)), vmem((HH, 2, 64, 2048)),
            vmem((4, 4, 48, HALF)), vmem((2, 4, 4, 48, HALF)),
            vmem((4, 4, 48, D)), vmem((4, 4, 48, D)), vmem((4, 4, 48, D)), vmem((4, 4, 48, D)),
            vmem((4, 4, 3, ROWS, 128)), vmem((4, 4, 3, ROWS, 128)),
            vmem((4, 4, 3, ROWS, 128)), vmem((4, 4, 3, ROWS, 128)),
            vmem((4, 3, ROWS, 128)), vmem((4, 3, ROWS, 128)), vmem((4, 3, ROWS, 128)), vmem((4, 3, ROWS, 128)),
            vmem((2, HALF, 128), F32), vmem((2, 8, 128), F32), vmem((2, 2, 128, HALF)), vmem((HH, ROWS, 128)),
            vmem((256, D), F32), vmem((256, D)), vmem((2, 256, D)), vmem((2, 256, D)), vmem((2, 256, D), F32),
            vmem((2, 2, 64, D), F32), vmem((2, 64, D), F32), vmem((2, 2, 64, D), F32), vmem((2, 2, 64, D), F32),
            dma(2, 8), dma(2, 6, 2, 3), dma(2, 2, 2, 3), pltpu.SemaphoreType.DMA,
        ],
        compiler_params=pltpu.CompilerParams(
            collective_id=0, has_side_effects=True, vmem_limit_bytes=60 << 20
        ),
    )(tokens, out_grad, pre, w_down, mix_table, mask, gain_mix.reshape(1, D), gain_ffn.reshape(1, D))
    out, mgrad, gch, vals, e, normed, tok, wv, dwu, dwd, dwo, gain_f = outs
    tg, input_grad, res = pl.pallas_call(
        back,
        name="back",
        out_shape=[sd((2, HH, 64, 256), F32), sd((2, 64, D), F32), sd((2, 256, D), BF)],
        in_specs=[IN_VMEM] * 14,
        out_specs=[IN_VMEM] * 3,
        scratch_shapes=[
            vmem((4, 4, 3, ROWS, 128)), vmem((4, 4, 3, ROWS, 128)),
            vmem((4, 4, 4, 48, D)), vmem((4, 4, 48, D)), vmem((4, 4, 48, D)),
            vmem((2, 4, 4, 48, HALF)), vmem((2, 4, 48, HALF)), vmem((2, 4, 48, HALF)), vmem((4, 4, 48, HALF)),
            vmem((16, D)), vmem((4, 4, 16, D)),
            vmem((4, 2, 3, 128, 256)), vmem((4, 2, 3, 128, 256)), vmem((3, 2, 3, 128, 256)), vmem((3, 2, 3, 128, 256)),
            vmem((HH, 2, 64, 256), F32), vmem((HH, 64, 256), F32),
            vmem((2, HALF, 128), F32), vmem((2, 128, D), F32), vmem((256, D), F32), vmem((256, D), F32),
            vmem((256, D)), vmem((8, 32, D)), vmem((8, 32, D)), vmem((2, 8, 32, D)),
            dma(2, 2, 2, 3), dma(2, 4, 2, 3), dma(2, 2, 2, 3), dma(2, 2, 3), dma(2, 4, 2), dma(2, 3, 2),
            dma(2, 3), dma(2, 2, 8),
        ],
        compiler_params=pltpu.CompilerParams(
            collective_id=1, has_side_effects=True, vmem_limit_bytes=60 << 20
        ),
    )(
        gch, vals, e, mask, mask_cols, normed, tok, wv, dwu, dwd,
        dwo.reshape(4, 4, 48, HALF), gain_f, gain_mix.reshape(1, D), mgrad,
    )
    own = lax.dynamic_index_in_dim(res, c, 0, False).astype(F32)
    rows = lax.dynamic_slice_in_dim(res[:, 0:96].reshape(2, 2, 48, D), 24 * c, 24, 2).astype(F32)
    up_grad = rows.reshape(2, 2, 24, 16, 48).transpose(2, 3, 0, 1, 4).reshape(24, 3072)
    down_grad = own[96:192]
    pair = lax.dynamic_slice_in_dim(res[:, 192:240], 24 * c, 24, 1).astype(F32)
    out_w = jnp.concatenate([pair[0, :, 0:HALF], pair[1, :, 0:HALF]], axis=1)
    value_w = jnp.concatenate([pair[0, :, HALF:D], pair[1, :, HALF:D]], axis=1)
    gains = lax.dynamic_slice_in_dim(own[240:242] + own[242:244], 24 * s, 24, 1)
    return (
        out, input_grad, value_w, out_w, up_grad, down_grad, gains[1], gains[0],
        tg.reshape(HEADS, 64, 256),
    )


def solution(mesh):
    return jax.shard_map(
        per_device,
        mesh=mesh,
        in_specs=(
            P("dp", "seq", None),
            P("dp"),
            P("seq", None),
            P("seq", None),
            P("seq", None),
            P("seq", None),
            P(),
            P(),
            P(None, "seq", None),
            P("dp", "seq", None),
        ),
        out_specs=(
            P("dp", "seq", None),
            P("dp", "seq", None),
            P("seq", None),
            P("seq", None),
            P("seq", None),
            P("seq", None),
            P("seq"),
            P("seq"),
            P(None, "seq", "dp"),
        ),
        check_vma=False,
    )
```

```python
import jax
import jax.numpy as jnp
from jax import lax
from jax.experimental import pallas as pl
from jax.experimental.pallas import tpu as pltpu
from jax.sharding import PartitionSpec as P

D = 768
HALF = 384
HEADS = 12
HH = 6
EPS = 1e-06
MESH = pl.DeviceIdType.MESH
BF = jnp.bfloat16
F32 = jnp.float32
OFFS = (1, 3, 2)
ROWS = 144
GELU_C = 0.7978845608028654
GELU_A = 0.044715


def here():
    s = lax.axis_index("seq")
    return lax.axis_index("dp"), s // 8, (s // 2) % 4, s % 2


def at(z, x, y, c):
    return (z, (x * 4 + y) * 2 + c)


def remote(src, dst, sems, idx, device):
    return pltpu.make_async_remote_copy(
        src_ref=src,
        dst_ref=dst,
        send_sem=sems.at[(0,) + idx],
        recv_sem=sems.at[(1,) + idx],
        device_id=device,
        device_id_type=MESH,
    )


def along(first, k):
    z, x, y, c = here()
    if first == "x":
        return at(z, lax.rem(x + k, 4), y, c)
    return at(z, x, lax.rem(y + k, 4), c)


OTHER = {"x": "y", "y": "x"}


def own_at(first):
    _, x, y, _ = here()
    return x if first == "x" else y


def gather_one(buf, first, sems):
    _, x, y, _ = here()
    return [
        remote(buf.at[x, y], buf.at[x, y], sems, (0, i), along(first, k))
        for i, k in enumerate(OFFS)
    ]


def gather_two(buf, first, sems):
    _, x, y, _ = here()
    view = buf.at[:, y] if first == "x" else buf.at[x]
    return [
        remote(view, view, sems, (1, i), along(OTHER[first], k)) for i, k in enumerate(OFFS)
    ]


def scatter_one(src, rcv, first, sems):
    mine = own_at(first)
    out = []
    for i, k in enumerate(OFFS):
        to = lax.rem(mine + k, 4)
        part = src.at[to] if first == "x" else src.at[:, to]
        out.append(remote(part, rcv.at[i], sems, (0, i), along(first, k)))
    return out


def scatter_sum(src, rcv, mid, first):
    mine = own_at(first)
    for j in range(4):
        own = src[mine, j] if first == "x" else src[j, mine]
        total = own.astype(F32)
        for i in range(3):
            total = total + rcv[i, j].astype(F32)
        mid[j] = total.astype(BF)


def scatter_two(mid, rcv, first, sems):
    second = OTHER[first]
    mine = own_at(second)
    return [
        remote(mid.at[lax.rem(mine + k, 4)], rcv.at[i], sems, (1, i), along(second, k))
        for i, k in enumerate(OFFS)
    ]


def scatter_end(mid, rcv, first):
    total = mid[own_at(OTHER[first])].astype(F32)
    for i in range(3):
        total = total + rcv[i].astype(F32)
    return total


def start(copies):
    for copy in copies:
        copy.start()


def wait_recv(copies):
    for copy in copies:
        copy.wait_recv()


def wait_send(copies):
    for copy in copies:
        copy.wait_send()


def signal(device):
    pl.semaphore_signal(
        pltpu.get_barrier_semaphore(), inc=1, device_id=device, device_id_type=MESH
    )


def greet():
    z, x, y, c = here()
    count = 0
    for k in range(1, 4):
        signal(at(z, lax.rem(x + k, 4), y, c))
        signal(at(z, x, lax.rem(y + k, 4), c))
        count += 2
    signal(at(z, x, y, 1 - c))
    count += 1
    for k in range(1, 8):
        signal(at(lax.rem(z + k, 8), x, y, c))
        count += 1
    return count


def meet(count):
    pl.semaphore_wait(pltpu.get_barrier_semaphore(), count)


def dot(a, b):
    return jnp.dot(a, b, preferred_element_type=F32)


def dot_nt(a, b):
    return lax.dot_general(a, b, (((1,), (1,)), ((), ())), preferred_element_type=F32)


def flip(a):
    return jnp.transpose(a)


def rms_of(v):
    return lax.rsqrt(jnp.mean(v * v, axis=-1, keepdims=True) + EPS)


def layer(
    lengths, tokens, out_grad, w_value, w_out, w_up, w_down, gain_mix, gain_ffn, table,
    out, input_grad, d_value, d_out, d_up, d_down, gsum, tg,
    perm, pre, got, tok, og, e, wv, wo_all, wz,
    ux, uy, rx, ry, mx, my, rx2, ry2, mt, rr, mix, vt, vals, mcol, normed, middle, nf, bgs, hid, pgr, act,
    part, part_r, fng, fng_r, mgrad, dwu, dwda, dwdb, dwo, dwv, gx, gy,
    ru, rd, rl, mu, md, ml, ru2, rd2, rl2, gs, gr, up_s, up_r, dn_s, dn_r, tgs, tg_r, vgt, ng_r,
    sums, zr, zr2, zs, zs2, post,
    s_sib, s_ag, s_wz, s_u, s_loc, s_g, s_w, s_gain, s_up, s_dn, s_z,
):
    z, x, y, c = here()
    sib = at(z, x, y, 1 - c)
    up = at(lax.rem(z + 1, 8), x, y, c)
    down = at(lax.rem(z + 7, 8), x, y, c)
    wo = wo_all.at[c]

    def to_sib(src, dst, i):
        return remote(src, dst, s_sib, (i,), sib)

    count = greet()
    own_tab = pltpu.make_async_copy(table.at[pl.ds(6 * c, 6)], e.at[:, c], s_loc)
    own_tab.start()
    col = lax.broadcasted_iota(jnp.int32, (1, D), 1)
    odd = jnp.where(col >= HALF, 1, 0)
    low = col - HALF * odd
    half = jnp.where(low >= 192, 1, 0)
    low = low - 192 * half
    quad = jnp.where(low >= 48, 1, 0) + jnp.where(low >= 96, 1, 0) + jnp.where(low >= 144, 1, 0)
    origin = low + 144 * quad + 96 * odd + 48 * half
    perm[...] = jnp.where(lax.broadcasted_iota(jnp.int32, (D, D), 0) == origin, 1.0, 0.0).astype(BF)
    block = pl.multiple_of(D * lax.rem(z, 4), D)
    mine = dot(w_up[:, pl.ds(block, D)], perm[...])
    for cc in range(2):
        cols = slice(HALF * cc, HALF * cc + HALF)
        pre[cc, :, 0:HALF] = w_out[:, cols].astype(F32)
        pre[cc, :, HALF:D] = w_value[:, cols].astype(F32)
        pre[cc, :, D : D + HALF] = mine[:, cols]
    meet(count)
    swap_pre = to_sib(pre.at[1 - c], got.at[c], 0)
    swap_tok = to_sib(tokens, tok.at[:, c], 1)
    swap_tab = to_sib(table.at[pl.ds(6 * (1 - c), 6)], e.at[:, c], 2)
    swap_og = to_sib(out_grad, og.at[:, c], 3)
    start([swap_pre, swap_tok, swap_tab, swap_og])
    got[c] = pre[c]
    tok[:, c] = tokens[...]
    og[:, c] = out_grad[...]
    wz_x = wz.at[z, :, :, pl.ds(0, 32)]
    wz_y = wz.at[z, :, :, pl.ds(32, 16)]
    bufs = ((wv, "x"), (wo, "y"), (wz_x, "x"), (wz_y, "y"))
    g1 = [gather_one(buf, first, s_ag.at[:, i]) for i, (buf, first) in enumerate(bufs)]
    g2 = [gather_two(buf, first, s_ag.at[:, i]) for i, (buf, first) in enumerate(bufs)]
    swap_pre.wait_recv()
    shard = got[...].reshape(48, D + HALF).astype(BF)
    wo[x, y] = shard[:, 0:HALF]
    wv[x, y] = shard[:, HALF:D]

    @pl.when(z < 4)
    def _():
        wz[z, x, y] = shard[:, D : D + HALF]

    @pl.when(z >= 4)
    def _():
        rows = pl.ds(pl.multiple_of(48 * (lax.rem(z, 4) // 2), 16), 48)
        cols = pl.ds(pl.multiple_of(HALF * lax.rem(z, 2), 128), HALF)
        wz[z, x, y] = w_down[rows, cols]

    for i in range(4):
        start(g1[i])

    def slab(t, half, sign):
        return wz.at[lax.rem(z + 8 - sign * t, 8), pl.ds(2 * half, 2)]

    wz_up = [[remote(slab(t, h, 1), slab(t, h, 1), s_wz, (0, t, h), up) for h in range(2)] for t in range(4)]
    wz_dn = [[remote(slab(t, h, -1), slab(t, h, -1), s_wz, (1, t, h), down) for h in range(2)] for t in range(4)]

    def pass_on(t, h):
        wz_up[t - 1][h].wait_recv()
        if t < 3 or h == 0:
            wz_up[t][h].start()
        wz_dn[t - 1][h].wait_recv()
        if t < 3 or h == 1:
            wz_dn[t][h].start()

    for i in range(4):
        wait_recv(g1[i])
        start(g2[i])
    swap_tok.wait_recv()
    values = tok[...].reshape(256, D).astype(F32)
    gm = gain_mix[...].reshape(1, D)
    gf = gain_ffn[...].reshape(1, D)
    normed[...] = (values * rms_of(values) * gm).astype(BF)
    place = (4 * x + y) * 128
    lane = lax.broadcasted_iota(jnp.int32, (1, 128), 1) + place
    row = lax.broadcasted_iota(jnp.int32, (128, 128), 0) + place
    masks = [jnp.where(lane < lengths[b], 1.0, 0.0) for b in range(2)]
    for b in range(2):
        mcol[b] = jnp.where(row < lengths[b], 1.0, 0.0)
    swap_tab.wait_recv()
    own_tab.wait()

    def exps(h, carry):
        e[h] = jnp.exp(e[h].astype(F32)).astype(BF)
        return carry

    lax.fori_loop(0, HH, exps, 0)
    wait_recv(g2[2])
    wait_recv(g2[3])
    for h in range(2):
        wz_up[0][h].start()
        wz_dn[0][h].start()
    wait_recv(g2[0])
    v = dot(normed[...], wv[...].reshape(D, HALF)).astype(BF).astype(F32)
    vall = flip(v) * jnp.concatenate(masks, axis=1)
    ones = jnp.concatenate(masks + [jnp.zeros((14, 128), F32)], axis=0)
    for h in range(HH):
        block = jnp.concatenate(
            [vall[64 * h : 64 * h + 64, 0:128], vall[64 * h : 64 * h + 64, 128:256]], axis=0
        )
        vt[h] = jnp.concatenate([block, ones], axis=0).astype(BF)
        vals[h] = flip(block).astype(BF)

    s1x = scatter_one(ux, rx, "x", s_u.at[:, 0])
    s1y = scatter_one(uy, ry, "y", s_u.at[:, 1])
    for i, k in enumerate(OFFS + (0,)):
        xx = lax.rem(x + k, 4)
        yy = lax.rem(y + k, 4)

        def head_x(h, carry, xx=xx):
            cols = pl.ds(pl.multiple_of(512 * xx, 512), 512)
            u = dot(vt[h], e[h, :, :, cols].reshape(128, 512))
            for j in range(4):
                ux[xx, j, h] = u[:, 128 * j : 128 * j + 128].astype(BF)
            return carry

        def head_y(h, carry, yy=yy):
            for j in range(4):
                cols = pl.ds(pl.multiple_of(512 * j + 128 * yy, 128), 128)
                uy[j, yy, h] = dot(vt[h + 3], e[h + 3, :, :, cols].reshape(128, 128)).astype(BF)
            return carry

        lax.fori_loop(0, 3, head_x, 0)
        if i < 3:
            s1x[i].start()
        lax.fori_loop(0, 3, head_y, 0)
        if i < 3:
            s1y[i].start()
    pass_on(1, 0)
    wait_recv(g2[1])
    swap_wo = to_sib(wo, wo, 5)
    swap_wo.start()
    pass_on(1, 1)
    pass_on(2, 0)
    s2x = scatter_two(mx, rx2, "x", s_u.at[:, 0])
    s2y = scatter_two(my, ry2, "y", s_u.at[:, 1])
    wait_recv(s1x)
    scatter_sum(ux, rx, mx, "x")
    start(s2x)
    wait_recv(s1y)
    scatter_sum(uy, ry, my, "y")
    start(s2y)
    pass_on(2, 1)
    pass_on(3, 0)
    for half, (copies, mid, rcv, first) in enumerate(((s2x, mx, rx2, "x"), (s2y, my, ry2, "y"))):
        wait_recv(copies)
        total = scatter_end(mid, rcv, first)
        for hh in range(3):
            h = half * 3 + hh
            for b in range(2):
                r = masks[b] / total[hh, 128 + b : 129 + b]
                rr[b, h : h + 1] = r
                mt[b, 64 * h : 64 * h + 64] = total[hh, 64 * b : 64 * b + 64] * r
    for b in range(2):
        mix[c, b] = flip(mt[b]).astype(BF)
    swap_mix = to_sib(mix.at[c], mix.at[c], 6)
    swap_mix.start()
    swap_wo.wait_recv()
    swap_mix.wait_recv()
    mixed = [mix[i].reshape(256, HALF) for i in range(2)]
    for cc in range(2):
        w = wo_all[cc].reshape(D, HALF)
        cols = slice(HALF * cc, HALF * cc + HALF)
        middle[:, cols] = (
            tok[...].reshape(256, D)[:, cols].astype(F32)
            + dot(mixed[0], w[0:HALF])
            + dot(mixed[1], w[HALF:D])
        )
    mid_v = middle[...]
    rms = rms_of(mid_v)
    nf[...] = (mid_v * rms * gf).astype(BF)
    swap_og.wait_recv()
    grad = og[...].reshape(256, D)
    pass_on(3, 1)
    wz_up[3][0].wait_recv()
    wz_dn[3][1].wait_recv()
    for hf in range(2):
        hp = jnp.concatenate([dot(nf[...], wz[2 * hf + i].reshape(D, HALF)) for i in range(2)], axis=1)
        t = jnp.tanh(GELU_C * (hp + GELU_A * hp * hp * hp))
        hid[hf] = (0.5 * hp * (1.0 + t)).astype(BF)
        act[hf] = 0.5 * (1.0 + t) + 0.5 * hp * (1.0 - t * t) * (
            GELU_C * (1.0 + 3.0 * GELU_A * hp * hp)
        )

    def down_rows(m, b):
        return jnp.concatenate([wz[4 + b, m].reshape(192, HALF), wz[6 + b, m].reshape(192, HALF)], axis=0)

    lots = (
        (dwda, rd.at[0], md.at[0], rd2.at[0], "x"),
        (dwdb, rd.at[1], md.at[1], rd2.at[1], "y"),
        (dwu.at[0], ru.at[0], mu.at[0], ru2.at[0], "x"),
        (dwu.at[1], ru.at[1], mu.at[1], ru2.at[1], "y"),
        (dwo, rl.at[0], ml.at[0], rl2.at[0], "x"),
        (dwv, rl.at[1], ml.at[1], rl2.at[1], "y"),
    )
    w1 = [scatter_one(lot[0], lot[1], lot[4], s_w.at[:, i]) for i, lot in enumerate(lots)]
    w2 = [scatter_two(lot[2], lot[3], lot[4], s_w.at[:, i]) for i, lot in enumerate(lots)]
    for hf in range(2):
        for i in range(2):
            m = 2 * hf + i
            cols = slice(HALF * i, HALF * i + HALF)
            hg = dot_nt(grad[:, 0:HALF], down_rows(m, 0)) + dot_nt(grad[:, HALF:D], down_rows(m, 1))
            pgr[hf, :, cols] = (act[hf, :, cols] * hg).astype(BF)
            more = dot_nt(pgr[hf, :, cols], wz[m].reshape(D, HALF)).reshape(2, 2, 64, D)
            fng[...] = more if m == 0 else fng[...] + more
    swap_fng = to_sib(fng, fng_r, 7)
    swap_fng.start()
    for hf in range(2):
        dwd = dot(flip(hid[hf]), grad).astype(BF)
        for i in range(2):
            for a in range(2):
                for q in range(4):
                    base = HALF * i + 192 * a + 48 * q
                    dwda[2 * hf + i, q, 48 * a : 48 * a + 48] = dwd[base : base + 48, 0:HALF]
                    dwdb[2 * hf + i, q, 48 * a : 48 * a + 48] = dwd[base : base + 48, HALF:D]
    swap_fng.wait_recv()
    full = (fng[...] + fng_r[...]).reshape(256, D)
    mid_v = middle[...]
    rms = rms_of(mid_v)
    gain_f = jnp.sum(full * mid_v * rms, axis=0, keepdims=True)
    weighted = full * gf
    inner = jnp.mean(weighted * mid_v, axis=-1, keepdims=True)
    mg = grad.astype(F32) + rms * weighted - mid_v * (rms * rms * rms) * inner
    mgrad[...] = mg.reshape(2, 2, 64, D)
    bg = mg.astype(BF)
    bgs[...] = bg
    xg = jnp.zeros((256, HALF), F32)
    for cc in range(2):
        w = wo_all[cc, pl.ds(2 * c, 2)].reshape(HALF, HALF)
        xg = xg + dot_nt(bg[:, HALF * cc : HALF * cc + HALF], w)
    deltas = []
    for b in range(2):
        xgt = flip(xg[128 * b : 128 * b + 128])
        for h in range(HH):
            rows = xgt[64 * h : 64 * h + 64]
            r = rr[b, h : h + 1]
            deltas.append(jnp.sum(rows * mt[b, 64 * h : 64 * h + 64], axis=0, keepdims=True) * r)
            own = gx if h < 3 else gy
            own[x, y, h % 3, 64 * b : 64 * b + 64] = (rows * r).astype(BF)
    for h in range(HH):
        d0, d1 = deltas[h], deltas[HH + h]
        h0 = d0.astype(BF).astype(F32)
        h1 = d1.astype(BF).astype(F32)
        own = gx if h < 3 else gy
        own[x, y, h % 3, 128:144] = jnp.concatenate(
            [h0, h1, d0 - h0, d1 - h1, jnp.zeros((12, 128), F32)], axis=0
        ).astype(BF)
    a1x = gather_one(gx, "x", s_g.at[:, 0])
    a1y = gather_one(gy, "y", s_g.at[:, 1])
    a2x = gather_two(gx, "x", s_g.at[:, 0])
    a2y = gather_two(gy, "y", s_g.at[:, 1])
    start(a1x)
    start(a1y)
    dwu[0] = dot(flip(nf[...]), pgr[0]).astype(BF).reshape(4, 4, 48, D)
    wait_recv(a1x)
    start(a2x)
    wait_recv(a1y)
    start(a2y)
    start(w1[0])
    start(w1[1])
    dwu[1] = dot(flip(nf[...]), pgr[1]).astype(BF).reshape(4, 4, 48, D)
    start(w1[2])
    start(w1[3])
    bg_c = bgs[:, pl.ds(pl.multiple_of(HALF * c, 128), HALF)]
    for i in range(2):
        dwo[pl.ds(2 * i, 2)] = dot(flip(mixed[i]), bg_c).astype(BF).reshape(2, 4, 48, HALF)
    start(w1[4])
    for hf in range(2):
        down_w = [jnp.concatenate([down_rows(2 * hf, b), down_rows(2 * hf + 1, b)], axis=0) for b in range(2)]
        more = jnp.concatenate([dot(hid[hf], w) for w in down_w], axis=1).reshape(2, 2, 64, D)
        part[...] = more if hf == 0 else part[...] + more
    swap_part = to_sib(part.at[:, 1 - c], part_r, 8)
    swap_part.start()
    swap_fng.wait_send()
    fng[...] = middle[...].reshape(2, 2, 64, D)
    swap_part.wait_recv()
    out[...] = (fng[:, c] + (part[:, c] + part_r[...])).astype(BF)
    wait_recv(a2x)
    wait_recv(a2y)

    def table_part(d, hf):
        buf = gx if hf == 0 else gy
        result = []
        for hh in range(3):
            h = 3 * hf + hh
            pair = []
            for i in range(2):
                k = 2 * d + i
                g = buf[k // 4, lax.rem(k, 4), hh]
                cols = pl.ds(pl.multiple_of(256 * d + 128 * i, 128), 128)
                extra = g[128:144].astype(F32)
                s = dot(vals[h], g[0:128])
                s = s - mcol[0] * (extra[0:1] + extra[2:3])
                s = s - mcol[1] * (extra[1:2] + extra[3:4])
                pair.append(s * e[h, :, :, cols].reshape(128, 128).astype(F32))
            result.append(jnp.concatenate(pair, axis=1))
        return result

    def ring(send, recv, sems, t, hf, device):
        return remote(send.at[hf, t], recv.at[hf, t], sems, (hf, t), device)

    ups = [[ring(up_s, up_r, s_up, t, hf, up) for t in range(4 - hf)] for hf in range(2)]
    dns = [[ring(dn_s, dn_r, s_dn, t, hf, down) for t in range(3 + hf)] for hf in range(2)]

    def step(t):
        for copies, send, recv, hf, d in (
            (ups[0], up_s, up_r, 0, lax.rem(z + 12 - t, 8)),
            (dns[1], dn_s, dn_r, 1, lax.rem(z + 4 + t, 8)),
            (ups[1], up_s, up_r, 1, lax.rem(z + 11 - t, 8)),
            (dns[0], dn_s, dn_r, 0, lax.rem(z + 5 + t, 8)),
        ):
            if t >= len(copies):
                continue
            parts = table_part(d, hf)
            if t > 0:
                copies[t - 1].wait_recv()
            for hh in range(3):
                p = parts[hh]
                if t > 0:
                    p = p + recv[hf, t - 1, hh].astype(F32)
                send[hf, t, hh] = p.astype(BF)
            copies[t].start()

    step(0)
    for h in range(HH):
        buf = gx if h < 3 else gy
        total = jnp.zeros((128, 128), F32)
        for k in range(16):
            total = total + dot_nt(
                buf[k // 4, k % 4, h % 3, 0:128], e[h, :, :, 128 * k : 128 * k + 128].reshape(128, 128)
            )
        for b in range(2):
            vgt[b, 64 * h : 64 * h + 64] = total[64 * b : 64 * b + 64] * masks[b]
    vg = jnp.concatenate([flip(vgt[b]) for b in range(2)], axis=0).astype(BF)
    dwv[...] = dot(flip(normed[...]), vg).astype(BF).reshape(4, 4, 48, HALF)
    start(w1[5])
    swap_part.wait_send()
    part[...] = dot_nt(vg, wv[...].reshape(D, HALF)).reshape(2, 2, 64, D)
    swap_ng = to_sib(part, ng_r, 9)
    swap_ng.start()
    step(1)
    swap_ng.wait_recv()
    full = (part[...] + ng_r[...]).reshape(256, D)
    xv = tok[...].reshape(256, D).astype(F32)
    rms = rms_of(xv)
    gain_m = jnp.sum(full * xv * rms, axis=0, keepdims=True)
    weighted = full * gm
    inner = jnp.mean(weighted * xv, axis=-1, keepdims=True)
    fng[...] = (rms * weighted - xv * (rms * rms * rms) * inner).reshape(2, 2, 64, D)
    input_grad[...] = mgrad[:, c] + fng[:, c]
    gains = jnp.concatenate([gain_m, gain_f], axis=0)
    high = gains.astype(BF).astype(F32)
    gs[...] = jnp.concatenate([high, gains - high, jnp.zeros((12, D), F32)], axis=0).astype(BF)
    gr[x, y] = gs[...]
    gain1 = gather_one(gr, "x", s_gain)
    gain2 = gather_two(gr, "x", s_gain)
    start(gain1)

    def middle_sum(i):
        wait_recv(w1[i])
        src, rcv, mid, _, first = lots[i]
        scatter_sum(src, rcv, mid, first)
        start(w2[i])

    def last_sum(i, rows, cols):
        wait_recv(w2[i])
        _, _, mid, rcv, first = lots[i]
        sums[rows, cols] = scatter_end(mid, rcv, first).astype(BF)

    def spread(base, rows, buf, i):
        def chunk(d):
            return sums.at[
                pl.ds(pl.multiple_of(base + rows * (d // 2), 16), rows),
                pl.ds(pl.multiple_of(HALF * lax.rem(d, 2), 128), HALF),
            ]

        return [
            remote(
                chunk(lax.rem(z + k, 8)), buf.at[k - 1], s_z, (i, k - 1), at(lax.rem(z + k, 8), x, y, c)
            )
            for k in range(1, 8)
        ]

    def collect(base, rows, buf, res, i):
        total = sums[
            pl.ds(pl.multiple_of(base + rows * (z // 2), 16), rows),
            pl.ds(pl.multiple_of(HALF * lax.rem(z, 2), 128), HALF),
        ].astype(F32)
        for k in range(7):
            total = total + buf[k].astype(F32)
        res[z] = total.astype(BF)
        return [
            remote(res.at[z], res.at[z], s_z, (i, k - 1), at(lax.rem(z + k, 8), x, y, c))
            for k in range(1, 8)
        ]

    middle_sum(0)
    middle_sum(1)
    step(2)
    middle_sum(2)
    middle_sum(3)
    middle_sum(4)
    middle_sum(5)
    wait_recv(gain1)
    start(gain2)
    step(3)
    last_sum(0, slice(96, 192), slice(0, HALF))
    last_sum(1, slice(96, 192), slice(HALF, D))
    last_sum(2, slice(0, 48), slice(0, D))
    last_sum(3, slice(48, 96), slice(0, D))
    z1 = spread(0, 48, zr, 0)
    start(z1)
    last_sum(4, slice(192, 240), slice(0, HALF))
    last_sum(5, slice(192, 240), slice(HALF, D))
    wait_recv(gain2)
    gtot = jnp.sum(gr[...].reshape(16, 16, D).astype(F32), axis=0)
    gains = gtot[0:2] + gtot[2:4]
    high = gains.astype(BF).astype(F32)
    sums[240:256] = jnp.concatenate([high, gains - high, jnp.zeros((12, D), F32)], axis=0).astype(BF)
    z3 = spread(192, 16, zr2, 1)
    start(z3)
    own = [table_part(z, hf) for hf in range(2)]
    swap_tg = to_sib(tgs, tg_r, 10)
    for hf in range(2):
        ups[hf][-1].wait_recv()
        dns[hf][-1].wait_recv()
        for hh in range(3):
            p = own[hf][hh] + (
                up_r[hf, 3 - hf, hh].astype(F32) + dn_r[hf, 2 + hf, hh].astype(F32)
            )
            act[0, 0:128, 0:256] = p
            tg[c, 3 * hf + hh] = act[0, pl.ds(pl.multiple_of(64 * c, 64), 64), 0:256]
            tgs[3 * hf + hh] = act[0, pl.ds(pl.multiple_of(64 * (1 - c), 64), 64), 0:256]
    swap_tg.start()
    wait_recv(z1)
    z2 = collect(0, 48, zr, zs, 2)
    start(z2)
    wait_recv(z3)
    z4 = collect(192, 16, zr2, zs2, 3)
    start(z4)
    swap_tg.wait_recv()
    tg[1 - c] = tg_r[...]
    wait_recv(z2)
    wait_recv(z4)
    for d in range(8):
        cols = slice(HALF * (d % 2), HALF * (d % 2) + HALF)
        act[0, 48 * (d // 2) : 48 * (d // 2) + 48, cols] = zs[d].astype(F32)
        act[0, 192 + 16 * (d // 2) : 208 + 16 * (d // 2), cols] = zs2[d].astype(F32)
    for cc, ref in ((c, post.at[0]), (1 - c, post.at[1])):
        base = pl.multiple_of(24 * cc, 8)
        ref[:, 0:D] = act[0, pl.ds(base, 24)]
        ref[:, D : 2 * D] = act[0, pl.ds(base + 48, 24)]
        ref[:, 2 * D : 3 * D] = act[0, pl.ds(base + 192, 24)]
    swap_post = to_sib(post.at[1], post.at[2], 11)
    swap_post.start()
    d_down[...] = act[0, 96:192]
    gsum[...] = jnp.concatenate(
        [act[0, 240:242] + act[0, 242:244], jnp.zeros((6, D), F32)], axis=0
    )
    swap_post.wait_recv()
    first_core = (c == 0).astype(F32)
    pair = (
        post[0] * first_core + post[2] * (1.0 - first_core),
        post[2] * first_core + post[0] * (1.0 - first_core),
    )
    for m in range(4):
        block = jnp.concatenate([p[:, HALF * m : HALF * m + HALF] for p in pair], axis=1).astype(BF)
        d_up[:, D * m : D * m + D] = dot_nt(block, perm[...])
    for cc in range(2):
        cols = slice(HALF * cc, HALF * cc + HALF)
        d_out[:, cols] = pair[cc][:, 2 * D : 2 * D + HALF]
        d_value[:, cols] = pair[cc][:, 2 * D + HALF : 3 * D]
    for copy in (
        swap_pre, swap_tok, swap_tab, swap_og, swap_wo, swap_mix, swap_ng, swap_tg, swap_post
    ):
        copy.wait_send()
    for group in g1 + g2 + w1 + w2 + ups + dns + wz_up[:3] + wz_dn[:3] + [
        wz_up[3][:1], wz_dn[3][1:],
        s1x, s1y, s2x, s2y, a1x, a1y, a2x, a2y, gain1, gain2, z1, z2, z3, z4
    ]:
        wait_send(group)


def finish(out, input_grad, d_value, d_out, d_up, d_down, gsum, tg, *outs):
    for src, dst in zip((out, input_grad, d_value, d_out, d_up, d_down, tg), outs):
        dst[...] = src[...]
    s = lax.axis_index("seq")
    row = lax.broadcasted_iota(jnp.int32, (D, 128), 0)
    lane = lax.broadcasted_iota(jnp.int32, (D, 128), 1)
    pick = jnp.where(row == lane + 24 * s, 1.0, 0.0)
    for i in range(2):
        got = jnp.dot(gsum[...], pick, precision=lax.Precision.HIGHEST, preferred_element_type=F32)
        outs[7 + i][...] = got[i, 0:24]


def vmem(*shape, kind=BF):
    return pltpu.VMEM(shape, kind)


def dma(*shape):
    return pltpu.SemaphoreType.DMA(shape)


IN_VMEM = pl.BlockSpec(memory_space=pltpu.VMEM)


def per_device(tokens, lengths, w_value, w_out, w_up, w_down, gain_mix, gain_ffn, mix_table, out_grad):
    sd = jax.ShapeDtypeStruct
    shapes = [
        sd((2, 64, D), BF), sd((2, 64, D), F32), sd((24, D), F32), sd((24, D), F32), sd((24, 4 * D), F32),
        sd((96, D), F32), sd((8, D), F32), sd((2, HH, 64, 256), F32),
    ]
    raw = pl.pallas_call(
        layer,
        name="layer",
        out_shape=shapes,
        in_specs=[pl.BlockSpec(memory_space=pltpu.SMEM)] + [IN_VMEM] * 8 + [pl.BlockSpec(memory_space=pl.ANY)],
        out_specs=[IN_VMEM] * 8,
        scratch_shapes=[
            vmem(D, D), vmem(2, 24, D + HALF, kind=F32), vmem(2, 24, D + HALF, kind=F32),
            vmem(2, 2, 64, D), vmem(2, 2, 64, D), vmem(HH, 2, 64, 2048),
            vmem(4, 4, 48, HALF), vmem(2, 4, 4, 48, HALF), vmem(8, 4, 4, 48, HALF),
            vmem(4, 4, 3, ROWS, 128), vmem(4, 4, 3, ROWS, 128), vmem(3, 4, 3, ROWS, 128), vmem(3, 4, 3, ROWS, 128),
            vmem(4, 3, ROWS, 128), vmem(4, 3, ROWS, 128), vmem(3, 3, ROWS, 128), vmem(3, 3, ROWS, 128),
            vmem(2, HALF, 128, kind=F32), vmem(2, 8, 128, kind=F32), vmem(2, 2, 128, HALF), vmem(HH, ROWS, 128),
            vmem(HH, 128, 128), vmem(2, 128, 128, kind=F32), vmem(256, D), vmem(256, D, kind=F32), vmem(256, D),
            vmem(256, D), vmem(2, 256, D), vmem(2, 256, D), vmem(2, 256, D, kind=F32),
            vmem(2, 2, 64, D, kind=F32), vmem(2, 64, D, kind=F32), vmem(2, 2, 64, D, kind=F32),
            vmem(2, 2, 64, D, kind=F32), vmem(2, 2, 64, D, kind=F32),
            vmem(2, 4, 4, 48, D), vmem(4, 4, 96, HALF), vmem(4, 4, 96, HALF), vmem(4, 4, 48, HALF),
            vmem(4, 4, 48, HALF), vmem(4, 4, 3, ROWS, 128), vmem(4, 4, 3, ROWS, 128),
            vmem(2, 3, 4, 48, D), vmem(2, 3, 4, 96, HALF), vmem(2, 3, 4, 48, HALF),
            vmem(2, 4, 48, D), vmem(2, 4, 96, HALF), vmem(2, 4, 48, HALF),
            vmem(2, 3, 48, D), vmem(2, 3, 96, HALF), vmem(2, 3, 48, HALF),
            vmem(16, D), vmem(4, 4, 16, D),
            vmem(2, 4, 3, 128, 256), vmem(2, 4, 3, 128, 256), vmem(2, 4, 3, 128, 256), vmem(2, 4, 3, 128, 256),
            vmem(HH, 64, 256, kind=F32), vmem(HH, 64, 256, kind=F32), vmem(2, HALF, 128, kind=F32),
            vmem(2, 2, 64, D, kind=F32), vmem(256, D), vmem(7, 48, HALF), vmem(7, 16, HALF), vmem(8, 48, HALF), vmem(8, 16, HALF),
            vmem(3, 24, 3 * D, kind=F32),
            dma(2, 12), dma(2, 4, 2, 3), dma(2, 2, 4, 2), dma(2, 2, 2, 3), pltpu.SemaphoreType.DMA, dma(2, 2, 2, 3),
            dma(2, 6, 2, 3), dma(2, 2, 3), dma(2, 2, 4), dma(2, 2, 4), dma(2, 4, 7),
        ],
        compiler_params=pltpu.CompilerParams(
            collective_id=0, has_side_effects=True, vmem_limit_bytes=63 << 20
        ),
    )(lengths, tokens, out_grad, w_value, w_out, w_up, w_down, gain_mix, gain_ffn, mix_table)
    out, input_grad, d_value, d_out, d_up, d_down, tg, mix_gain, ffn_gain = pl.pallas_call(
        finish,
        name="finish",
        out_shape=shapes[:6] + [shapes[7], sd((24,), F32), sd((24,), F32)],
        in_specs=[IN_VMEM] * 8,
        out_specs=[IN_VMEM] * 9,
    )(*raw)
    return (
        out, input_grad, d_value, d_out, d_up, d_down, mix_gain, ffn_gain, tg.reshape(HEADS, 64, 256),
    )


def solution(mesh):
    return jax.shard_map(
        per_device,
        mesh=mesh,
        in_specs=(
            P("dp", "seq", None),
            P("dp"),
            P("seq", None),
            P("seq", None),
            P("seq", None),
            P("seq", None),
            P(),
            P(),
            P(None, "seq", None),
            P("dp", "seq", None),
        ),
        out_specs=(
            P("dp", "seq", None),
            P("dp", "seq", None),
            P("seq", None),
            P("seq", None),
            P("seq", None),
            P("seq", None),
            P("seq"),
            P("seq"),
            P(None, "seq", "dp"),
        ),
        check_vma=False,
    )
```

```python
import jax
import jax.numpy as jnp
from jax import lax
from jax.experimental import pallas as pl
from jax.experimental.pallas import tpu as pltpu
from jax.sharding import PartitionSpec as P

D = 768
HALF = 384
HEADS = 12
HH = 6
EPS = 1e-06
MESH = pl.DeviceIdType.MESH
BF = jnp.bfloat16
F32 = jnp.float32
OFFS = (1, 3, 2)
ROWS = 400
GELU_C = 0.7978845608028654
GELU_A = 0.044715


def here():
    s = lax.axis_index("seq")
    return lax.axis_index("dp"), s // 8, (s // 2) % 4, s % 2


def at(z, x, y, c):
    return (z, (x * 4 + y) * 2 + c)


def remote(src, dst, sems, idx, device):
    return pltpu.make_async_remote_copy(
        src_ref=src,
        dst_ref=dst,
        send_sem=sems.at[(0,) + idx],
        recv_sem=sems.at[(1,) + idx],
        device_id=device,
        device_id_type=MESH,
    )


def along(first, k):
    z, x, y, c = here()
    if first == "x":
        return at(z, lax.rem(x + k, 4), y, c)
    return at(z, x, lax.rem(y + k, 4), c)


OTHER = {"x": "y", "y": "x"}


def own_at(first):
    _, x, y, _ = here()
    return x if first == "x" else y


def gather_one(buf, first, sems):
    _, x, y, _ = here()
    return [
        remote(buf.at[x, y], buf.at[x, y], sems, (0, i), along(first, k))
        for i, k in enumerate(OFFS)
    ]


def gather_two(buf, first, sems):
    _, x, y, _ = here()
    view = buf.at[:, y] if first == "x" else buf.at[x]
    return [
        remote(view, view, sems, (1, i), along(OTHER[first], k)) for i, k in enumerate(OFFS)
    ]


def scatter_one(src, rcv, first, sems):
    mine = own_at(first)
    out = []
    for i, k in enumerate(OFFS):
        to = lax.rem(mine + k, 4)
        part = src.at[to] if first == "x" else src.at[:, to]
        out.append(remote(part, rcv.at[i], sems, (0, i), along(first, k)))
    return out


def scatter_sum(src, rcv, mid, first):
    mine = own_at(first)
    for j in range(4):
        own = src[mine, j] if first == "x" else src[j, mine]
        total = own.astype(F32)
        for i in range(3):
            total = total + rcv[i, j].astype(F32)
        mid[j] = total.astype(BF)


def scatter_two(mid, rcv, first, sems):
    second = OTHER[first]
    mine = own_at(second)
    return [
        remote(mid.at[lax.rem(mine + k, 4)], rcv.at[i], sems, (1, i), along(second, k))
        for i, k in enumerate(OFFS)
    ]


def scatter_end(mid, rcv, first):
    total = mid[own_at(OTHER[first])].astype(F32)
    for i in range(3):
        total = total + rcv[i].astype(F32)
    return total


def start(copies):
    for copy in copies:
        copy.start()


def wait_recv(copies):
    for copy in copies:
        copy.wait_recv()


def wait_send(copies):
    for copy in copies:
        copy.wait_send()


def signal(device):
    pl.semaphore_signal(
        pltpu.get_barrier_semaphore(), inc=1, device_id=device, device_id_type=MESH
    )


def greet():
    z, x, y, c = here()
    count = 0
    for k in range(1, 4):
        signal(at(z, lax.rem(x + k, 4), y, c))
        signal(at(z, x, lax.rem(y + k, 4), c))
        count += 2
    signal(at(z, x, y, 1 - c))
    count += 1
    for k in range(1, 8):
        signal(at(lax.rem(z + k, 8), x, y, c))
        count += 1
    return count


def meet(count):
    pl.semaphore_wait(pltpu.get_barrier_semaphore(), count)


def dot(a, b):
    return jnp.dot(a, b, preferred_element_type=F32)


def dot_nt(a, b):
    return lax.dot_general(a, b, (((1,), (1,)), ((), ())), preferred_element_type=F32)


def flip(a):
    return jnp.transpose(a)


def rms_of(v):
    return lax.rsqrt(jnp.mean(v * v, axis=-1, keepdims=True) + EPS)


def layer(
    lengths, tokens, out_grad, w_value, w_out, w_up, w_down, gain_mix, gain_ffn, table,
    out, input_grad, d_value, d_out, d_up, d_down, gsum, tg,
    perm, pre, got, tok, og, e, wv, wo_all, wz,
    ux, uy, rx, ry, mx, my, rx2, ry2, mt, rr, mix, vt, vals, mcol, normed, middle, nf, bgs, hid, pgr, act,
    part, part_r, fng, fng_r, mgrad, dwu, dwd, dws, dwo, dwv, gx, gy,
    ru, rl, mu, ml, ru2, rl2, dfar, dnear, dlast, dsum, gs, gr, up_s, up_r, dn_s, dn_r, tgs, tg_r, vgt, ng_r,
    up_sum, rest, zr_up, zr_rest, half_up, half_down, half_rest, other_up, other_down, other_rest,
    zs_up, zs_down, zs_rest, post,
    s_sib, s_ag, s_wz, s_u, s_loc, s_g, s_w, s_d, s_gain, s_up, s_dn, s_z,
):
    z, x, y, c = here()
    sib = at(z, x, y, 1 - c)
    up = at(lax.rem(z + 1, 8), x, y, c)
    down = at(lax.rem(z + 7, 8), x, y, c)
    wo = wo_all.at[c]

    def to_sib(src, dst, i):
        return remote(src, dst, s_sib, (i,), sib)

    count = greet()
    own_tab = pltpu.make_async_copy(table.at[pl.ds(6 * c, 6)], e.at[:, c], s_loc)
    own_tab.start()
    col = lax.broadcasted_iota(jnp.int32, (1, D), 1)
    odd = jnp.where(col >= HALF, 1, 0)
    low = col - HALF * odd
    half = jnp.where(low >= 192, 1, 0)
    low = low - 192 * half
    quad = jnp.where(low >= 48, 1, 0) + jnp.where(low >= 96, 1, 0) + jnp.where(low >= 144, 1, 0)
    origin = low + 144 * quad + 96 * odd + 48 * half
    perm[...] = jnp.where(lax.broadcasted_iota(jnp.int32, (D, D), 0) == origin, 1.0, 0.0).astype(BF)
    par = lax.rem(z, 2)
    for cc in range(2):
        cols = slice(HALF * cc, HALF * cc + HALF)
        pre[cc, :, 0:HALF] = w_out[:, cols].astype(F32)
        pre[cc, :, HALF:D] = w_value[:, cols].astype(F32)
    for i in range(2):
        mine = dot(w_up[:, pl.ds(pl.multiple_of(D * (2 * par + i), D), D)], perm[...])
        for cc in range(2):
            pre[cc, :, D + HALF * i : D + HALF * i + HALF] = mine[:, HALF * cc : HALF * cc + HALF]
    meet(count)
    swap_pre = to_sib(pre.at[1 - c], got.at[c], 0)
    swap_tok = to_sib(tokens, tok.at[:, c], 1)
    swap_tab = to_sib(table.at[pl.ds(6 * (1 - c), 6)], e.at[:, c], 2)
    swap_og = to_sib(out_grad, og.at[:, c], 3)
    swap_pre.start()
    got[c] = pre[c]
    tok[:, c] = tokens[...]
    og[:, c] = out_grad[...]
    for b in range(2):
        rows = pl.ds(pl.multiple_of(48 * par, 16), 48)
        wz[4 + 2 * par + b, x, y] = w_down[rows, HALF * b : HALF * b + HALF]
    bufs = (
        (wv, "x"), (wo, "y"), (wz.at[2 * par], "x"), (wz.at[2 * par + 1], "y"),
        (wz.at[4 + 2 * par], "x"), (wz.at[5 + 2 * par], "y"),
    )
    g1 = [gather_one(buf, first, s_ag.at[:, i]) for i, (buf, first) in enumerate(bufs)]
    g2 = [gather_two(buf, first, s_ag.at[:, i]) for i, (buf, first) in enumerate(bufs)]
    swap_pre.wait_recv()
    shard = got[...].reshape(48, 2 * D).astype(BF)
    wo[x, y] = shard[:, 0:HALF]
    wv[x, y] = shard[:, HALF:D]
    for i in range(2):
        wz[2 * par + i, x, y] = shard[:, D + HALF * i : D + HALF * i + HALF]
    for i in range(6):
        start(g1[i])
    start([swap_tok, swap_tab, swap_og])
    share = [
        remote(wz.at[4 * i + 2 * par + j], wz.at[4 * i + 2 * par + j], s_wz, (i, j), (up, down)[j])
        for i in range(2)
        for j in range(2)
    ]
    for i in range(6):
        wait_recv(g1[i])
        start(g2[i])
    swap_tok.wait_recv()
    values = tok[...].reshape(256, D).astype(F32)
    gm = gain_mix[...].reshape(1, D)
    gf = gain_ffn[...].reshape(1, D)
    normed[...] = (values * rms_of(values) * gm).astype(BF)
    place = (4 * x + y) * 128
    lane = lax.broadcasted_iota(jnp.int32, (1, 128), 1) + place
    row = lax.broadcasted_iota(jnp.int32, (128, 128), 0) + place
    masks = [jnp.where(lane < lengths[b], 1.0, 0.0) for b in range(2)]
    for b in range(2):
        mcol[b] = jnp.where(row < lengths[b], 1.0, 0.0)
    swap_tab.wait_recv()
    own_tab.wait()

    def exps(h, carry):
        e[h] = jnp.exp(e[h].astype(F32)).astype(BF)
        return carry

    lax.fori_loop(0, HH, exps, 0)
    wait_recv(g2[0])
    v = dot(normed[...], wv[...].reshape(D, HALF)).astype(BF).astype(F32)
    vall = flip(v) * jnp.concatenate(masks, axis=1)
    for h in range(HH):
        block = jnp.concatenate(
            [vall[64 * h : 64 * h + 64, 0:128], vall[64 * h : 64 * h + 64, 128:256]], axis=0
        )
        place = [jnp.zeros((2, 128), F32)] * (h % 3) + masks
        place = place + [jnp.zeros((14 - 2 * (h % 3), 128), F32)]
        vt[h] = jnp.concatenate([block] + place, axis=0).astype(BF)
        vals[h] = flip(block).astype(BF)

    s1x = scatter_one(ux, rx, "x", s_u.at[:, 0])
    s1y = scatter_one(uy, ry, "y", s_u.at[:, 1])
    for i, k in enumerate(OFFS + (0,)):
        xx = lax.rem(x + k, 4)
        yy = lax.rem(y + k, 4)

        cols = pl.ds(pl.multiple_of(512 * xx, 512), 512)
        extra = jnp.zeros((16, 512), F32)
        for h in range(3):
            u = dot(vt[h], e[h, :, :, cols].reshape(128, 512))
            extra = extra + u[128:144]
            for j in range(4):
                ux[xx, j, 128 * h : 128 * h + 128] = u[0:128, 128 * j : 128 * j + 128].astype(BF)
        for j in range(4):
            ux[xx, j, 384:400] = extra[:, 128 * j : 128 * j + 128].astype(BF)
        if i < 3:
            s1x[i].start()
        for j in range(4):
            cols = pl.ds(pl.multiple_of(512 * j + 128 * yy, 128), 128)
            extra = jnp.zeros((16, 128), F32)
            for h in range(3):
                u = dot(vt[h + 3], e[h + 3, :, :, cols].reshape(128, 128))
                extra = extra + u[128:144]
                uy[j, yy, 128 * h : 128 * h + 128] = u[0:128].astype(BF)
            uy[j, yy, 384:400] = extra.astype(BF)
        if i < 3:
            s1y[i].start()
    for i in (0, 1):
        wait_recv(g2[2 + i])
        share[i].start()
    wait_recv(g2[1])
    swap_wo = to_sib(wo, wo, 5)
    swap_wo.start()
    for i in (2, 3):
        wait_recv(g2[2 + i])
        share[i].start()
    s2x = scatter_two(mx, rx2, "x", s_u.at[:, 0])
    s2y = scatter_two(my, ry2, "y", s_u.at[:, 1])
    wait_recv(s1x)
    scatter_sum(ux, rx, mx, "x")
    start(s2x)
    wait_recv(s1y)
    scatter_sum(uy, ry, my, "y")
    start(s2y)
    for half, (copies, mid, rcv, first) in enumerate(((s2x, mx, rx2, "x"), (s2y, my, ry2, "y"))):
        wait_recv(copies)
        total = scatter_end(mid, rcv, first)
        for hh in range(3):
            h = half * 3 + hh
            for b in range(2):
                r = masks[b] / total[384 + 2 * hh + b : 385 + 2 * hh + b]
                rr[b, h : h + 1] = r
                mt[b, 64 * h : 64 * h + 64] = total[128 * hh + 64 * b : 128 * hh + 64 * b + 64] * r
    for b in range(2):
        mix[c, b] = flip(mt[b]).astype(BF)
    swap_mix = to_sib(mix.at[c], mix.at[c], 6)
    swap_mix.start()
    swap_wo.wait_recv()
    swap_mix.wait_recv()
    mixed = [mix[i].reshape(256, HALF) for i in range(2)]
    for cc in range(2):
        w = wo_all[cc].reshape(D, HALF)
        cols = slice(HALF * cc, HALF * cc + HALF)
        middle[:, cols] = (
            tok[...].reshape(256, D)[:, cols].astype(F32)
            + dot(mixed[0], w[0:HALF])
            + dot(mixed[1], w[HALF:D])
        )
    mid_v = middle[...]
    rms = rms_of(mid_v)
    nf[...] = (mid_v * rms * gf).astype(BF)
    swap_og.wait_recv()
    grad = og[...].reshape(256, D)
    share[0].wait_recv()
    share[1].wait_recv()
    for hf in range(2):
        hp = jnp.concatenate([dot(nf[...], wz[2 * hf + i].reshape(D, HALF)) for i in range(2)], axis=1)
        t = jnp.tanh(GELU_C * (hp + GELU_A * hp * hp * hp))
        hid[hf] = (0.5 * hp * (1.0 + t)).astype(BF)
        act[hf] = 0.5 * (1.0 + t) + 0.5 * hp * (1.0 - t * t) * (
            GELU_C * (1.0 + 3.0 * GELU_A * hp * hp)
        )

    def down_rows(m, b):
        return jnp.concatenate([wz[4 + b, m].reshape(192, HALF), wz[6 + b, m].reshape(192, HALF)], axis=0)

    lots = (
        (dwu.at[0], ru.at[0], mu.at[0], ru2.at[0], "x"),
        (dwu.at[1], ru.at[1], mu.at[1], ru2.at[1], "y"),
        (dws, rl.at[0], ml.at[0], rl2.at[0], "x"),
        (dwo, rl.at[1], ml.at[1], rl2.at[1], "y"),
        (
            dwv.at[:, :, pl.ds(0, 32)], rl.at[2, :, :, pl.ds(0, 32)], ml.at[2, :, pl.ds(0, 32)],
            rl2.at[2, :, pl.ds(0, 32)], "x",
        ),
        (
            dwv.at[:, :, pl.ds(32, 16)], rl.at[2, :, :, pl.ds(32, 16)], ml.at[2, :, pl.ds(32, 16)],
            rl2.at[2, :, pl.ds(32, 16)], "y",
        ),
    )
    w1 = [scatter_one(lot[0], lot[1], lot[4], s_w.at[:, i]) for i, lot in enumerate(lots)]
    w2 = [scatter_two(lot[2], lot[3], lot[4], s_w.at[:, i]) for i, lot in enumerate(lots)]

    def dw_part(shift, h):
        return dwd.at[lax.rem(z + 8 + shift, 4), pl.ds(2 * h, 2)]

    ways = (up, down)
    far = [remote(dw_part(2 - 4 * h, h), dfar.at[h], s_d, (0, h), ways[h]) for h in range(2)]
    near = [remote(dw_part(2 * h - 1, h), dnear.at[h], s_d, (1, h), ways[1 - h]) for h in range(2)]
    last = [remote(dsum.at[h], dlast.at[h], s_d, (2, h), ways[h]) for h in range(2)]
    share[2].wait_recv()
    share[3].wait_recv()
    for hf in range(2):
        for i in range(2):
            m = 2 * hf + i
            cols = slice(HALF * i, HALF * i + HALF)
            hg = dot_nt(grad[:, 0:HALF], down_rows(m, 0)) + dot_nt(grad[:, HALF:D], down_rows(m, 1))
            pgr[hf, :, cols] = (act[hf, :, cols] * hg).astype(BF)
            more = dot_nt(pgr[hf, :, cols], wz[m].reshape(D, HALF)).reshape(2, 2, 64, D)
            fng[...] = more if m == 0 else fng[...] + more
    swap_fng = to_sib(fng, fng_r, 7)
    swap_fng.start()
    for hf in range(2):
        grad_w = dot(flip(hid[hf]), grad).astype(BF)
        for i in range(2):
            for a in range(2):
                for q in range(4):
                    base = HALF * i + 192 * a + 48 * q
                    for b in range(2):
                        dwd[2 * a + b, 2 * hf + i, q] = grad_w[base : base + 48, HALF * b : HALF * b + HALF]
    start(far)
    start(near)
    swap_fng.wait_recv()
    full = (fng[...] + fng_r[...]).reshape(256, D)
    mid_v = middle[...]
    rms = rms_of(mid_v)
    gain_f = jnp.sum(full * mid_v * rms, axis=0, keepdims=True)
    weighted = full * gf
    inner = jnp.mean(weighted * mid_v, axis=-1, keepdims=True)
    mg = grad.astype(F32) + rms * weighted - mid_v * (rms * rms * rms) * inner
    mgrad[...] = mg.reshape(2, 2, 64, D)
    bg = mg.astype(BF)
    bgs[...] = bg
    xg = jnp.zeros((256, HALF), F32)
    for cc in range(2):
        w = wo_all[cc, pl.ds(2 * c, 2)].reshape(HALF, HALF)
        xg = xg + dot_nt(bg[:, HALF * cc : HALF * cc + HALF], w)
    deltas = []
    for b in range(2):
        xgt = flip(xg[128 * b : 128 * b + 128])
        for h in range(HH):
            rows = xgt[64 * h : 64 * h + 64]
            r = rr[b, h : h + 1]
            deltas.append(jnp.sum(rows * mt[b, 64 * h : 64 * h + 64], axis=0, keepdims=True) * r)
            own = gx if h < 3 else gy
            base = 128 * (h % 3) + 64 * b
            own[x, y, base : base + 64] = (rows * r).astype(BF)
    for own, first in ((gx, 0), (gy, 3)):
        rows = []
        for h in range(first, first + 3):
            d0, d1 = deltas[h], deltas[HH + h]
            h0 = d0.astype(BF).astype(F32)
            h1 = d1.astype(BF).astype(F32)
            rows = rows + [h0, h1, d0 - h0, d1 - h1]
        own[x, y, 384:400] = jnp.concatenate(rows + [jnp.zeros((4, 128), F32)], axis=0).astype(BF)
    a1x = gather_one(gx, "x", s_g.at[:, 0])
    a1y = gather_one(gy, "y", s_g.at[:, 1])
    a2x = gather_two(gx, "x", s_g.at[:, 0])
    a2y = gather_two(gy, "y", s_g.at[:, 1])
    start(a1x)
    start(a1y)
    dwu[0] = dot(flip(nf[...]), pgr[0]).astype(BF).reshape(4, 4, 48, D)
    wait_recv(a1x)
    start(a2x)
    wait_recv(a1y)
    start(a2y)
    dwu[1] = dot(flip(nf[...]), pgr[1]).astype(BF).reshape(4, 4, 48, D)
    start(w1[0])
    start(w1[1])
    for h in range(2):
        far[h].wait_recv()
        dsum[h] = (dw_part(1 - 2 * h, h)[...].astype(F32) + dfar[h].astype(F32)).astype(BF)
        last[h].start()
    bg_c = bgs[:, pl.ds(pl.multiple_of(HALF * c, 128), HALF)]
    for i in range(2):
        dwo[pl.ds(2 * i, 2)] = dot(flip(mixed[i]), bg_c).astype(BF).reshape(2, 4, 48, HALF)
    start(w1[3])
    for hf in range(2):
        down_w = [jnp.concatenate([down_rows(2 * hf, b), down_rows(2 * hf + 1, b)], axis=0) for b in range(2)]
        more = jnp.concatenate([dot(hid[hf], w) for w in down_w], axis=1).reshape(2, 2, 64, D)
        part[...] = more if hf == 0 else part[...] + more
    swap_part = to_sib(part.at[:, 1 - c], part_r, 8)
    swap_part.start()
    swap_fng.wait_send()
    fng[...] = middle[...].reshape(2, 2, 64, D)
    swap_part.wait_recv()
    out[...] = (fng[:, c] + (part[:, c] + part_r[...])).astype(BF)
    for h in range(2):
        near[h].wait_recv()
        last[h].wait_recv()
        total = dw_part(0, h)[...].astype(F32) + dnear[h].astype(F32) + dlast[h].astype(F32)
        dws[pl.ds(2 * h, 2)] = total.astype(BF)
    start(w1[2])
    wait_recv(a2x)
    wait_recv(a2y)

    def table_part(d, hf):
        buf = gx if hf == 0 else gy
        result = []
        for hh in range(3):
            h = 3 * hf + hh
            pair = []
            for i in range(2):
                k = 2 * d + i
                g = buf[k // 4, lax.rem(k, 4), 128 * hh : 128 * hh + 128]
                cols = pl.ds(pl.multiple_of(256 * d + 128 * i, 128), 128)
                extra = buf[k // 4, lax.rem(k, 4), 384:400].astype(F32)[4 * hh : 4 * hh + 4]
                s = dot(vals[h], g)
                s = s - mcol[0] * (extra[0:1] + extra[2:3])
                s = s - mcol[1] * (extra[1:2] + extra[3:4])
                pair.append(s * e[h, :, :, cols].reshape(128, 128).astype(F32))
            result.append(jnp.concatenate(pair, axis=1))
        return result

    def ring(send, recv, sems, t, hf, device):
        return remote(send.at[hf, t], recv.at[hf, t], sems, (hf, t), device)

    ups = [[ring(up_s, up_r, s_up, t, hf, up) for t in range(4 - hf)] for hf in range(2)]
    dns = [[ring(dn_s, dn_r, s_dn, t, hf, down) for t in range(3 + hf)] for hf in range(2)]

    def step(t):
        for copies, send, recv, hf, d in (
            (ups[0], up_s, up_r, 0, lax.rem(z + 12 - t, 8)),
            (dns[1], dn_s, dn_r, 1, lax.rem(z + 4 + t, 8)),
            (ups[1], up_s, up_r, 1, lax.rem(z + 11 - t, 8)),
            (dns[0], dn_s, dn_r, 0, lax.rem(z + 5 + t, 8)),
        ):
            if t >= len(copies):
                continue
            parts = table_part(d, hf)
            if t > 0:
                copies[t - 1].wait_recv()
            for hh in range(3):
                p = parts[hh]
                if t > 0:
                    p = p + recv[hf, t - 1, hh].astype(F32)
                send[hf, t, hh] = p.astype(BF)
            copies[t].start()

    step(0)
    for h in range(HH):
        buf = gx if h < 3 else gy
        total = jnp.zeros((128, 128), F32)
        for k in range(16):
            total = total + dot_nt(
                buf[k // 4, k % 4, 128 * (h % 3) : 128 * (h % 3) + 128], e[h, :, :, 128 * k : 128 * k + 128].reshape(128, 128)
            )
        for b in range(2):
            vgt[b, 64 * h : 64 * h + 64] = total[64 * b : 64 * b + 64] * masks[b]
    vg = jnp.concatenate([flip(vgt[b]) for b in range(2)], axis=0).astype(BF)
    dwv[...] = dot(flip(normed[...]), vg).astype(BF).reshape(4, 4, 48, HALF)
    start(w1[4])
    start(w1[5])
    swap_part.wait_send()
    part[...] = dot_nt(vg, wv[...].reshape(D, HALF)).reshape(2, 2, 64, D)
    swap_ng = to_sib(part, ng_r, 9)
    swap_ng.start()
    step(1)
    swap_ng.wait_recv()
    full = (part[...] + ng_r[...]).reshape(256, D)
    xv = tok[...].reshape(256, D).astype(F32)
    rms = rms_of(xv)
    gain_m = jnp.sum(full * xv * rms, axis=0, keepdims=True)
    weighted = full * gm
    inner = jnp.mean(weighted * xv, axis=-1, keepdims=True)
    fng[...] = (rms * weighted - xv * (rms * rms * rms) * inner).reshape(2, 2, 64, D)
    input_grad[...] = mgrad[:, c] + fng[:, c]
    gains = jnp.concatenate([gain_m, gain_f], axis=0)
    high = gains.astype(BF).astype(F32)
    gs[...] = jnp.concatenate([high, gains - high, jnp.zeros((12, D), F32)], axis=0).astype(BF)
    gr[x, y] = gs[...]
    gain1 = gather_one(gr, "x", s_gain)
    gain2 = gather_two(gr, "x", s_gain)
    start(gain1)

    def middle_sum(i):
        wait_recv(w1[i])
        src, rcv, mid, _, first = lots[i]
        scatter_sum(src, rcv, mid, first)
        start(w2[i])

    def last_sum(i):
        wait_recv(w2[i])
        _, _, mid, rcv, first = lots[i]
        return scatter_end(mid, rcv, first)

    def z_send(src, dst, i, j, k):
        return remote(src, dst, s_z, (i, j), at(lax.rem(z + k, 8), x, y, c))

    q = lax.rem(z, 4)

    def up_part(d):
        return up_sum.at[:, pl.ds(pl.multiple_of(HALF * lax.rem(d, 4), 128), HALF)]

    def rest_part(d):
        return rest.at[pl.ds(pl.multiple_of(16 * lax.rem(d, 4), 16), 16)]

    def z_first(part, buf, i, ks):
        return [z_send(part(z + k), buf.at[j], i, j, k) for j, k in enumerate(ks)]

    def z_half(part, buf, res):
        total = part(z)[...].astype(F32)
        for j in range(3):
            total = total + buf[j].astype(F32)
        res[...] = total.astype(BF)

    def z_swap(half, other, i):
        return z_send(half, other, i, 3, 4)

    def z_last(half, other, full, i, ks):
        full[q] = (half[...].astype(F32) + other[...].astype(F32)).astype(BF)
        return [z_send(full.at[q], full.at[q], i, 4 + j, k) for j, k in enumerate(ks)]

    middle_sum(0)
    middle_sum(1)
    step(2)
    middle_sum(2)
    middle_sum(3)
    for i in range(2):
        up_sum[:, D * i : D * i + D] = last_sum(i).astype(BF)
    z_up1 = z_first(up_part, zr_up, 0, (1, 2, 7))
    start(z_up1)
    middle_sum(4)
    middle_sum(5)
    wait_recv(gain1)
    start(gain2)
    step(3)
    half_down[...] = last_sum(2).astype(BF)
    z_down2 = z_swap(half_down, other_down, 1)
    z_down2.start()
    wait_recv(z_up1)
    z_half(up_part, zr_up, half_up)
    z_up2 = z_swap(half_up, other_up, 0)
    z_up2.start()
    rest[0:48, 0:HALF] = last_sum(3).astype(BF)
    rest[0:32, HALF:D] = last_sum(4).astype(BF)
    rest[32:48, HALF:D] = last_sum(5).astype(BF)
    wait_recv(gain2)
    gtot = jnp.sum(gr[...].reshape(16, 16, D).astype(F32), axis=0)
    gains = gtot[0:2] + gtot[2:4]
    high = gains.astype(BF).astype(F32)
    rest[48:64] = jnp.concatenate([high, gains - high, jnp.zeros((12, D), F32)], axis=0).astype(BF)
    z_rest1 = z_first(rest_part, zr_rest, 2, (7, 6, 1))
    start(z_rest1)
    z_down2.wait_recv()
    z_down3 = z_last(half_down, other_down, zs_down, 1, (1, 7, 6))
    start(z_down3)
    z_up2.wait_recv()
    z_up3 = z_last(half_up, other_up, zs_up, 0, (1, 7, 2))
    start(z_up3)
    wait_recv(z_rest1)
    z_half(rest_part, zr_rest, half_rest)
    z_rest2 = z_swap(half_rest, other_rest, 2)
    z_rest2.start()
    own = [table_part(z, hf) for hf in range(2)]
    swap_tg = to_sib(tgs, tg_r, 10)
    for hf in range(2):
        ups[hf][-1].wait_recv()
        dns[hf][-1].wait_recv()
        for hh in range(3):
            p = own[hf][hh] + (
                up_r[hf, 3 - hf, hh].astype(F32) + dn_r[hf, 2 + hf, hh].astype(F32)
            )
            act[0, 0:128, 0:256] = p
            tg[c, 3 * hf + hh] = act[0, pl.ds(pl.multiple_of(64 * c, 64), 64), 0:256]
            tgs[3 * hf + hh] = act[0, pl.ds(pl.multiple_of(64 * (1 - c), 64), 64), 0:256]
    swap_tg.start()
    z_rest2.wait_recv()
    z_rest3 = z_last(half_rest, other_rest, zs_rest, 2, (1, 7, 6))
    start(z_rest3)
    wait_recv(z_up3)
    wait_recv(z_down3)
    for a in range(2):
        for b in range(2):
            cols = slice(HALF * b, HALF * b + HALF)
            act[0, 48 * a : 48 * a + 48, cols] = zs_up[2 * a + b].astype(F32)
            d_down[48 * a : 48 * a + 48, cols] = zs_down[2 * a + b].astype(F32)
    wait_recv(z_rest3)
    act[0, 96:160] = zs_rest[...].reshape(64, D).astype(F32)
    for cc, ref in ((c, post.at[0]), (1 - c, post.at[1])):
        base = pl.multiple_of(24 * cc, 8)
        ref[:, 0:D] = act[0, pl.ds(base, 24)]
        ref[:, D : 2 * D] = act[0, pl.ds(base + 48, 24)]
        ref[:, 2 * D : 3 * D] = act[0, pl.ds(base + 96, 24)]
    swap_post = to_sib(post.at[1], post.at[2], 11)
    swap_post.start()
    gsum[...] = jnp.concatenate([act[0, 144:146] + act[0, 146:148], jnp.zeros((6, D), F32)], axis=0)
    swap_tg.wait_recv()
    tg[1 - c] = tg_r[...]
    swap_post.wait_recv()
    first_core = (c == 0).astype(F32)
    pair = (
        post[0] * first_core + post[2] * (1.0 - first_core),
        post[2] * first_core + post[0] * (1.0 - first_core),
    )
    for m in range(4):
        block = jnp.concatenate([p[:, HALF * m : HALF * m + HALF] for p in pair], axis=1).astype(BF)
        d_up[:, D * m : D * m + D] = dot_nt(block, perm[...])
    for cc in range(2):
        cols = slice(HALF * cc, HALF * cc + HALF)
        d_out[:, cols] = pair[cc][:, 2 * D : 2 * D + HALF]
        d_value[:, cols] = pair[cc][:, 2 * D + HALF : 3 * D]
    for copy in (
        swap_pre, swap_tok, swap_tab, swap_og, swap_wo, swap_mix, swap_ng, swap_tg, swap_post
    ):
        copy.wait_send()
    for group in g1 + g2 + w1 + w2 + ups + dns + [
        share, far, near, last,
        s1x, s1y, s2x, s2y, a1x, a1y, a2x, a2y, gain1, gain2,
        z_up1, [z_up2], z_up3, [z_down2], z_down3, z_rest1, [z_rest2], z_rest3,
    ]:
        wait_send(group)


def finish(out, input_grad, d_value, d_out, d_up, d_down, gsum, tg, *outs):
    for src, dst in zip((out, input_grad, d_value, d_out, d_up, d_down, tg), outs):
        dst[...] = src[...]
    s = lax.axis_index("seq")
    row = lax.broadcasted_iota(jnp.int32, (D, 128), 0)
    lane = lax.broadcasted_iota(jnp.int32, (D, 128), 1)
    pick = jnp.where(row == lane + 24 * s, 1.0, 0.0)
    for i in range(2):
        got = jnp.dot(gsum[...], pick, precision=lax.Precision.HIGHEST, preferred_element_type=F32)
        outs[7 + i][...] = got[i, 0:24]


def vmem(*shape, kind=BF):
    return pltpu.VMEM(shape, kind)


def dma(*shape):
    return pltpu.SemaphoreType.DMA(shape)


IN_VMEM = pl.BlockSpec(memory_space=pltpu.VMEM)


def per_device(tokens, lengths, w_value, w_out, w_up, w_down, gain_mix, gain_ffn, mix_table, out_grad):
    sd = jax.ShapeDtypeStruct
    shapes = [
        sd((2, 64, D), BF), sd((2, 64, D), F32), sd((24, D), F32), sd((24, D), F32), sd((24, 4 * D), F32),
        sd((96, D), F32), sd((8, D), F32), sd((2, HH, 64, 256), F32),
    ]
    raw = pl.pallas_call(
        layer,
        name="layer",
        out_shape=shapes,
        in_specs=[pl.BlockSpec(memory_space=pltpu.SMEM)] + [IN_VMEM] * 8 + [pl.BlockSpec(memory_space=pl.ANY)],
        out_specs=[IN_VMEM] * 8,
        scratch_shapes=[
            vmem(D, D), vmem(2, 24, 2 * D, kind=F32), vmem(2, 24, 2 * D, kind=F32),
            vmem(2, 2, 64, D), vmem(2, 2, 64, D), vmem(HH, 2, 64, 2048),
            vmem(4, 4, 48, HALF), vmem(2, 4, 4, 48, HALF), vmem(8, 4, 4, 48, HALF),
            vmem(4, 4, ROWS, 128), vmem(4, 4, ROWS, 128), vmem(3, 4, ROWS, 128), vmem(3, 4, ROWS, 128),
            vmem(4, ROWS, 128), vmem(4, ROWS, 128), vmem(3, ROWS, 128), vmem(3, ROWS, 128),
            vmem(2, HALF, 128, kind=F32), vmem(2, 8, 128, kind=F32), vmem(2, 2, 128, HALF), vmem(HH, 144, 128),
            vmem(HH, 128, 128), vmem(2, 128, 128, kind=F32), vmem(256, D), vmem(256, D, kind=F32), vmem(256, D),
            vmem(256, D), vmem(2, 256, D), vmem(2, 256, D), vmem(2, 256, D, kind=F32),
            vmem(2, 2, 64, D, kind=F32), vmem(2, 64, D, kind=F32), vmem(2, 2, 64, D, kind=F32),
            vmem(2, 2, 64, D, kind=F32), vmem(2, 2, 64, D, kind=F32),
            vmem(2, 4, 4, 48, D), vmem(4, 4, 4, 48, HALF), vmem(4, 4, 48, HALF), vmem(4, 4, 48, HALF),
            vmem(4, 4, 48, HALF), vmem(4, 4, ROWS, 128), vmem(4, 4, ROWS, 128),
            vmem(2, 3, 4, 48, D), vmem(3, 3, 4, 48, HALF), vmem(2, 4, 48, D), vmem(3, 4, 48, HALF),
            vmem(2, 3, 48, D), vmem(3, 3, 48, HALF),
            vmem(2, 2, 4, 48, HALF), vmem(2, 2, 4, 48, HALF), vmem(2, 2, 4, 48, HALF), vmem(2, 2, 4, 48, HALF),
            vmem(16, D), vmem(4, 4, 16, D),
            vmem(2, 4, 3, 128, 256), vmem(2, 4, 3, 128, 256), vmem(2, 4, 3, 128, 256), vmem(2, 4, 3, 128, 256),
            vmem(HH, 64, 256, kind=F32), vmem(HH, 64, 256, kind=F32), vmem(2, HALF, 128, kind=F32),
            vmem(2, 2, 64, D, kind=F32), vmem(48, 2 * D), vmem(64, D), vmem(3, 48, HALF), vmem(3, 16, D),
            vmem(48, HALF), vmem(48, HALF), vmem(16, D), vmem(48, HALF), vmem(48, HALF), vmem(16, D),
            vmem(4, 48, HALF), vmem(4, 48, HALF), vmem(4, 16, D),
            vmem(3, 24, 3 * D, kind=F32),
            dma(2, 12), dma(2, 6, 2, 3), dma(2, 2, 2), dma(2, 2, 2, 3), pltpu.SemaphoreType.DMA, dma(2, 2, 2, 3),
            dma(2, 6, 2, 3), dma(2, 3, 2), dma(2, 2, 3), dma(2, 2, 4), dma(2, 2, 4), dma(2, 3, 7),
        ],
        compiler_params=pltpu.CompilerParams(
            collective_id=0, has_side_effects=True, vmem_limit_bytes=63 << 20
        ),
    )(lengths, tokens, out_grad, w_value, w_out, w_up, w_down, gain_mix, gain_ffn, mix_table)
    out, input_grad, d_value, d_out, d_up, d_down, tg, mix_gain, ffn_gain = pl.pallas_call(
        finish,
        name="finish",
        out_shape=shapes[:6] + [shapes[7], sd((24,), F32), sd((24,), F32)],
        in_specs=[IN_VMEM] * 8,
        out_specs=[IN_VMEM] * 9,
    )(*raw)
    return (
        out, input_grad, d_value, d_out, d_up, d_down, mix_gain, ffn_gain, tg.reshape(HEADS, 64, 256),
    )


def solution(mesh):
    return jax.shard_map(
        per_device,
        mesh=mesh,
        in_specs=(
            P("dp", "seq", None),
            P("dp"),
            P("seq", None),
            P("seq", None),
            P("seq", None),
            P("seq", None),
            P(),
            P(),
            P(None, "seq", None),
            P("dp", "seq", None),
        ),
        out_specs=(
            P("dp", "seq", None),
            P("dp", "seq", None),
            P("seq", None),
            P("seq", None),
            P("seq", None),
            P("seq", None),
            P("seq"),
            P("seq"),
            P(None, "seq", "dp"),
        ),
        check_vma=False,
    )
```

```python
import jax
import jax.numpy as jnp
from jax import lax
from jax.experimental import pallas as pl
from jax.experimental.pallas import tpu as pltpu
from jax.sharding import PartitionSpec as P

D = 768
HALF = 384
HEADS = 12
HH = 6
EPS = 1e-06
MESH = pl.DeviceIdType.MESH
BF = jnp.bfloat16
F32 = jnp.float32
OFFS = (1, 3, 2)
ROWS = 400
SEMS = 204
GELU_C = 0.7978845608028654
GELU_A = 0.044715


def here():
    s = lax.axis_index("seq")
    return lax.axis_index("dp"), s // 8, (s // 2) % 4, s % 2


def at(z, x, y, c):
    return (z, (x * 4 + y) * 2 + c)


class Pool:
    def __init__(self, ref):
        self.ref, self.used = ref, 0

    def take(self):
        self.used += 1
        return self.ref.at[self.used - 1]


def remote(src, dst, send, recv, device):
    return pltpu.make_async_remote_copy(
        src_ref=src, dst_ref=dst, send_sem=send, recv_sem=recv, device_id=device, device_id_type=MESH
    )


class Batch:
    def __init__(self, pool, pieces, sent, got):
        self.send, self.recv = pool.take(), pool.take()
        self.all_sent, self.all_got = sent, got
        self.copies = [remote(src, dst, self.send, self.recv, device) for src, dst, device in pieces]

    def start(self):
        start(self.copies)

    def wait_recv(self):
        pltpu.make_async_copy(self.all_got, self.all_got, self.recv).wait()

    def wait_send(self):
        pltpu.make_async_copy(self.all_sent, self.all_sent, self.send).wait()


def along(first, k):
    z, x, y, c = here()
    if first == "x":
        return at(z, lax.rem(x + k, 4), y, c)
    return at(z, x, lax.rem(y + k, 4), c)


OTHER = {"x": "y", "y": "x"}


def own_at(first):
    _, x, y, _ = here()
    return x if first == "x" else y


def gather_one(buf, first, pool):
    _, x, y, _ = here()
    three = buf.at[0, pl.ds(0, 3)]
    return Batch(pool, [(buf.at[x, y], buf.at[x, y], along(first, k)) for k in OFFS], three, three)


def gather_two(buf, first, pool):
    _, x, y, _ = here()
    view = buf.at[:, y] if first == "x" else buf.at[x]
    three = buf.at[pl.ds(0, 3)]
    return Batch(pool, [(view, view, along(OTHER[first], k)) for k in OFFS], three, three)


class Bytes:
    def __init__(self, view, sem):
        self.view, self.sem = view, sem

    def wait_recv(self):
        pltpu.make_async_copy(self.view, self.view, self.sem).wait()

    wait_send = wait_recv


class Spread:
    def __init__(self, buf, first, pool):
        second = OTHER[first]
        mine = own_at(second)

        def part(k, half):
            place = lax.rem(mine + k, 4)
            pair = pl.ds(2 * half, 2)
            return buf.at[pair, place] if second == "y" else buf.at[place, pair]

        self.buf, self.send, self.recv = buf, pool.take(), pool.take()

        def send(k, half, way, recv):
            return remote(part(k, half), part(k, half), self.send, recv, along(second, way))

        self.early = [send(0, 0, 1, pool.take()), send(0, 1, 3, pool.take())]
        self.late = [send(0, 1, 1, self.recv), send(0, 0, 3, self.recv)]
        self.on = [send(3, 0, 1, self.recv), send(1, 1, 3, self.recv)]

    def start(self):
        start(self.early + self.late)

    def relay(self):
        for got, copy in zip(self.early, self.on):
            wait_recv([got])
            copy.start()

    def end(self):
        view = self.buf.at[pl.ds(0, 2)]
        wait_recv([Bytes(view, self.recv)])

    def sent(self):
        wait_send([Bytes(self.buf.at[pl.ds(0, 3)], self.send)])


class Sum:
    def __init__(self, src, rcv, first, pool):
        self.src, self.rcv, self.first = src, rcv, first
        self.send, self.recv = pool.take(), pool.take()
        self.mine = own_at(first)

        def send(k, half, slot, way, recv):
            return remote(
                self.part(k, half), rcv.at[slot, pl.ds(2 * half, 2)], self.send, recv, along(first, way)
            )

        self.far = [send(2, 0, 2, 1, pool.take()), send(2, 1, 2, 3, pool.take())]
        self.near = [send(1, 1, 0, 1, self.recv), send(3, 0, 1, 3, self.recv)]
        self.on = [send(1, 0, 0, 1, self.recv), send(3, 1, 1, 3, self.recv)]

    def part(self, k, half):
        place = lax.rem(self.mine + k, 4)
        pair = pl.ds(2 * half, 2)
        return self.src.at[place, pair] if self.first == "x" else self.src.at[pair, place]

    def start(self):
        start(self.far + self.near)

    def relay(self):
        for half in range(2):
            wait_recv([self.far[half]])
            part = self.part(1 + 2 * half, half)
            got = self.rcv[2, 2 * half : 2 * half + 2]
            part[...] = (part[...].astype(F32) + got.astype(F32)).astype(BF)
            self.on[half].start()

    def end(self, mid):
        wait_recv([Bytes(self.rcv.at[pl.ds(0, 2)], self.recv)])
        for j in range(4):
            own = self.src[self.mine, j] if self.first == "x" else self.src[j, self.mine]
            total = own.astype(F32) + self.rcv[0, j].astype(F32) + self.rcv[1, j].astype(F32)
            mid[j] = total.astype(BF)

    def sent(self):
        wait_send([Bytes(self.src.at[pl.ds(0, 3)], self.send)])


def scatter_two(mid, rcv, first, pool):
    second = OTHER[first]
    mine = own_at(second)
    pieces = [(mid.at[lax.rem(mine + k, 4)], rcv.at[i], along(second, k)) for i, k in enumerate(OFFS)]
    return Batch(pool, pieces, mid.at[pl.ds(0, 3)], rcv)


def scatter_end(mid, rcv, first):
    total = mid[own_at(OTHER[first])].astype(F32)
    for i in range(3):
        total = total + rcv[i].astype(F32)
    return total


def start(copies):
    for copy in copies:
        copy.start()


def wait_recv(copies):
    for copy in copies:
        copy.wait_recv()


def wait_send(copies):
    for copy in copies:
        copy.wait_send()


def signal(device):
    pl.semaphore_signal(
        pltpu.get_barrier_semaphore(), inc=1, device_id=device, device_id_type=MESH
    )


def greet():
    z, x, y, c = here()
    count = 0
    for k in range(1, 4):
        signal(at(z, lax.rem(x + k, 4), y, c))
        signal(at(z, x, lax.rem(y + k, 4), c))
        count += 2
    signal(at(z, x, y, 1 - c))
    count += 1
    for k in range(1, 8):
        signal(at(lax.rem(z + k, 8), x, y, c))
        count += 1
    return count


def meet(count):
    pl.semaphore_wait(pltpu.get_barrier_semaphore(), count)


def dot(a, b):
    return jnp.dot(a, b, preferred_element_type=F32)


def dot_nt(a, b):
    return lax.dot_general(a, b, (((1,), (1,)), ((), ())), preferred_element_type=F32)


def flip(a):
    return jnp.transpose(a)


def rms_of(v):
    return lax.rsqrt(jnp.mean(v * v, axis=-1, keepdims=True) + EPS)


def layer(
    lengths, tokens, out_grad, w_value, w_out, w_up, w_down, gain_mix, gain_ffn, table,
    out, input_grad, d_value, d_out, d_up, d_down, gsum, tg,
    perm, pre, got, tok, og, e, wv, wo_all, wz,
    ux, uy, rx, ry, mx, my, rx2, ry2, mt, rr, mix, vt, vals, mcol, normed, middle, nf, bgs, hid, pgr, act,
    part, part_r, fng, fng_r, mgrad, dwu, dwda, dwdb, dws, dwo, dwv, gx, gy,
    rd, rl, md, ml, rd2, rl2, dfar, dnear, dlast, dsum, gs, gr, up_s, up_r, dn_s, dn_r, tgs, tg_r, vgt, ng_r,
    down_sum, rest, zr_down, zr_rest, half_up, half_down, half_rest, other_up, other_down, other_rest,
    zs_up, zs_down, zs_rest, post_up, post_rest,
    out_s, ig_s, down_s, up_s_out, tgo, gsum_s, two_s,
    sems,
):
    z, x, y, c = here()
    sib = at(z, x, y, 1 - c)
    up = at(lax.rem(z + 1, 8), x, y, c)
    down = at(lax.rem(z + 7, 8), x, y, c)
    wo = wo_all.at[c]
    pool = Pool(sems)

    def to_sib(src, dst):
        return remote(src, dst, pool.take(), pool.take(), sib)

    saved = []

    def save(src, dst):
        copy = pltpu.make_async_copy(src, dst, pool.take())
        copy.start()
        saved.append(copy)

    count = greet()
    own_tab = pltpu.make_async_copy(table.at[pl.ds(6 * c, 6)], e.at[:, c], pool.take())
    own_tab.start()
    col = lax.broadcasted_iota(jnp.int32, (1, D), 1)
    odd = jnp.where(col >= HALF, 1, 0)
    low = col - HALF * odd
    half = jnp.where(low >= 192, 1, 0)
    low = low - 192 * half
    quad = jnp.where(low >= 48, 1, 0) + jnp.where(low >= 96, 1, 0) + jnp.where(low >= 144, 1, 0)
    origin = low + 144 * quad + 96 * odd + 48 * half
    perm[...] = jnp.where(lax.broadcasted_iota(jnp.int32, (D, D), 0) == origin, 1.0, 0.0).astype(BF)
    q = lax.rem(z, 4)
    for cc in range(2):
        cols = slice(HALF * cc, HALF * cc + HALF)
        pre[cc, :, 0:HALF] = w_out[:, cols].astype(F32)
        pre[cc, :, HALF:D] = w_value[:, cols].astype(F32)
    par = lax.rem(z, 2)
    for i in range(2):
        mine = dot(w_up[:, pl.ds(pl.multiple_of(D * (2 * par + i), D), D)], perm[...])
        for cc in range(2):
            pre[cc, :, D + HALF * i : D + HALF * i + HALF] = mine[:, HALF * cc : HALF * cc + HALF]
    meet(count)
    swap_pre = to_sib(pre.at[1 - c], got.at[c])
    swap_tok = to_sib(tokens, tok.at[:, c])
    swap_tab = to_sib(table.at[pl.ds(6 * (1 - c), 6)], e.at[:, c])
    swap_og = to_sib(out_grad, og.at[:, c])
    swap_pre.start()
    got[c] = pre[c]
    tok[:, c] = tokens[...]
    og[:, c] = out_grad[...]
    for b in range(2):
        rows = pl.ds(pl.multiple_of(48 * par, 16), 48)
        wz[4 + 2 * par + b, x, y] = w_down[rows, HALF * b : HALF * b + HALF]
    bufs = (
        (wv, "x"), (wo, "y"), (wz.at[2 * par], "x"), (wz.at[2 * par + 1], "y"),
        (wz.at[4 + 2 * par], "x"), (wz.at[5 + 2 * par], "y"),
    )
    g1 = [gather_one(buf, first, pool) for buf, first in bufs]
    g2 = [Spread(buf, first, pool) for buf, first in bufs]
    swap_pre.wait_recv()
    shard = got[...].reshape(48, 2 * D).astype(BF)
    wo[x, y] = shard[:, 0:HALF]
    wv[x, y] = shard[:, HALF:D]
    for i in range(2):
        wz[2 * par + i, x, y] = shard[:, D + HALF * i : D + HALF * i + HALF]
    order = (2, 3, 0, 1, 4, 5)
    for i in order:
        start([g1[i]])
    start([swap_tok, swap_tab, swap_og])

    share = [
        [
            remote(
                wz.at[4 * i + 2 * par + way], wz.at[4 * i + 2 * par + way], pool.take(), pool.take(), (up, down)[way]
            )
            for way in range(2)
        ]
        for i in range(2)
    ]
    for i in order:
        wait_recv([g1[i]])
        g2[i].start()
    swap_tok.wait_recv()
    values = tok[...].reshape(256, D).astype(F32)
    gm = gain_mix[...].reshape(1, D)
    gf = gain_ffn[...].reshape(1, D)
    normed[...] = (values * rms_of(values) * gm).astype(BF)
    place = (4 * x + y) * 128
    lane = lax.broadcasted_iota(jnp.int32, (1, 128), 1) + place
    row = lax.broadcasted_iota(jnp.int32, (128, 128), 0) + place
    masks = [jnp.where(lane < lengths[b], 1.0, 0.0) for b in range(2)]
    for b in range(2):
        mcol[b] = jnp.where(row < lengths[b], 1.0, 0.0)
    swap_tab.wait_recv()
    own_tab.wait()

    def exps(h, carry):
        e[h] = jnp.exp(e[h].astype(F32)).astype(BF)
        return carry

    lax.fori_loop(0, HH, exps, 0)
    for i in order:
        g2[i].relay()
    for way in range(2):
        g2[2 + way].end()
        share[0][way].start()
    g2[0].end()
    v = dot(normed[...], wv[...].reshape(D, HALF)).astype(BF).astype(F32)
    vall = flip(v) * jnp.concatenate(masks, axis=1)
    for h in range(HH):
        block = jnp.concatenate(
            [vall[64 * h : 64 * h + 64, 0:128], vall[64 * h : 64 * h + 64, 128:256]], axis=0
        )
        place = [jnp.zeros((2, 128), F32)] * (h % 3) + masks
        place = place + [jnp.zeros((14 - 2 * (h % 3), 128), F32)]
        vt[h] = jnp.concatenate([block] + place, axis=0).astype(BF)
        vals[h] = flip(block).astype(BF)

    s1x = Sum(ux, rx, "x", pool)
    s1y = Sum(uy, ry, "y", pool)
    for k in (2, 1, 3, 0):
        xx = lax.rem(x + k, 4)
        yy = lax.rem(y + k, 4)

        cols = pl.ds(pl.multiple_of(512 * xx, 512), 512)
        extra = jnp.zeros((16, 512), F32)
        for h in range(3):
            u = dot(vt[h], e[h, :, :, cols].reshape(128, 512))
            extra = extra + u[128:144]
            for j in range(4):
                ux[xx, j, 128 * h : 128 * h + 128] = u[0:128, 128 * j : 128 * j + 128].astype(BF)
        for j in range(4):
            ux[xx, j, 384:400] = extra[:, 128 * j : 128 * j + 128].astype(BF)
        if k == 2:
            start(s1x.far)
        elif k > 0:
            s1x.near[k // 2].start()
        for j in range(4):
            cols = pl.ds(pl.multiple_of(512 * j + 128 * yy, 128), 128)
            extra = jnp.zeros((16, 128), F32)
            for h in range(3):
                u = dot(vt[h + 3], e[h + 3, :, :, cols].reshape(128, 128))
                extra = extra + u[128:144]
                uy[j, yy, 128 * h : 128 * h + 128] = u[0:128].astype(BF)
            uy[j, yy, 384:400] = extra.astype(BF)
        if k == 2:
            start(s1y.far)
        elif k > 0:
            s1y.near[k // 2].start()
    g2[1].end()
    swap_wo = to_sib(wo, wo)
    swap_wo.start()
    for way in range(2):
        g2[4 + way].end()
        share[1][way].start()
    s1x.relay()
    s1y.relay()
    s2x = scatter_two(mx, rx2, "x", pool)
    s2y = scatter_two(my, ry2, "y", pool)
    for pattern in g2:
        pattern.sent()
    wait_send(g1)
    wait_send([swap_pre, swap_tok, swap_tab, swap_og])
    s1x.end(mx)
    start([s2x])
    s1y.end(my)
    start([s2y])
    for half, (copies, mid, rcv, first) in enumerate(((s2x, mx, rx2, "x"), (s2y, my, ry2, "y"))):
        wait_recv([copies])
        total = scatter_end(mid, rcv, first)
        for hh in range(3):
            h = half * 3 + hh
            for b in range(2):
                r = masks[b] / total[384 + 2 * hh + b : 385 + 2 * hh + b]
                rr[b, h : h + 1] = r
                mt[b, 64 * h : 64 * h + 64] = total[128 * hh + 64 * b : 128 * hh + 64 * b + 64] * r
    for b in range(2):
        mix[c, b] = flip(mt[b]).astype(BF)
    swap_mix = to_sib(mix.at[c], mix.at[c])
    swap_mix.start()
    swap_wo.wait_recv()
    swap_mix.wait_recv()
    mixed = [mix[i].reshape(256, HALF) for i in range(2)]
    for cc in range(2):
        w = wo_all[cc].reshape(D, HALF)
        cols = slice(HALF * cc, HALF * cc + HALF)
        middle[:, cols] = (
            tok[...].reshape(256, D)[:, cols].astype(F32)
            + dot(mixed[0], w[0:HALF])
            + dot(mixed[1], w[HALF:D])
        )
    mid_v = middle[...]
    rms = rms_of(mid_v)
    nf[...] = (mid_v * rms * gf).astype(BF)
    swap_og.wait_recv()
    grad = og[...].reshape(256, D)
    wait_recv(share[0])
    for hf in range(2):
        hp = jnp.concatenate([dot(nf[...], wz[2 * hf + i].reshape(D, HALF)) for i in range(2)], axis=1)
        t = jnp.tanh(GELU_C * (hp + GELU_A * hp * hp * hp))
        hid[hf] = (0.5 * hp * (1.0 + t)).astype(BF)
        act[hf] = 0.5 * (1.0 + t) + 0.5 * hp * (1.0 - t * t) * (
            GELU_C * (1.0 + 3.0 * GELU_A * hp * hp)
        )

    def down_rows(m, b):
        return jnp.concatenate([wz[4 + b, m].reshape(192, HALF), wz[6 + b, m].reshape(192, HALF)], axis=0)

    lots = (
        (dwda, rd.at[0], md.at[0], rd2.at[0], "x"),
        (dwdb, rd.at[1], md.at[1], rd2.at[1], "y"),
        (dws, rl.at[0], ml.at[0], rl2.at[0], "x"),
        (dwo, rl.at[1], ml.at[1], rl2.at[1], "y"),
        (
            dwv.at[:, :, pl.ds(0, 32)], rl.at[2, :, :, pl.ds(0, 32)], ml.at[2, :, pl.ds(0, 32)],
            rl2.at[2, :, pl.ds(0, 32)], "x",
        ),
        (
            dwv.at[:, :, pl.ds(32, 16)], rl.at[2, :, :, pl.ds(32, 16)], ml.at[2, :, pl.ds(32, 16)],
            rl2.at[2, :, pl.ds(32, 16)], "y",
        ),
    )
    def middle_sum(i):
        w1[i].end(lots[i][2])
        start([w2[i]])

    def last_sum(i):
        wait_recv([w2[i]])
        _, _, mid, rcv, first = lots[i]
        return scatter_end(mid, rcv, first)

    def z_at(k):
        return at(lax.rem(z + k, 8), x, y, c)

    def down_part(d):
        return down_sum.at[
            pl.ds(pl.multiple_of(48 * (lax.rem(d, 4) // 2), 16), 48),
            pl.ds(pl.multiple_of(HALF * lax.rem(d, 2), 128), HALF),
        ]

    def rest_part(d):
        return rest.at[pl.ds(pl.multiple_of(16 * lax.rem(d, 4), 16), 16)]

    def z_first(part, buf, ks):
        return Batch(pool, [(part(z + k), buf.at[j], z_at(k)) for j, k in enumerate(ks)], buf, buf)

    def z_half(part, buf, res):
        total = part(z)[...].astype(F32)
        for j in range(3):
            total = total + buf[j].astype(F32)
        res[...] = total.astype(BF)

    def z_swap(half, other):
        return remote(half, other, pool.take(), pool.take(), z_at(4))

    def z_last(half, other, full, ks):
        full[q] = (half[...].astype(F32) + other[...].astype(F32)).astype(BF)
        three = full.at[pl.ds(0, 3)]
        return Batch(pool, [(full.at[q], full.at[q], z_at(k)) for k in ks], three, three)

    w1 = [Sum(lot[0], lot[1], lot[4], pool) for lot in lots]
    w2 = [scatter_two(lot[2], lot[3], lot[4], pool) for lot in lots]

    def dw_part(shift, h):
        return dwu.at[lax.rem(z + 8 + shift, 4), pl.ds(2 * h, 2)]

    ways = (up, down)
    far = [remote(dw_part(2 - 4 * h, h), dfar.at[h], pool.take(), pool.take(), ways[h]) for h in range(2)]
    near = [remote(dw_part(2 * h - 1, h), dnear.at[h], pool.take(), pool.take(), ways[1 - h]) for h in range(2)]
    last = [remote(dsum.at[h], dlast.at[h], pool.take(), pool.take(), ways[h]) for h in range(2)]
    wait_recv(share[1])
    s1x.sent()
    s1y.sent()
    wait_send([s2x, s2y] + share[0] + [swap_wo, swap_mix])
    for hf in range(2):
        for i in range(2):
            m = 2 * hf + i
            cols = slice(HALF * i, HALF * i + HALF)
            hg = dot_nt(grad[:, 0:HALF], down_rows(m, 0)) + dot_nt(grad[:, HALF:D], down_rows(m, 1))
            pgr[hf, :, cols] = (act[hf, :, cols] * hg).astype(BF)
            more = dot_nt(pgr[hf, :, cols], wz[m].reshape(D, HALF)).reshape(2, 2, 64, D)
            fng[...] = more if m == 0 else fng[...] + more
    swap_fng = to_sib(fng, fng_r)
    swap_fng.start()
    for hf in range(2):
        grad_w = dot(flip(nf[...]), pgr[hf]).astype(BF)
        for i in range(2):
            dwu[2 * hf + i] = grad_w[:, HALF * i : HALF * i + HALF].reshape(4, 4, 48, HALF)
    start(far)
    swap_fng.wait_recv()
    full = (fng[...] + fng_r[...]).reshape(256, D)
    mid_v = middle[...]
    rms = rms_of(mid_v)
    gain_f = jnp.sum(full * mid_v * rms, axis=0, keepdims=True)
    weighted = full * gf
    inner = jnp.mean(weighted * mid_v, axis=-1, keepdims=True)
    mg = grad.astype(F32) + rms * weighted - mid_v * (rms * rms * rms) * inner
    mgrad[...] = mg.reshape(2, 2, 64, D)
    bg = mg.astype(BF)
    bgs[...] = bg
    xg = jnp.zeros((256, HALF), F32)
    for cc in range(2):
        w = wo_all[cc, pl.ds(2 * c, 2)].reshape(HALF, HALF)
        xg = xg + dot_nt(bg[:, HALF * cc : HALF * cc + HALF], w)
    deltas = []
    for b in range(2):
        xgt = flip(xg[128 * b : 128 * b + 128])
        for h in range(HH):
            rows = xgt[64 * h : 64 * h + 64]
            r = rr[b, h : h + 1]
            deltas.append(jnp.sum(rows * mt[b, 64 * h : 64 * h + 64], axis=0, keepdims=True) * r)
            own = gx if h < 3 else gy
            base = 128 * (h % 3) + 64 * b
            own[x, y, base : base + 64] = (rows * r).astype(BF)
    for own, first in ((gx, 0), (gy, 3)):
        rows = []
        for h in range(first, first + 3):
            d0, d1 = deltas[h], deltas[HH + h]
            h0 = d0.astype(BF).astype(F32)
            h1 = d1.astype(BF).astype(F32)
            rows = rows + [h0, h1, d0 - h0, d1 - h1]
        own[x, y, 384:400] = jnp.concatenate(rows + [jnp.zeros((4, 128), F32)], axis=0).astype(BF)
    parts_g = [
        (buf.at[:, :, pl.ds(base, size)], first)
        for buf in (gx, gy)
        for base, size, first in ((0, 208, "x"), (208, 192, "y"))
    ]
    a1 = [gather_one(buf, first, pool) for buf, first in parts_g]
    a2 = [Spread(buf, first, pool) for buf, first in parts_g]
    start(a1)
    start(near)
    for hf in range(2):
        grad_w = dot(flip(hid[hf]), grad).astype(BF)
        for i in range(2):
            for a in range(2):
                for k in range(4):
                    base = HALF * i + 192 * a + 48 * k
                    dwda[2 * hf + i, k, 48 * a : 48 * a + 48] = grad_w[base : base + 48, 0:HALF]
                    dwdb[2 * hf + i, k, 48 * a : 48 * a + 48] = grad_w[base : base + 48, HALF:D]
    for i in range(2):
        wait_recv([a1[i]])
        a2[i].start()
    bg_c = bgs[:, pl.ds(pl.multiple_of(HALF * c, 128), HALF)]
    for i in range(2):
        dwo[pl.ds(2 * i, 2)] = dot(flip(mixed[i]), bg_c).astype(BF).reshape(2, 4, 48, HALF)
    for hf in range(2):
        down_w = [jnp.concatenate([down_rows(2 * hf, b), down_rows(2 * hf + 1, b)], axis=0) for b in range(2)]
        more = jnp.concatenate([dot(hid[hf], w) for w in down_w], axis=1).reshape(2, 2, 64, D)
        part[...] = more if hf == 0 else part[...] + more
    swap_part = to_sib(part.at[:, 1 - c], part_r)
    swap_part.start()
    for i in range(2):
        a2[i].relay()
    for h in range(2):
        far[h].wait_recv()
        dsum[h] = (dw_part(1 - 2 * h, h)[...].astype(F32) + dfar[h].astype(F32)).astype(BF)
        last[h].start()
    for i in range(2, 4):
        wait_recv([a1[i]])
        a2[i].start()
    swap_fng.wait_send()
    fng[...] = middle[...].reshape(2, 2, 64, D)
    swap_part.wait_recv()
    out_s[...] = (fng[:, c] + (part[:, c] + part_r[...])).astype(BF)
    save(out_s, out)
    wait_send(a1)
    wait_send(far + share[1])
    for i in range(2):
        a2[i].end()

    def table_part(d, hf):
        buf = gx if hf == 0 else gy
        result = []
        for hh in range(3):
            h = 3 * hf + hh
            pair = []
            for i in range(2):
                k = 2 * d + i
                g = buf[k // 4, lax.rem(k, 4), 128 * hh : 128 * hh + 128]
                cols = pl.ds(pl.multiple_of(256 * d + 128 * i, 128), 128)
                extra = buf[k // 4, lax.rem(k, 4), 384:400].astype(F32)[4 * hh : 4 * hh + 4]
                s = dot(vals[h], g)
                s = s - mcol[0] * (extra[0:1] + extra[2:3])
                s = s - mcol[1] * (extra[1:2] + extra[3:4])
                pair.append(s * e[h, :, :, cols].reshape(128, 128).astype(F32))
            result.append(jnp.concatenate(pair, axis=1))
        return result

    def ring(send, recv, count, hf, device):
        sent = pool.take()
        return [
            remote(send.at[hf, t], recv.at[hf, t], sent, pool.take(), device) for t in range(count)
        ], Bytes(send.at[hf, pl.ds(0, count)], sent)

    ups, up_sent = zip(*[ring(up_s, up_r, 4 - hf, hf, up) for hf in range(2)])
    dns, dn_sent = zip(*[ring(dn_s, dn_r, 3 + hf, hf, down) for hf in range(2)])

    def step(t, hf):
        for copies, send, recv, d in (
            (ups[hf], up_s, up_r, lax.rem(z + 12 - hf - t, 8)),
            (dns[hf], dn_s, dn_r, lax.rem(z + 5 - hf + t, 8)),
        ):
            if t >= len(copies):
                continue
            parts = table_part(d, hf)
            if t > 0:
                copies[t - 1].wait_recv()
            for hh in range(3):
                p = parts[hh]
                if t > 0:
                    p = p + recv[hf, t - 1, hh].astype(F32)
                send[hf, t, hh] = p.astype(BF)
            copies[t].start()

    def value_part(hf):
        buf = (gx, gy)[hf]
        for hh in range(3):
            total = jnp.zeros((128, 128), F32)
            for k in range(16):
                cols = slice(128 * k, 128 * k + 128)
                total = total + dot_nt(
                    buf[k // 4, k % 4, 128 * hh : 128 * hh + 128], e[3 * hf + hh, :, :, cols].reshape(128, 128)
                )
            rows = slice(64 * (3 * hf + hh), 64 * (3 * hf + hh) + 64)
            for b in range(2):
                vgt[b, rows] = total[64 * b : 64 * b + 64] * masks[b]

    step(0, 0)
    for i in range(2, 4):
        a2[i].relay()
    w1[0].start()
    w1[1].start()
    value_part(0)
    for h in range(2):
        near[h].wait_recv()
        last[h].wait_recv()
        total = dw_part(0, h)[...].astype(F32) + dnear[h].astype(F32) + dlast[h].astype(F32)
        dws[pl.ds(2 * h, 2)] = total.astype(BF)
    w1[2].start()
    step(1, 0)
    for i in range(2, 4):
        a2[i].end()
    step(0, 1)
    value_part(1)
    vg = jnp.concatenate([flip(vgt[b]) for b in range(2)], axis=0).astype(BF)
    dwv[...] = dot(flip(normed[...]), vg).astype(BF).reshape(4, 4, 48, HALF)
    w1[4].start()
    w1[5].start()
    w1[3].start()
    swap_part.wait_send()
    part[...] = dot_nt(vg, wv[...].reshape(D, HALF)).reshape(2, 2, 64, D)
    swap_ng = to_sib(part, ng_r)
    swap_ng.start()
    w1[0].relay()
    w1[1].relay()
    for pattern in a2:
        pattern.sent()
    step(2, 0)
    w1[2].relay()
    w1[3].relay()
    step(1, 1)
    swap_ng.wait_recv()
    full = (part[...] + ng_r[...]).reshape(256, D)
    xv = tok[...].reshape(256, D).astype(F32)
    rms = rms_of(xv)
    gain_m = jnp.sum(full * xv * rms, axis=0, keepdims=True)
    weighted = full * gm
    inner = jnp.mean(weighted * xv, axis=-1, keepdims=True)
    fng[...] = (rms * weighted - xv * (rms * rms * rms) * inner).reshape(2, 2, 64, D)
    ig_s[...] = mgrad[:, c] + fng[:, c]
    save(ig_s, input_grad)
    gains = jnp.concatenate([gain_m, gain_f], axis=0)
    high = gains.astype(BF).astype(F32)
    gs[...] = jnp.concatenate([high, gains - high, jnp.zeros((12, D), F32)], axis=0).astype(BF)
    gr[x, y] = gs[...]
    gain1 = gather_one(gr, "x", pool)
    gain2 = gather_two(gr, "x", pool)
    start([gain1])

    def rows_of(src, base, cc):
        return src[0, pl.ds(pl.multiple_of(base + 24 * cc, 8), 24)]

    def finish_ring(hf):
        own = table_part(z, hf)
        ups[hf][-1].wait_recv()
        dns[hf][-1].wait_recv()
        for hh in range(3):
            h = 3 * hf + hh
            p = own[hh] + (up_r[hf, 3 - hf, hh].astype(F32) + dn_r[hf, 2 + hf, hh].astype(F32))
            act[1, 0:128, 0:256] = p
            tgo[h] = act[1, pl.ds(pl.multiple_of(64 * c, 64), 64), 0:256]
            tgs[h] = act[1, pl.ds(pl.multiple_of(64 * (1 - c), 64), 64), 0:256]
        swap_tg[hf].start()
        save(tgo.at[pl.ds(3 * hf, 3)], tg.at[c, pl.ds(3 * hf, 3)])

    swap_tg = [
        to_sib(tgs.at[pl.ds(3 * hf, 3)], tg_r.at[pl.ds(3 * hf, 3)]) for hf in range(2)
    ]
    w1[4].relay()
    w1[5].relay()
    step(3, 0)
    middle_sum(0)
    middle_sum(1)
    step(2, 1)
    middle_sum(2)
    middle_sum(3)
    wait_recv([gain1])
    start([gain2])
    middle_sum(4)
    middle_sum(5)
    for i in range(2):
        down_sum[:, HALF * i : HALF * i + HALF] = last_sum(i).astype(BF)
    z_down1 = z_first(down_part, zr_down, (1, 2, 7))
    start([z_down1])
    half_up[...] = last_sum(2).astype(BF)
    z_up2 = z_swap(half_up, other_up)
    z_up2.start()
    for pattern in w1[:3]:
        pattern.sent()
    wait_send(near + last)
    step(3, 1)
    rest[0:48, 0:HALF] = last_sum(3).astype(BF)
    rest[0:32, HALF:D] = last_sum(4).astype(BF)
    rest[32:48, HALF:D] = last_sum(5).astype(BF)
    wait_recv([gain2])
    gtot = jnp.sum(gr[...].reshape(16, 16, D).astype(F32), axis=0)
    gains = gtot[0:2] + gtot[2:4]
    high = gains.astype(BF).astype(F32)
    rest[48:64] = jnp.concatenate([high, gains - high, jnp.zeros((12, D), F32)], axis=0).astype(BF)
    z_rest1 = z_first(rest_part, zr_rest, (7, 6, 1))
    start([z_rest1])
    wait_recv([z_down1])
    z_half(down_part, zr_down, half_down)
    z_down2 = z_swap(half_down, other_down)
    z_down2.start()
    finish_ring(0)
    z_up2.wait_recv()
    z_up3 = z_last(half_up, other_up, zs_up, (1, 7, 2))
    start([z_up3])
    wait_recv([z_rest1])
    z_half(rest_part, zr_rest, half_rest)
    z_rest2 = z_swap(half_rest, other_rest)
    z_rest2.start()
    z_down2.wait_recv()
    z_down3 = z_last(half_down, other_down, zs_down, (1, 7, 6))
    start([z_down3])
    for pattern in w1[3:]:
        pattern.sent()
    wait_send(w2 + [z_down1, z_rest1, gain1, gain2])
    finish_ring(1)
    wait_recv([z_up3])
    for m in range(4):
        act[0, 48 * (m // 2) : 48 * (m // 2) + 48, HALF * (m % 2) : HALF * (m % 2) + HALF] = zs_up[m].astype(F32)
    for cc, ref in ((c, post_up.at[0]), (1 - c, post_up.at[1])):
        ref[:, 0:D] = rows_of(act, 0, cc)
        ref[:, D : 2 * D] = rows_of(act, 48, cc)
    swap_up = to_sib(post_up.at[1], post_up.at[2])
    swap_up.start()
    z_rest2.wait_recv()
    z_rest3 = z_last(half_rest, other_rest, zs_rest, (1, 7, 6))
    start([z_rest3])
    wait_recv([z_down3])
    for m in range(4):
        rows, cols = slice(48 * (m // 2), 48 * (m // 2) + 48), slice(HALF * (m % 2), HALF * (m % 2) + HALF)
        down_s[rows, cols] = zs_down[m].astype(F32)
    save(down_s, d_down)
    first_core = (c == 0).astype(F32)

    def by_core(ref):
        own, got = ref[0], ref[2]
        return own * first_core + got * (1.0 - first_core), got * first_core + own * (1.0 - first_core)

    swap_up.wait_recv()
    pair = by_core(post_up)
    for m in range(4):
        block = jnp.concatenate([p[:, HALF * m : HALF * m + HALF] for p in pair], axis=1).astype(BF)
        up_s_out[:, D * m : D * m + D] = dot_nt(block, perm[...])
    save(up_s_out, d_up)
    wait_recv([z_rest3])
    act[0, 0:64] = zs_rest[...].reshape(64, D).astype(F32)
    for cc, ref in ((c, post_rest.at[0]), (1 - c, post_rest.at[1])):
        ref[...] = rows_of(act, 0, cc)
    swap_rest = to_sib(post_rest.at[1], post_rest.at[2])
    swap_rest.start()
    gsum_s[...] = jnp.concatenate([act[0, 48:50] + act[0, 50:52], jnp.zeros((6, D), F32)], axis=0)
    save(gsum_s, gsum)
    for hf in range(2):
        swap_tg[hf].wait_recv()
        save(tg_r.at[pl.ds(3 * hf, 3)], tg.at[1 - c, pl.ds(3 * hf, 3)])
    swap_rest.wait_recv()
    pair = by_core(post_rest)
    for cc in range(2):
        cols = slice(HALF * cc, HALF * cc + HALF)
        two_s[0, :, cols] = pair[cc][:, 0:HALF]
        two_s[1, :, cols] = pair[cc][:, HALF:D]
    save(two_s.at[0], d_out)
    save(two_s.at[1], d_value)
    for copy in saved:
        copy.wait()
    wait_send(list(up_sent + dn_sent) + swap_tg + [z_up3, z_down3, z_rest3])
    assert pool.used == SEMS, pool.used
    wait_send([swap_ng, swap_up, swap_rest, z_up2, z_down2, z_rest2])


def finish(out, input_grad, d_value, d_out, d_up, d_down, gsum, tg, *outs):
    for src, dst in zip((out, input_grad, d_value, d_out, d_up, d_down, tg), outs):
        dst[...] = src[...]
    s = lax.axis_index("seq")
    row = lax.broadcasted_iota(jnp.int32, (D, 128), 0)
    lane = lax.broadcasted_iota(jnp.int32, (D, 128), 1)
    pick = jnp.where(row == lane + 24 * s, 1.0, 0.0)
    for i in range(2):
        got = jnp.dot(gsum[...], pick, precision=lax.Precision.HIGHEST, preferred_element_type=F32)
        outs[7 + i][...] = got[i, 0:24]


def vmem(*shape, kind=BF):
    return pltpu.VMEM(shape, kind)


IN_VMEM = pl.BlockSpec(memory_space=pltpu.VMEM)
ANY = pl.BlockSpec(memory_space=pl.ANY)


def per_device(tokens, lengths, w_value, w_out, w_up, w_down, gain_mix, gain_ffn, mix_table, out_grad):
    sd = jax.ShapeDtypeStruct
    shapes = [
        sd((2, 64, D), BF), sd((2, 64, D), F32), sd((24, D), F32), sd((24, D), F32), sd((24, 4 * D), F32),
        sd((96, D), F32), sd((8, D), F32), sd((2, HH, 64, 256), F32),
    ]
    raw = pl.pallas_call(
        layer,
        name="layer",
        out_shape=shapes,
        in_specs=[pl.BlockSpec(memory_space=pltpu.SMEM)] + [IN_VMEM] * 8 + [pl.BlockSpec(memory_space=pl.ANY)],
        out_specs=[ANY] * 8,
        scratch_shapes=[
            vmem(D, D), vmem(2, 24, 2 * D, kind=F32), vmem(2, 24, 2 * D, kind=F32),
            vmem(2, 2, 64, D), vmem(2, 2, 64, D), vmem(HH, 2, 64, 2048),
            vmem(4, 4, 48, HALF), vmem(2, 4, 4, 48, HALF), vmem(8, 4, 4, 48, HALF),
            vmem(4, 4, ROWS, 128), vmem(4, 4, ROWS, 128), vmem(3, 4, ROWS, 128), vmem(3, 4, ROWS, 128),
            vmem(4, ROWS, 128), vmem(4, ROWS, 128), vmem(3, ROWS, 128), vmem(3, ROWS, 128),
            vmem(2, HALF, 128, kind=F32), vmem(2, 8, 128, kind=F32), vmem(2, 2, 128, HALF), vmem(HH, 144, 128),
            vmem(HH, 128, 128), vmem(2, 128, 128, kind=F32), vmem(256, D), vmem(256, D, kind=F32), vmem(256, D),
            vmem(256, D), vmem(2, 256, D), vmem(2, 256, D), vmem(2, 256, D, kind=F32),
            vmem(2, 2, 64, D, kind=F32), vmem(2, 64, D, kind=F32), vmem(2, 2, 64, D, kind=F32),
            vmem(2, 2, 64, D, kind=F32), vmem(2, 2, 64, D, kind=F32),
            vmem(4, 4, 4, 48, HALF), vmem(4, 4, 96, HALF), vmem(4, 4, 96, HALF), vmem(4, 4, 48, HALF), vmem(4, 4, 48, HALF),
            vmem(4, 4, 48, HALF), vmem(4, 4, ROWS, 128), vmem(4, 4, ROWS, 128),
            vmem(2, 3, 4, 96, HALF), vmem(3, 3, 4, 48, HALF), vmem(2, 4, 96, HALF), vmem(3, 4, 48, HALF),
            vmem(2, 3, 96, HALF), vmem(3, 3, 48, HALF),
            vmem(2, 2, 4, 48, HALF), vmem(2, 2, 4, 48, HALF), vmem(2, 2, 4, 48, HALF), vmem(2, 2, 4, 48, HALF),
            vmem(16, D), vmem(4, 4, 16, D),
            vmem(2, 4, 3, 128, 256), vmem(2, 4, 3, 128, 256), vmem(2, 4, 3, 128, 256), vmem(2, 4, 3, 128, 256),
            vmem(HH, 64, 256, kind=F32), vmem(HH, 64, 256, kind=F32), vmem(2, HALF, 128, kind=F32),
            vmem(2, 2, 64, D, kind=F32), vmem(96, D), vmem(64, D), vmem(3, 48, HALF), vmem(3, 16, D),
            vmem(48, HALF), vmem(48, HALF), vmem(16, D), vmem(48, HALF), vmem(48, HALF), vmem(16, D),
            vmem(4, 48, HALF), vmem(4, 48, HALF), vmem(4, 16, D),
            vmem(3, 24, 2 * D, kind=F32), vmem(3, 24, D, kind=F32), vmem(2, 64, D), vmem(2, 64, D, kind=F32),
            vmem(96, D, kind=F32), vmem(24, 4 * D, kind=F32), vmem(HH, 64, 256, kind=F32),
            vmem(8, D, kind=F32), vmem(2, 24, D, kind=F32),
            pltpu.SemaphoreType.DMA((SEMS,)),
        ],
        compiler_params=pltpu.CompilerParams(
            collective_id=0, has_side_effects=True, vmem_limit_bytes=63 << 20
        ),
    )(lengths, tokens, out_grad, w_value, w_out, w_up, w_down, gain_mix, gain_ffn, mix_table)
    out, input_grad, d_value, d_out, d_up, d_down, tg, mix_gain, ffn_gain = pl.pallas_call(
        finish,
        name="finish",
        out_shape=shapes[:6] + [shapes[7], sd((24,), F32), sd((24,), F32)],
        in_specs=[IN_VMEM] * 8,
        out_specs=[IN_VMEM] * 9,
    )(*raw)
    return (
        out, input_grad, d_value, d_out, d_up, d_down, mix_gain, ffn_gain, tg.reshape(HEADS, 64, 256),
    )


def solution(mesh):
    return jax.shard_map(
        per_device,
        mesh=mesh,
        in_specs=(
            P("dp", "seq", None),
            P("dp"),
            P("seq", None),
            P("seq", None),
            P("seq", None),
            P("seq", None),
            P(),
            P(),
            P(None, "seq", None),
            P("dp", "seq", None),
        ),
        out_specs=(
            P("dp", "seq", None),
            P("dp", "seq", None),
            P("seq", None),
            P("seq", None),
            P("seq", None),
            P("seq", None),
            P("seq"),
            P("seq"),
            P(None, "seq", "dp"),
        ),
        check_vma=False,
    )
```

```python
import jax
import jax.numpy as jnp
from jax import lax
from jax.experimental import pallas as pl
from jax.experimental.pallas import tpu as pltpu
from jax.sharding import PartitionSpec as P

D = 768
HALF = 384
HEADS = 12
HH = 6
EPS = 1e-06
MESH = pl.DeviceIdType.MESH
BF = jnp.bfloat16
F32 = jnp.float32
OFFS = (1, 3, 2)
ROWS = 400
SEMS = 206
GELU_C = 0.7978845608028654
GELU_A = 0.044715


def here():
    s = lax.axis_index("seq")
    return lax.axis_index("dp"), s // 8, (s // 2) % 4, s % 2


def at(z, x, y, c):
    return (z, (x * 4 + y) * 2 + c)


class Pool:
    def __init__(self, ref):
        self.ref, self.used = ref, 0

    def take(self):
        self.used += 1
        return self.ref.at[self.used - 1]


def remote(src, dst, send, recv, device):
    return pltpu.make_async_remote_copy(
        src_ref=src, dst_ref=dst, send_sem=send, recv_sem=recv, device_id=device, device_id_type=MESH
    )


class Batch:
    def __init__(self, pool, pieces, sent, got):
        self.send, self.recv = pool.take(), pool.take()
        self.all_sent, self.all_got = sent, got
        self.copies = [remote(src, dst, self.send, self.recv, device) for src, dst, device in pieces]

    def start(self):
        start(self.copies)

    def wait_recv(self):
        pltpu.make_async_copy(self.all_got, self.all_got, self.recv).wait()

    def wait_send(self):
        pltpu.make_async_copy(self.all_sent, self.all_sent, self.send).wait()


def along(first, k):
    z, x, y, c = here()
    if first == "x":
        return at(z, lax.rem(x + k, 4), y, c)
    return at(z, x, lax.rem(y + k, 4), c)


OTHER = {"x": "y", "y": "x"}


def own_at(first):
    _, x, y, _ = here()
    return x if first == "x" else y


def gather_one(buf, first, pool):
    _, x, y, _ = here()
    three = buf.at[0, pl.ds(0, 3)]
    return Batch(pool, [(buf.at[x, y], buf.at[x, y], along(first, k)) for k in OFFS], three, three)


def gather_two(buf, first, pool):
    _, x, y, _ = here()
    view = buf.at[:, y] if first == "x" else buf.at[x]
    three = buf.at[pl.ds(0, 3)]
    return Batch(pool, [(view, view, along(OTHER[first], k)) for k in OFFS], three, three)


class Bytes:
    def __init__(self, view, sem):
        self.view, self.sem = view, sem

    def wait_recv(self):
        pltpu.make_async_copy(self.view, self.view, self.sem).wait()

    wait_send = wait_recv


class Spread:
    def __init__(self, buf, first, pool):
        second = OTHER[first]
        mine = own_at(second)

        def part(k, half):
            place = lax.rem(mine + k, 4)
            pair = pl.ds(2 * half, 2)
            return buf.at[pair, place] if second == "y" else buf.at[place, pair]

        self.buf, self.send, self.recv = buf, pool.take(), pool.take()

        def send(k, half, way, recv):
            return remote(part(k, half), part(k, half), self.send, recv, along(second, way))

        self.early = [send(0, 0, 1, pool.take()), send(0, 1, 3, pool.take())]
        self.late = [send(0, 1, 1, self.recv), send(0, 0, 3, self.recv)]
        self.on = [send(3, 0, 1, self.recv), send(1, 1, 3, self.recv)]

    def start(self):
        start(self.early + self.late)

    def relay(self):
        for got, copy in zip(self.early, self.on):
            wait_recv([got])
            copy.start()

    def end(self):
        view = self.buf.at[pl.ds(0, 2)]
        wait_recv([Bytes(view, self.recv)])

    def sent(self):
        wait_send([Bytes(self.buf.at[pl.ds(0, 3)], self.send)])


class Sum:
    def __init__(self, src, rcv, first, pool):
        self.src, self.rcv, self.first = src, rcv, first
        self.send, self.recv = pool.take(), pool.take()
        self.mine = own_at(first)

        def send(k, half, slot, way, recv):
            return remote(
                self.part(k, half), rcv.at[slot, pl.ds(2 * half, 2)], self.send, recv, along(first, way)
            )

        self.far = [send(2, 0, 2, 1, pool.take()), send(2, 1, 2, 3, pool.take())]
        self.near = [send(1, 1, 0, 1, self.recv), send(3, 0, 1, 3, self.recv)]
        self.on = [send(1, 0, 0, 1, self.recv), send(3, 1, 1, 3, self.recv)]

    def part(self, k, half):
        place = lax.rem(self.mine + k, 4)
        pair = pl.ds(2 * half, 2)
        return self.src.at[place, pair] if self.first == "x" else self.src.at[pair, place]

    def start(self):
        start(self.far + self.near)

    def relay(self):
        for half in range(2):
            wait_recv([self.far[half]])
            part = self.part(1 + 2 * half, half)
            got = self.rcv[2, 2 * half : 2 * half + 2]
            part[...] = (part[...].astype(F32) + got.astype(F32)).astype(BF)
            self.on[half].start()

    def end(self, mid):
        wait_recv([Bytes(self.rcv.at[pl.ds(0, 2)], self.recv)])
        for j in range(4):
            own = self.src[self.mine, j] if self.first == "x" else self.src[j, self.mine]
            total = own.astype(F32) + self.rcv[0, j].astype(F32) + self.rcv[1, j].astype(F32)
            mid[j] = total.astype(BF)

    def sent(self):
        wait_send([Bytes(self.src.at[pl.ds(0, 3)], self.send)])


def scatter_two(mid, rcv, first, pool):
    second = OTHER[first]
    mine = own_at(second)
    pieces = [(mid.at[lax.rem(mine + k, 4)], rcv.at[i], along(second, k)) for i, k in enumerate(OFFS)]
    return Batch(pool, pieces, mid.at[pl.ds(0, 3)], rcv)


def scatter_end(mid, rcv, first):
    total = mid[own_at(OTHER[first])].astype(F32)
    for i in range(3):
        total = total + rcv[i].astype(F32)
    return total


def start(copies):
    for copy in copies:
        copy.start()


def wait_recv(copies):
    for copy in copies:
        copy.wait_recv()


def wait_send(copies):
    for copy in copies:
        copy.wait_send()


def signal(device):
    pl.semaphore_signal(
        pltpu.get_barrier_semaphore(), inc=1, device_id=device, device_id_type=MESH
    )


def greet():
    z, x, y, c = here()
    count = 0
    for k in range(1, 4):
        signal(at(z, lax.rem(x + k, 4), y, c))
        signal(at(z, x, lax.rem(y + k, 4), c))
        count += 2
    signal(at(z, x, y, 1 - c))
    count += 1
    for k in range(1, 8):
        signal(at(lax.rem(z + k, 8), x, y, c))
        count += 1
    return count


def meet(count):
    pl.semaphore_wait(pltpu.get_barrier_semaphore(), count)


def dot(a, b):
    return jnp.dot(a, b, preferred_element_type=F32)


def dot_nt(a, b):
    return lax.dot_general(a, b, (((1,), (1,)), ((), ())), preferred_element_type=F32)


def flip(a):
    return jnp.transpose(a)


def rms_of(v):
    return lax.rsqrt(jnp.mean(v * v, axis=-1, keepdims=True) + EPS)


def layer(
    lengths, tokens, out_grad, w_value, w_out, w_up, w_down, gain_mix, gain_ffn, table,
    out, input_grad, d_value, d_out, d_up, d_down, gsum, tg,
    perm, pre_a, pre_b, got_a, got_b, tok, og, e, wv, wo_all, wz,
    ux, uy, rx, ry, mx, my, rx2, ry2, mt, rr, mix, vt, vals, mcol, normed, middle, nf, bgs, hid, pgr, act,
    part, part_r, fng, fng_r, mgrad, dwu, dwda, dwdb, dws, dwo, dwv, gx, gy,
    rd, rl, md, ml, rd2, rl2, dfar, dnear, dlast, dsum, gs, gr, up_s, up_r, dn_s, dn_r, tgs, tg_r, vgt, ng_r,
    down_sum, rest, zr_down, zr_rest, half_up, half_down, half_rest, other_up, other_down, other_rest,
    zs_up, zs_down, zs_rest, post_up, post_rest,
    out_s, ig_s, down_s, up_s_out, tgo, gsum_s, two_s,
    sems,
):
    z, x, y, c = here()
    sib = at(z, x, y, 1 - c)
    up = at(lax.rem(z + 1, 8), x, y, c)
    down = at(lax.rem(z + 7, 8), x, y, c)
    wo = wo_all.at[c]
    pool = Pool(sems)

    def to_sib(src, dst):
        return remote(src, dst, pool.take(), pool.take(), sib)

    saved = []

    def save(src, dst):
        copy = pltpu.make_async_copy(src, dst, pool.take())
        copy.start()
        saved.append(copy)

    count = greet()
    own_tab = pltpu.make_async_copy(table.at[pl.ds(6 * c, 6)], e.at[:, c], pool.take())
    own_tab.start()
    q = lax.rem(z, 4)
    par = lax.rem(z, 2)
    for cc in range(2):
        cols = slice(HALF * cc, HALF * cc + HALF)
        pre_a[cc, :, 0:HALF] = w_out[:, cols].astype(F32)
        pre_a[cc, :, HALF:D] = w_value[:, cols].astype(F32)
    meet(count)
    swap_a = to_sib(pre_a.at[1 - c], got_a.at[c])
    swap_a.start()
    got_a[c] = pre_a[c]
    col = lax.broadcasted_iota(jnp.int32, (1, D), 1)
    odd = jnp.where(col >= HALF, 1, 0)
    low = col - HALF * odd
    half = jnp.where(low >= 192, 1, 0)
    low = low - 192 * half
    quad = jnp.where(low >= 48, 1, 0) + jnp.where(low >= 96, 1, 0) + jnp.where(low >= 144, 1, 0)
    origin = low + 144 * quad + 96 * odd + 48 * half
    perm[...] = jnp.where(lax.broadcasted_iota(jnp.int32, (D, D), 0) == origin, 1.0, 0.0).astype(BF)
    for i in range(2):
        mine = dot(w_up[:, pl.ds(pl.multiple_of(D * (2 * par + i), D), D)], perm[...])
        for cc in range(2):
            pre_b[cc, :, HALF * i : HALF * i + HALF] = mine[:, HALF * cc : HALF * cc + HALF]
    swap_b = to_sib(pre_b.at[1 - c], got_b.at[c])
    swap_b.start()
    got_b[c] = pre_b[c]
    bufs = (
        (wv, "x"), (wo, "y"), (wz.at[2 * par], "x"), (wz.at[2 * par + 1], "y"),
        (wz.at[4 + 2 * par], "x"), (wz.at[5 + 2 * par], "y"),
    )
    g1 = [gather_one(buf, first, pool) for buf, first in bufs]
    g2 = [Spread(buf, first, pool) for buf, first in bufs]
    swap_a.wait_recv()
    shard = got_a[...].reshape(48, D).astype(BF)
    wo[x, y] = shard[:, 0:HALF]
    wv[x, y] = shard[:, HALF:D]
    start(g1[0:2])
    swap_tok = to_sib(tokens, tok.at[:, c])
    swap_tab = to_sib(table.at[pl.ds(6 * (1 - c), 6)], e.at[:, c])
    swap_og = to_sib(out_grad, og.at[:, c])
    start([swap_tok, swap_tab, swap_og])
    tok[:, c] = tokens[...]
    og[:, c] = out_grad[...]
    for b in range(2):
        rows = pl.ds(pl.multiple_of(48 * par, 16), 48)
        wz[4 + 2 * par + b, x, y] = w_down[rows, HALF * b : HALF * b + HALF]
    swap_b.wait_recv()
    shard = got_b[...].reshape(48, D).astype(BF)
    for i in range(2):
        wz[2 * par + i, x, y] = shard[:, HALF * i : HALF * i + HALF]
    start(g1[2:4])
    share = [
        [
            remote(
                wz.at[4 * i + 2 * par + way], wz.at[4 * i + 2 * par + way], pool.take(), pool.take(), (up, down)[way]
            )
            for way in range(2)
        ]
        for i in range(2)
    ]
    for i in range(4):
        wait_recv([g1[i]])
        g2[i].start()
    start(g1[4:6])
    swap_tok.wait_recv()
    values = tok[...].reshape(256, D).astype(F32)
    gm = gain_mix[...].reshape(1, D)
    gf = gain_ffn[...].reshape(1, D)
    normed[...] = (values * rms_of(values) * gm).astype(BF)
    place = (4 * x + y) * 128
    lane = lax.broadcasted_iota(jnp.int32, (1, 128), 1) + place
    row = lax.broadcasted_iota(jnp.int32, (128, 128), 0) + place
    masks = [jnp.where(lane < lengths[b], 1.0, 0.0) for b in range(2)]
    for b in range(2):
        mcol[b] = jnp.where(row < lengths[b], 1.0, 0.0)
    swap_tab.wait_recv()
    own_tab.wait()

    def exps(h, carry):
        e[h] = jnp.exp(e[h].astype(F32)).astype(BF)
        return carry

    lax.fori_loop(0, HH, exps, 0)
    for i in range(4):
        g2[i].relay()
    for i in (4, 5):
        wait_recv([g1[i]])
        g2[i].start()
    g2[0].end()
    v = dot(normed[...], wv[...].reshape(D, HALF)).astype(BF).astype(F32)
    vall = flip(v) * jnp.concatenate(masks, axis=1)
    for h in range(HH):
        block = jnp.concatenate(
            [vall[64 * h : 64 * h + 64, 0:128], vall[64 * h : 64 * h + 64, 128:256]], axis=0
        )
        place = [jnp.zeros((2, 128), F32)] * (h % 3) + masks
        place = place + [jnp.zeros((14 - 2 * (h % 3), 128), F32)]
        vt[h] = jnp.concatenate([block] + place, axis=0).astype(BF)
        vals[h] = flip(block).astype(BF)

    s1x = Sum(ux, rx, "x", pool)
    s1y = Sum(uy, ry, "y", pool)
    for k in (2, 1, 3, 0):
        xx = lax.rem(x + k, 4)
        yy = lax.rem(y + k, 4)

        cols = pl.ds(pl.multiple_of(512 * xx, 512), 512)
        extra = jnp.zeros((16, 512), F32)
        for h in range(3):
            u = dot(vt[h], e[h, :, :, cols].reshape(128, 512))
            extra = extra + u[128:144]
            for j in range(4):
                ux[xx, j, 128 * h : 128 * h + 128] = u[0:128, 128 * j : 128 * j + 128].astype(BF)
        for j in range(4):
            ux[xx, j, 384:400] = extra[:, 128 * j : 128 * j + 128].astype(BF)
        if k == 2:
            start(s1x.far)
        elif k > 0:
            s1x.near[k // 2].start()
        for j in range(4):
            cols = pl.ds(pl.multiple_of(512 * j + 128 * yy, 128), 128)
            extra = jnp.zeros((16, 128), F32)
            for h in range(3):
                u = dot(vt[h + 3], e[h + 3, :, :, cols].reshape(128, 128))
                extra = extra + u[128:144]
                uy[j, yy, 128 * h : 128 * h + 128] = u[0:128].astype(BF)
            uy[j, yy, 384:400] = extra.astype(BF)
        if k == 2:
            start(s1y.far)
        elif k > 0:
            s1y.near[k // 2].start()
    for way in range(2):
        g2[2 + way].end()
        share[0][way].start()
    g2[1].end()
    swap_wo = to_sib(wo, wo)
    swap_wo.start()
    g2[4].relay()
    g2[5].relay()
    s1x.relay()
    s1y.relay()
    for way in range(2):
        g2[4 + way].end()
        share[1][way].start()
    s2x = scatter_two(mx, rx2, "x", pool)
    s2y = scatter_two(my, ry2, "y", pool)
    for pattern in g2:
        pattern.sent()
    wait_send(g1)
    wait_send([swap_a, swap_b, swap_tok, swap_tab, swap_og])
    s1x.end(mx)
    start([s2x])
    s1y.end(my)
    start([s2y])
    for half, (copies, mid, rcv, first) in enumerate(((s2x, mx, rx2, "x"), (s2y, my, ry2, "y"))):
        wait_recv([copies])
        total = scatter_end(mid, rcv, first)
        for hh in range(3):
            h = half * 3 + hh
            for b in range(2):
                r = masks[b] / total[384 + 2 * hh + b : 385 + 2 * hh + b]
                rr[b, h : h + 1] = r
                mt[b, 64 * h : 64 * h + 64] = total[128 * hh + 64 * b : 128 * hh + 64 * b + 64] * r
    for b in range(2):
        mix[c, b] = flip(mt[b]).astype(BF)
    swap_mix = to_sib(mix.at[c], mix.at[c])
    swap_mix.start()
    swap_wo.wait_recv()
    swap_mix.wait_recv()
    mixed = [mix[i].reshape(256, HALF) for i in range(2)]
    for cc in range(2):
        w = wo_all[cc].reshape(D, HALF)
        cols = slice(HALF * cc, HALF * cc + HALF)
        middle[:, cols] = (
            tok[...].reshape(256, D)[:, cols].astype(F32)
            + dot(mixed[0], w[0:HALF])
            + dot(mixed[1], w[HALF:D])
        )
    mid_v = middle[...]
    rms = rms_of(mid_v)
    nf[...] = (mid_v * rms * gf).astype(BF)
    swap_og.wait_recv()
    grad = og[...].reshape(256, D)
    wait_recv(share[0])

    def up_rows(hf):
        return jnp.concatenate([wz[2 * hf + i].reshape(D, HALF) for i in range(2)], axis=1)

    for hf in range(2):
        hp = dot(nf[...], up_rows(hf))
        t = jnp.tanh(GELU_C * (hp + GELU_A * hp * hp * hp))
        hid[hf] = (0.5 * hp * (1.0 + t)).astype(BF)
        act[hf] = 0.5 * (1.0 + t) + 0.5 * hp * (1.0 - t * t) * (
            GELU_C * (1.0 + 3.0 * GELU_A * hp * hp)
        )

    def down_rows(m, b):
        return jnp.concatenate([wz[4 + b, m].reshape(192, HALF), wz[6 + b, m].reshape(192, HALF)], axis=0)

    lots = (
        (dwda, rd.at[0], md.at[0], rd2.at[0], "x"),
        (dwdb, rd.at[1], md.at[1], rd2.at[1], "y"),
        (dws, rl.at[0], ml.at[0], rl2.at[0], "x"),
        (dwo, rl.at[1], ml.at[1], rl2.at[1], "y"),
        (
            dwv.at[:, :, pl.ds(0, 32)], rl.at[2, :, :, pl.ds(0, 32)], ml.at[2, :, pl.ds(0, 32)],
            rl2.at[2, :, pl.ds(0, 32)], "x",
        ),
        (
            dwv.at[:, :, pl.ds(32, 16)], rl.at[2, :, :, pl.ds(32, 16)], ml.at[2, :, pl.ds(32, 16)],
            rl2.at[2, :, pl.ds(32, 16)], "y",
        ),
    )
    def middle_sum(i):
        w1[i].end(lots[i][2])
        start([w2[i]])

    def last_sum(i):
        wait_recv([w2[i]])
        _, _, mid, rcv, first = lots[i]
        return scatter_end(mid, rcv, first)

    def z_at(k):
        return at(lax.rem(z + k, 8), x, y, c)

    def down_part(d):
        return down_sum.at[lax.rem(d, 4)]

    def rest_part(d):
        return rest.at[pl.ds(pl.multiple_of(16 * lax.rem(d, 4), 16), 16)]

    def z_first(part, buf, ks):
        return Batch(pool, [(part(z + k), buf.at[j], z_at(k)) for j, k in enumerate(ks)], buf, buf)

    def z_half(part, buf, res):
        total = part(z)[...].astype(F32)
        for j in range(3):
            total = total + buf[j].astype(F32)
        res[...] = total.astype(BF)

    def z_swap(half, other):
        return remote(half, other, pool.take(), pool.take(), z_at(4))

    def z_last(half, other, full, ks):
        full[q] = (half[...].astype(F32) + other[...].astype(F32)).astype(BF)
        three = full.at[pl.ds(0, 3)]
        return Batch(pool, [(full.at[q], full.at[q], z_at(k)) for k in ks], three, three)

    w1 = [Sum(lot[0], lot[1], lot[4], pool) for lot in lots]
    w2 = [scatter_two(lot[2], lot[3], lot[4], pool) for lot in lots]

    def dw_part(shift, h):
        return dwu.at[lax.rem(z + 8 + shift, 4), pl.ds(2 * h, 2)]

    ways = (up, down)
    far = [remote(dw_part(2 - 4 * h, h), dfar.at[h], pool.take(), pool.take(), ways[h]) for h in range(2)]
    near = [remote(dw_part(2 * h - 1, h), dnear.at[h], pool.take(), pool.take(), ways[1 - h]) for h in range(2)]
    last = [remote(dsum.at[h], dlast.at[h], pool.take(), pool.take(), ways[h]) for h in range(2)]
    wait_recv(share[1])
    s1x.sent()
    s1y.sent()
    wait_send([s2x, s2y] + share[0] + [swap_wo, swap_mix])
    def down_cols(hf):
        pair = [jnp.concatenate([down_rows(2 * hf + i, b) for b in range(2)], axis=1) for i in range(2)]
        return jnp.concatenate(pair, axis=0)

    for hf in range(2):
        pgr[hf] = (act[hf] * dot_nt(grad, down_cols(hf))).astype(BF)
        more = dot_nt(pgr[hf], up_rows(hf)).reshape(2, 2, 64, D)
        fng[...] = more if hf == 0 else fng[...] + more
    swap_fng = to_sib(fng, fng_r)
    swap_fng.start()
    for hf in range(2):
        grad_w = dot(flip(nf[...]), pgr[hf]).astype(BF)
        for i in range(2):
            dwu[2 * hf + i] = grad_w[:, HALF * i : HALF * i + HALF].reshape(4, 4, 48, HALF)
    start(far)
    swap_fng.wait_recv()
    full = (fng[...] + fng_r[...]).reshape(256, D)
    mid_v = middle[...]
    rms = rms_of(mid_v)
    gain_f = jnp.sum(full * mid_v * rms, axis=0, keepdims=True)
    weighted = full * gf
    inner = jnp.mean(weighted * mid_v, axis=-1, keepdims=True)
    mg = grad.astype(F32) + rms * weighted - mid_v * (rms * rms * rms) * inner
    mgrad[...] = mg.reshape(2, 2, 64, D)
    bg = mg.astype(BF)
    bgs[...] = bg
    xg = jnp.zeros((256, HALF), F32)
    for cc in range(2):
        w = wo_all[cc, pl.ds(2 * c, 2)].reshape(HALF, HALF)
        xg = xg + dot_nt(bg[:, HALF * cc : HALF * cc + HALF], w)
    deltas = []
    for b in range(2):
        xgt = flip(xg[128 * b : 128 * b + 128])
        for h in range(HH):
            rows = xgt[64 * h : 64 * h + 64]
            r = rr[b, h : h + 1]
            deltas.append(jnp.sum(rows * mt[b, 64 * h : 64 * h + 64], axis=0, keepdims=True) * r)
            own = gx if h < 3 else gy
            base = 128 * (h % 3) + 64 * b
            own[x, y, base : base + 64] = (rows * r).astype(BF)
    for own, first in ((gx, 0), (gy, 3)):
        rows = []
        for h in range(first, first + 3):
            d0, d1 = deltas[h], deltas[HH + h]
            h0 = d0.astype(BF).astype(F32)
            h1 = d1.astype(BF).astype(F32)
            rows = rows + [h0, h1, d0 - h0, d1 - h1]
        own[x, y, 384:400] = jnp.concatenate(rows + [jnp.zeros((4, 128), F32)], axis=0).astype(BF)
    parts_g = [
        (buf.at[:, :, pl.ds(base, size)], first)
        for buf in (gx, gy)
        for base, size, first in ((0, 208, "x"), (208, 192, "y"))
    ]
    a1 = [gather_one(buf, first, pool) for buf, first in parts_g]
    a2 = [Spread(buf, first, pool) for buf, first in parts_g]
    start(a1)
    start(near)
    for hf in range(2):
        grad_w = dot(flip(hid[hf]), grad).astype(BF)
        for i in range(2):
            for a in range(2):
                for k in range(4):
                    base = HALF * i + 192 * a + 48 * k
                    dwda[2 * hf + i, k, 48 * a : 48 * a + 48] = grad_w[base : base + 48, 0:HALF]
                    dwdb[2 * hf + i, k, 48 * a : 48 * a + 48] = grad_w[base : base + 48, HALF:D]
    for i in range(2):
        wait_recv([a1[i]])
        a2[i].start()
    bg_c = bgs[:, pl.ds(pl.multiple_of(HALF * c, 128), HALF)]
    for i in range(2):
        dwo[pl.ds(2 * i, 2)] = dot(flip(mixed[i]), bg_c).astype(BF).reshape(2, 4, 48, HALF)
    for hf in range(2):
        more = dot(hid[hf], down_cols(hf)).reshape(2, 2, 64, D)
        part[...] = more if hf == 0 else part[...] + more
    swap_part = to_sib(part.at[:, 1 - c], part_r)
    swap_part.start()
    for i in range(2):
        a2[i].relay()
    for h in range(2):
        far[h].wait_recv()
        dsum[h] = (dw_part(1 - 2 * h, h)[...].astype(F32) + dfar[h].astype(F32)).astype(BF)
        last[h].start()
    for i in range(2, 4):
        wait_recv([a1[i]])
        a2[i].start()
    swap_fng.wait_send()
    fng[...] = middle[...].reshape(2, 2, 64, D)
    swap_part.wait_recv()
    out_s[...] = (fng[:, c] + (part[:, c] + part_r[...])).astype(BF)
    save(out_s, out)
    wait_send(a1)
    wait_send(far + share[1])
    for i in range(2):
        a2[i].end()

    def table_part(d, hf):
        buf = gx if hf == 0 else gy
        result = []
        for hh in range(3):
            h = 3 * hf + hh
            pair = []
            for i in range(2):
                k = 2 * d + i
                g = buf[k // 4, lax.rem(k, 4), 128 * hh : 128 * hh + 128]
                cols = pl.ds(pl.multiple_of(256 * d + 128 * i, 128), 128)
                extra = buf[k // 4, lax.rem(k, 4), 384:400].astype(F32)[4 * hh : 4 * hh + 4]
                s = dot(vals[h], g)
                s = s - mcol[0] * (extra[0:1] + extra[2:3])
                s = s - mcol[1] * (extra[1:2] + extra[3:4])
                pair.append(s * e[h, :, :, cols].reshape(128, 128).astype(F32))
            result.append(jnp.concatenate(pair, axis=1))
        return result

    def ring(send, recv, count, hf, device):
        sent = pool.take()
        return [
            remote(send.at[hf, t], recv.at[hf, t], sent, pool.take(), device) for t in range(count)
        ], Bytes(send.at[hf, pl.ds(0, count)], sent)

    ups, up_sent = zip(*[ring(up_s, up_r, 4 - hf, hf, up) for hf in range(2)])
    dns, dn_sent = zip(*[ring(dn_s, dn_r, 3 + hf, hf, down) for hf in range(2)])

    def step(t, hf):
        for copies, send, recv, d in (
            (ups[hf], up_s, up_r, lax.rem(z + 12 - hf - t, 8)),
            (dns[hf], dn_s, dn_r, lax.rem(z + 5 - hf + t, 8)),
        ):
            if t >= len(copies):
                continue
            parts = table_part(d, hf)
            if t > 0:
                copies[t - 1].wait_recv()
            for hh in range(3):
                p = parts[hh]
                if t > 0:
                    p = p + recv[hf, t - 1, hh].astype(F32)
                send[hf, t, hh] = p.astype(BF)
            copies[t].start()

    def value_part(hf):
        buf = (gx, gy)[hf]
        for hh in range(3):
            total = jnp.zeros((128, 128), F32)
            for k in range(16):
                cols = slice(128 * k, 128 * k + 128)
                total = total + dot_nt(
                    buf[k // 4, k % 4, 128 * hh : 128 * hh + 128], e[3 * hf + hh, :, :, cols].reshape(128, 128)
                )
            rows = slice(64 * (3 * hf + hh), 64 * (3 * hf + hh) + 64)
            for b in range(2):
                vgt[b, rows] = total[64 * b : 64 * b + 64] * masks[b]

    step(0, 0)
    for i in range(2, 4):
        a2[i].relay()
    w1[0].start()
    w1[1].start()
    value_part(0)
    for h in range(2):
        near[h].wait_recv()
        last[h].wait_recv()
        total = dw_part(0, h)[...].astype(F32) + dnear[h].astype(F32) + dlast[h].astype(F32)
        dws[pl.ds(2 * h, 2)] = total.astype(BF)
    w1[2].start()
    w1[3].start()
    step(1, 0)
    for i in range(2, 4):
        a2[i].end()
    w1[0].relay()
    w1[1].relay()
    step(0, 1)
    value_part(1)
    vg = jnp.concatenate([flip(vgt[b]) for b in range(2)], axis=0).astype(BF)
    dwv[...] = dot(flip(normed[...]), vg).astype(BF).reshape(4, 4, 48, HALF)
    w1[4].start()
    w1[5].start()
    swap_part.wait_send()
    part[...] = dot_nt(vg, wv[...].reshape(D, HALF)).reshape(2, 2, 64, D)
    swap_ng = to_sib(part, ng_r)
    swap_ng.start()
    xv = tok[...].reshape(256, D).astype(F32)
    rms = rms_of(xv)
    gain_m = jnp.sum(part[...].reshape(256, D) * xv * rms, axis=0, keepdims=True)

    def packed(gains):
        high = gains.astype(BF).astype(F32)
        rows = [high, gains - high]
        rows = [r[:, HALF * i : HALF * i + HALF] for i in range(2) for r in rows]
        return jnp.concatenate(rows + [jnp.zeros((8, HALF), F32)], axis=0).astype(BF)

    def unpacked(rows):
        return jnp.concatenate([rows[0:2] + rows[2:4], rows[4:6] + rows[6:8]], axis=1)

    gs[...] = packed(jnp.concatenate([gain_m, 0.5 * gain_f], axis=0))
    gr[x, y] = gs[...]
    gain1 = gather_one(gr, "x", pool)
    gain2 = gather_two(gr, "x", pool)
    start([gain1])
    for pattern in a2:
        pattern.sent()
    step(2, 0)
    w1[2].relay()
    w1[3].relay()
    w1[4].relay()
    w1[5].relay()
    wait_recv([gain1])
    start([gain2])
    step(1, 1)
    for i in (0, 1, 3, 4, 5, 2):
        middle_sum(i)
    step(3, 0)
    swap_ng.wait_recv()
    full = (part[...] + ng_r[...]).reshape(256, D)
    weighted = full * gm
    inner = jnp.mean(weighted * xv, axis=-1, keepdims=True)
    fng[...] = (rms * weighted - xv * (rms * rms * rms) * inner).reshape(2, 2, 64, D)
    ig_s[...] = mgrad[:, c] + fng[:, c]
    save(ig_s, input_grad)
    for i in range(2):
        total = last_sum(i).astype(BF)
        for a in range(2):
            down_sum[2 * a + i, 0:48] = total[48 * a : 48 * a + 48]
    total = last_sum(3).astype(BF)
    for r in range(3):
        down_sum[r, 48:64] = total[16 * r : 16 * r + 16]
    down_sum[3, 48:64] = jnp.zeros((16, HALF), BF)
    z_down1 = z_first(down_part, zr_down, (1, 2, 7))
    start([z_down1])
    rest[0:32] = last_sum(4).astype(BF)
    rest[32:48] = last_sum(5).astype(BF)
    wait_recv([gain2])
    rest[48:64] = packed(unpacked(jnp.sum(gr[...].reshape(16, 16, HALF).astype(F32), axis=0)))
    z_rest1 = z_first(rest_part, zr_rest, (7, 6, 1))
    start([z_rest1])
    half_up[...] = last_sum(2).astype(BF)
    z_up2 = z_swap(half_up, other_up)
    z_up2.start()
    step(2, 1)
    for pattern in w1[:3]:
        pattern.sent()
    wait_send(near + last)
    wait_recv([z_down1])
    z_half(down_part, zr_down, half_down)
    z_down2 = z_swap(half_down, other_down)
    z_down2.start()
    wait_recv([z_rest1])
    z_half(rest_part, zr_rest, half_rest)
    z_rest2 = z_swap(half_rest, other_rest)
    z_rest2.start()
    step(3, 1)

    def rows_of(src, base, cc):
        return src[0, pl.ds(pl.multiple_of(base + 24 * cc, 8), 24)]

    def finish_ring(hf):
        own = table_part(z, hf)
        ups[hf][-1].wait_recv()
        dns[hf][-1].wait_recv()
        for hh in range(3):
            h = 3 * hf + hh
            p = own[hh] + (up_r[hf, 3 - hf, hh].astype(F32) + dn_r[hf, 2 + hf, hh].astype(F32))
            act[1, 0:128, 0:256] = p
            tgo[h] = act[1, pl.ds(pl.multiple_of(64 * c, 64), 64), 0:256]
            tgs[h] = act[1, pl.ds(pl.multiple_of(64 * (1 - c), 64), 64), 0:256]
        swap_tg[hf].start()
        save(tgo.at[pl.ds(3 * hf, 3)], tg.at[c, pl.ds(3 * hf, 3)])

    swap_tg = [
        to_sib(tgs.at[pl.ds(3 * hf, 3)], tg_r.at[pl.ds(3 * hf, 3)]) for hf in range(2)
    ]
    z_up2.wait_recv()
    z_up3 = z_last(half_up, other_up, zs_up, (1, 7, 2))
    start([z_up3])
    z_down2.wait_recv()
    z_down3 = z_last(half_down, other_down, zs_down, (1, 7, 6))
    start([z_down3])
    z_rest2.wait_recv()
    z_rest3 = z_last(half_rest, other_rest, zs_rest, (1, 7, 6))
    start([z_rest3])
    finish_ring(0)
    finish_ring(1)
    wait_recv([z_up3])
    for m in range(4):
        act[0, 48 * (m // 2) : 48 * (m // 2) + 48, HALF * (m % 2) : HALF * (m % 2) + HALF] = zs_up[m].astype(F32)
    for cc, ref in ((c, post_up.at[0]), (1 - c, post_up.at[1])):
        ref[:, 0:D] = rows_of(act, 0, cc)
        ref[:, D : 2 * D] = rows_of(act, 48, cc)
    swap_up = to_sib(post_up.at[1], post_up.at[2])
    swap_up.start()
    for pattern in w1[3:]:
        pattern.sent()
    wait_send(w2 + [z_down1, z_rest1, gain1, gain2])
    first_core = (c == 0).astype(F32)

    def by_core(ref):
        own, got = ref[0], ref[2]
        return own * first_core + got * (1.0 - first_core), got * first_core + own * (1.0 - first_core)

    wait_recv([z_rest3])
    for r in range(3):
        act[0, 96 + 16 * r : 112 + 16 * r, HALF:D] = zs_rest[r].astype(F32)
    gains = unpacked(zs_rest[3].astype(F32))
    wait_recv([z_down3])
    for r in range(3):
        act[0, 96 + 16 * r : 112 + 16 * r, 0:HALF] = zs_down[r, 48:64].astype(F32)
    for i, cc in enumerate((c, 1 - c)):
        post_rest[i, 0:24] = rows_of(act, 96, cc)
        post_rest[i, 24:32] = jnp.concatenate([gains, jnp.zeros((6, D), F32)], axis=0)
    swap_rest = to_sib(post_rest.at[1], post_rest.at[2])
    swap_rest.start()
    for m in range(4):
        rows, cols = slice(48 * (m // 2), 48 * (m // 2) + 48), slice(HALF * (m % 2), HALF * (m % 2) + HALF)
        down_s[rows, cols] = zs_down[m, 0:48].astype(F32)
    save(down_s, d_down)
    for hf in range(2):
        swap_tg[hf].wait_recv()
        save(tg_r.at[pl.ds(3 * hf, 3)], tg.at[1 - c, pl.ds(3 * hf, 3)])
    swap_up.wait_recv()
    pair = by_core(post_up)
    for m in range(4):
        block = jnp.concatenate([p[:, HALF * m : HALF * m + HALF] for p in pair], axis=1).astype(BF)
        up_s_out[:, D * m : D * m + D] = dot_nt(block, perm[...])
    save(up_s_out, d_up)
    swap_rest.wait_recv()
    gsum_s[...] = post_rest[0, 24:32] + post_rest[2, 24:32]
    save(gsum_s, gsum)
    pair = by_core(post_rest)
    for cc in range(2):
        cols = slice(HALF * cc, HALF * cc + HALF)
        two_s[0, :, cols] = pair[cc][0:24, 0:HALF]
        two_s[1, :, cols] = pair[cc][0:24, HALF:D]
    save(two_s.at[0], d_out)
    save(two_s.at[1], d_value)
    for copy in saved:
        copy.wait()
    wait_send(list(up_sent + dn_sent) + swap_tg + [z_up3, z_down3, z_rest3])
    assert pool.used == SEMS, pool.used
    wait_send([swap_ng, swap_up, swap_rest, z_up2, z_down2, z_rest2])


def finish(out, input_grad, d_value, d_out, d_up, d_down, gsum, tg, *outs):
    for src, dst in zip((out, input_grad, d_value, d_out, d_up, d_down, tg), outs):
        dst[...] = src[...]
    s = lax.axis_index("seq")
    row = lax.broadcasted_iota(jnp.int32, (D, 128), 0)
    lane = lax.broadcasted_iota(jnp.int32, (D, 128), 1)
    pick = jnp.where(row == lane + 24 * s, 1.0, 0.0)
    for i in range(2):
        got = jnp.dot(gsum[...], pick, precision=lax.Precision.HIGHEST, preferred_element_type=F32)
        outs[7 + i][...] = got[i, 0:24]


def vmem(*shape, kind=BF):
    return pltpu.VMEM(shape, kind)


IN_VMEM = pl.BlockSpec(memory_space=pltpu.VMEM)
ANY = pl.BlockSpec(memory_space=pl.ANY)


def per_device(tokens, lengths, w_value, w_out, w_up, w_down, gain_mix, gain_ffn, mix_table, out_grad):
    sd = jax.ShapeDtypeStruct
    shapes = [
        sd((2, 64, D), BF), sd((2, 64, D), F32), sd((24, D), F32), sd((24, D), F32), sd((24, 4 * D), F32),
        sd((96, D), F32), sd((8, D), F32), sd((2, HH, 64, 256), F32),
    ]
    raw = pl.pallas_call(
        layer,
        name="layer",
        out_shape=shapes,
        in_specs=[pl.BlockSpec(memory_space=pltpu.SMEM)] + [IN_VMEM] * 8 + [pl.BlockSpec(memory_space=pl.ANY)],
        out_specs=[ANY] * 8,
        scratch_shapes=[
            vmem(D, D), vmem(2, 24, D, kind=F32), vmem(2, 24, D, kind=F32), vmem(2, 24, D, kind=F32), vmem(2, 24, D, kind=F32),
            vmem(2, 2, 64, D), vmem(2, 2, 64, D), vmem(HH, 2, 64, 2048),
            vmem(4, 4, 48, HALF), vmem(2, 4, 4, 48, HALF), vmem(8, 4, 4, 48, HALF),
            vmem(4, 4, ROWS, 128), vmem(4, 4, ROWS, 128), vmem(3, 4, ROWS, 128), vmem(3, 4, ROWS, 128),
            vmem(4, ROWS, 128), vmem(4, ROWS, 128), vmem(3, ROWS, 128), vmem(3, ROWS, 128),
            vmem(2, HALF, 128, kind=F32), vmem(2, 8, 128, kind=F32), vmem(2, 2, 128, HALF), vmem(HH, 144, 128),
            vmem(HH, 128, 128), vmem(2, 128, 128, kind=F32), vmem(256, D), vmem(256, D, kind=F32), vmem(256, D),
            vmem(256, D), vmem(2, 256, D), vmem(2, 256, D), vmem(2, 256, D, kind=F32),
            vmem(2, 2, 64, D, kind=F32), vmem(2, 64, D, kind=F32), vmem(2, 2, 64, D, kind=F32),
            vmem(2, 2, 64, D, kind=F32), vmem(2, 2, 64, D, kind=F32),
            vmem(4, 4, 4, 48, HALF), vmem(4, 4, 96, HALF), vmem(4, 4, 96, HALF), vmem(4, 4, 48, HALF), vmem(4, 4, 48, HALF),
            vmem(4, 4, 48, HALF), vmem(4, 4, ROWS, 128), vmem(4, 4, ROWS, 128),
            vmem(2, 3, 4, 96, HALF), vmem(3, 3, 4, 48, HALF), vmem(2, 4, 96, HALF), vmem(3, 4, 48, HALF),
            vmem(2, 3, 96, HALF), vmem(3, 3, 48, HALF),
            vmem(2, 2, 4, 48, HALF), vmem(2, 2, 4, 48, HALF), vmem(2, 2, 4, 48, HALF), vmem(2, 2, 4, 48, HALF),
            vmem(16, HALF), vmem(4, 4, 16, HALF),
            vmem(2, 4, 3, 128, 256), vmem(2, 4, 3, 128, 256), vmem(2, 4, 3, 128, 256), vmem(2, 4, 3, 128, 256),
            vmem(HH, 64, 256, kind=F32), vmem(HH, 64, 256, kind=F32), vmem(2, HALF, 128, kind=F32),
            vmem(2, 2, 64, D, kind=F32), vmem(4, 64, HALF), vmem(64, HALF), vmem(3, 64, HALF), vmem(3, 16, HALF),
            vmem(48, HALF), vmem(64, HALF), vmem(16, HALF), vmem(48, HALF), vmem(64, HALF), vmem(16, HALF),
            vmem(4, 48, HALF), vmem(4, 64, HALF), vmem(4, 16, HALF),
            vmem(3, 24, 2 * D, kind=F32), vmem(3, 32, D, kind=F32), vmem(2, 64, D), vmem(2, 64, D, kind=F32),
            vmem(96, D, kind=F32), vmem(24, 4 * D, kind=F32), vmem(HH, 64, 256, kind=F32),
            vmem(8, D, kind=F32), vmem(2, 24, D, kind=F32),
            pltpu.SemaphoreType.DMA((SEMS,)),
        ],
        compiler_params=pltpu.CompilerParams(
            collective_id=0, has_side_effects=True, vmem_limit_bytes=63 << 20
        ),
    )(lengths, tokens, out_grad, w_value, w_out, w_up, w_down, gain_mix, gain_ffn, mix_table)
    out, input_grad, d_value, d_out, d_up, d_down, tg, mix_gain, ffn_gain = pl.pallas_call(
        finish,
        name="finish",
        out_shape=shapes[:6] + [shapes[7], sd((24,), F32), sd((24,), F32)],
        in_specs=[IN_VMEM] * 8,
        out_specs=[IN_VMEM] * 9,
    )(*raw)
    return (
        out, input_grad, d_value, d_out, d_up, d_down, mix_gain, ffn_gain, tg.reshape(HEADS, 64, 256),
    )


def solution(mesh):
    return jax.shard_map(
        per_device,
        mesh=mesh,
        in_specs=(
            P("dp", "seq", None),
            P("dp"),
            P("seq", None),
            P("seq", None),
            P("seq", None),
            P("seq", None),
            P(),
            P(),
            P(None, "seq", None),
            P("dp", "seq", None),
        ),
        out_specs=(
            P("dp", "seq", None),
            P("dp", "seq", None),
            P("seq", None),
            P("seq", None),
            P("seq", None),
            P("seq", None),
            P("seq"),
            P("seq"),
            P(None, "seq", "dp"),
        ),
        check_vma=False,
    )
```

```python
import jax
import jax.numpy as jnp
from jax import lax
from jax.experimental import pallas as pl
from jax.experimental.pallas import tpu as pltpu
from jax.sharding import PartitionSpec as P

D = 768
HALF = 384
HEADS = 12
HH = 6
EPS = 1e-06
MESH = pl.DeviceIdType.MESH
BF = jnp.bfloat16
F32 = jnp.float32
OFFS = (1, 3, 2)
ROWS = 400
SEMS = 206
GELU_C = 0.7978845608028654
GELU_A = 0.044715


def here():
    s = lax.axis_index("seq")
    return lax.axis_index("dp"), s // 8, (s // 2) % 4, s % 2


def at(z, x, y, c):
    return (z, (x * 4 + y) * 2 + c)


class Pool:
    def __init__(self, ref):
        self.ref, self.used = ref, 0

    def take(self):
        self.used += 1
        return self.ref.at[self.used - 1]


def remote(src, dst, send, recv, device):
    return pltpu.make_async_remote_copy(
        src_ref=src, dst_ref=dst, send_sem=send, recv_sem=recv, device_id=device, device_id_type=MESH
    )


class Batch:
    def __init__(self, pool, pieces, sent, got):
        self.send, self.recv = pool.take(), pool.take()
        self.all_sent, self.all_got = sent, got
        self.copies = [remote(src, dst, self.send, self.recv, device) for src, dst, device in pieces]

    def start(self):
        start(self.copies)

    def wait_recv(self):
        pltpu.make_async_copy(self.all_got, self.all_got, self.recv).wait()

    def wait_send(self):
        pltpu.make_async_copy(self.all_sent, self.all_sent, self.send).wait()


def along(first, k):
    z, x, y, c = here()
    if first == "x":
        return at(z, lax.rem(x + k, 4), y, c)
    return at(z, x, lax.rem(y + k, 4), c)


OTHER = {"x": "y", "y": "x"}


def own_at(first):
    _, x, y, _ = here()
    return x if first == "x" else y


def gather_one(buf, first, pool):
    _, x, y, _ = here()
    three = buf.at[0, pl.ds(0, 3)]
    return Batch(pool, [(buf.at[x, y], buf.at[x, y], along(first, k)) for k in OFFS], three, three)


def gather_two(buf, first, pool):
    _, x, y, _ = here()
    view = buf.at[:, y] if first == "x" else buf.at[x]
    three = buf.at[pl.ds(0, 3)]
    return Batch(pool, [(view, view, along(OTHER[first], k)) for k in OFFS], three, three)


class Bytes:
    def __init__(self, view, sem):
        self.view, self.sem = view, sem

    def wait_recv(self):
        pltpu.make_async_copy(self.view, self.view, self.sem).wait()

    wait_send = wait_recv


class Spread:
    def __init__(self, buf, first, pool):
        second = OTHER[first]
        mine = own_at(second)

        def part(k, half):
            place = lax.rem(mine + k, 4)
            pair = pl.ds(2 * half, 2)
            return buf.at[pair, place] if second == "y" else buf.at[place, pair]

        self.buf, self.send, self.recv = buf, pool.take(), pool.take()

        def send(k, half, way, recv):
            return remote(part(k, half), part(k, half), self.send, recv, along(second, way))

        self.early = [send(0, 0, 1, pool.take()), send(0, 1, 3, pool.take())]
        self.late = [send(0, 1, 1, self.recv), send(0, 0, 3, self.recv)]
        self.on = [send(3, 0, 1, self.recv), send(1, 1, 3, self.recv)]

    def start(self):
        start(self.early + self.late)

    def relay(self):
        for got, copy in zip(self.early, self.on):
            wait_recv([got])
            copy.start()

    def end(self):
        view = self.buf.at[pl.ds(0, 2)]
        wait_recv([Bytes(view, self.recv)])

    def sent(self):
        wait_send([Bytes(self.buf.at[pl.ds(0, 3)], self.send)])


class Sum:
    def __init__(self, src, rcv, first, pool):
        self.src, self.rcv, self.first = src, rcv, first
        self.send, self.recv = pool.take(), pool.take()
        self.mine = own_at(first)

        def send(k, half, slot, way, recv):
            return remote(
                self.part(k, half), rcv.at[slot, pl.ds(2 * half, 2)], self.send, recv, along(first, way)
            )

        self.far = [send(2, 0, 2, 1, pool.take()), send(2, 1, 2, 3, pool.take())]
        self.near = [send(1, 1, 0, 1, self.recv), send(3, 0, 1, 3, self.recv)]
        self.on = [send(1, 0, 0, 1, self.recv), send(3, 1, 1, 3, self.recv)]

    def part(self, k, half):
        place = lax.rem(self.mine + k, 4)
        pair = pl.ds(2 * half, 2)
        return self.src.at[place, pair] if self.first == "x" else self.src.at[pair, place]

    def start(self):
        start(self.far + self.near)

    def relay(self):
        for half in range(2):
            wait_recv([self.far[half]])
            part = self.part(1 + 2 * half, half)
            got = self.rcv[2, 2 * half : 2 * half + 2]
            part[...] = (part[...].astype(F32) + got.astype(F32)).astype(BF)
            self.on[half].start()

    def end(self, mid):
        wait_recv([Bytes(self.rcv.at[pl.ds(0, 2)], self.recv)])
        for j in range(4):
            own = self.src[self.mine, j] if self.first == "x" else self.src[j, self.mine]
            total = own.astype(F32) + self.rcv[0, j].astype(F32) + self.rcv[1, j].astype(F32)
            mid[j] = total.astype(BF)

    def sent(self):
        wait_send([Bytes(self.src.at[pl.ds(0, 3)], self.send)])


def scatter_two(mid, rcv, first, pool):
    second = OTHER[first]
    mine = own_at(second)
    pieces = [(mid.at[lax.rem(mine + k, 4)], rcv.at[i], along(second, k)) for i, k in enumerate(OFFS)]
    return Batch(pool, pieces, mid.at[pl.ds(0, 3)], rcv)


def scatter_end(mid, rcv, first):
    total = mid[own_at(OTHER[first])].astype(F32)
    for i in range(3):
        total = total + rcv[i].astype(F32)
    return total


def start(copies):
    for copy in copies:
        copy.start()


def wait_recv(copies):
    for copy in copies:
        copy.wait_recv()


def wait_send(copies):
    for copy in copies:
        copy.wait_send()


def signal(device):
    pl.semaphore_signal(
        pltpu.get_barrier_semaphore(), inc=1, device_id=device, device_id_type=MESH
    )


def greet():
    z, x, y, c = here()
    count = 0
    for k in range(1, 4):
        signal(at(z, lax.rem(x + k, 4), y, c))
        signal(at(z, x, lax.rem(y + k, 4), c))
        count += 2
    signal(at(z, x, y, 1 - c))
    count += 1
    for k in range(1, 8):
        signal(at(lax.rem(z + k, 8), x, y, c))
        count += 1
    return count


def meet(count):
    pl.semaphore_wait(pltpu.get_barrier_semaphore(), count)


def dot(a, b):
    return jnp.dot(a, b, preferred_element_type=F32)


def dot_nt(a, b):
    return lax.dot_general(a, b, (((1,), (1,)), ((), ())), preferred_element_type=F32)


def flip(a):
    return jnp.transpose(a)


def rms_of(v):
    return lax.rsqrt(jnp.mean(v * v, axis=-1, keepdims=True) + EPS)


def layer(
    lengths, tokens, out_grad, w_value, w_out, w_up, w_down, gain_mix, gain_ffn, table,
    out, input_grad, d_value, d_out, d_up, d_down, gsum, tg,
    perm, pre_a, pre_b, got_a, got_b, tok, og, e, wv, wo_all, wz,
    ux, uy, rx, ry, mx, my, rx2, ry2, mt, rr, mix, vt, vals, mcol, normed, middle, nf, bgs, hid, pgr, act,
    part, part_r, fng, fng_b, fng_r, mgrad, dwu, dwda, dwdb, dws, dwo, dwv, gx, gy,
    rd, rl, md, ml, rd2, rl2, dfar, dnear, dlast, dsum, gs, gr, up_s, up_r, dn_s, dn_r, tgs, tg_r, vgt, ng_r,
    down_sum, rest, zr_down, zr_rest, half_up, half_down, half_rest, other_up, other_down, other_rest,
    zs_up, zs_down, zs_rest, post_up, post_rest,
    out_s, ig_s, down_s, up_s_out, tgo, gsum_s, two_s,
    sems,
):
    z, x, y, c = here()
    sib = at(z, x, y, 1 - c)
    up = at(lax.rem(z + 1, 8), x, y, c)
    down = at(lax.rem(z + 7, 8), x, y, c)
    wo = wo_all.at[c]
    pool = Pool(sems)

    def to_sib(src, dst):
        return remote(src, dst, pool.take(), pool.take(), sib)

    saved = []

    def save(src, dst):
        copy = pltpu.make_async_copy(src, dst, pool.take())
        copy.start()
        saved.append(copy)

    count = greet()
    own_tab = pltpu.make_async_copy(table.at[pl.ds(6 * c, 6)], e.at[:, c], pool.take())
    own_tab.start()
    q = lax.rem(z, 4)
    par = lax.rem(z, 2)
    for cc in range(2):
        cols = slice(HALF * cc, HALF * cc + HALF)
        pre_a[cc, :, 0:HALF] = w_out[:, cols].astype(F32)
        pre_a[cc, :, HALF:D] = w_value[:, cols].astype(F32)
    meet(count)
    swap_a = to_sib(pre_a.at[1 - c], got_a.at[c])
    swap_a.start()
    got_a[c] = pre_a[c]
    col = lax.broadcasted_iota(jnp.int32, (1, D), 1)
    odd = jnp.where(col >= HALF, 1, 0)
    low = col - HALF * odd
    half = jnp.where(low >= 192, 1, 0)
    low = low - 192 * half
    quad = jnp.where(low >= 48, 1, 0) + jnp.where(low >= 96, 1, 0) + jnp.where(low >= 144, 1, 0)
    origin = low + 144 * quad + 96 * odd + 48 * half
    perm[...] = jnp.where(lax.broadcasted_iota(jnp.int32, (D, D), 0) == origin, 1.0, 0.0).astype(BF)
    for i in range(2):
        mine = dot(w_up[:, pl.ds(pl.multiple_of(D * (2 * par + i), D), D)], perm[...])
        for cc in range(2):
            pre_b[cc, :, HALF * i : HALF * i + HALF] = mine[:, HALF * cc : HALF * cc + HALF]
    swap_b = to_sib(pre_b.at[1 - c], got_b.at[c])
    swap_b.start()
    got_b[c] = pre_b[c]
    bufs = (
        (wv, "x"), (wo, "y"), (wz.at[2 * par], "x"), (wz.at[2 * par + 1], "y"),
        (wz.at[4 + 2 * par], "x"), (wz.at[5 + 2 * par], "y"),
    )
    g1 = [gather_one(buf, first, pool) for buf, first in bufs]
    g2 = [Spread(buf, first, pool) for buf, first in bufs]
    swap_a.wait_recv()
    shard = got_a[...].reshape(48, D).astype(BF)
    wo[x, y] = shard[:, 0:HALF]
    wv[x, y] = shard[:, HALF:D]
    start(g1[0:2])
    swap_tok = to_sib(tokens, tok.at[:, c])
    swap_tab = to_sib(table.at[pl.ds(6 * (1 - c), 6)], e.at[:, c])
    swap_og = to_sib(out_grad, og.at[:, c])
    start([swap_tok, swap_tab, swap_og])
    tok[:, c] = tokens[...]
    og[:, c] = out_grad[...]
    for b in range(2):
        rows = pl.ds(pl.multiple_of(48 * par, 16), 48)
        wz[4 + 2 * par + b, x, y] = w_down[rows, HALF * b : HALF * b + HALF]
    swap_b.wait_recv()
    shard = got_b[...].reshape(48, D).astype(BF)
    for i in range(2):
        wz[2 * par + i, x, y] = shard[:, HALF * i : HALF * i + HALF]
    start(g1[2:4])
    share = [
        [
            remote(
                wz.at[4 * i + 2 * par + way], wz.at[4 * i + 2 * par + way], pool.take(), pool.take(), (up, down)[way]
            )
            for way in range(2)
        ]
        for i in range(2)
    ]
    for i in range(4):
        wait_recv([g1[i]])
        g2[i].start()
    start(g1[4:6])
    swap_tok.wait_recv()
    values = tok[...].reshape(256, D).astype(F32)
    gm = gain_mix[...].reshape(1, D)
    gf = gain_ffn[...].reshape(1, D)
    normed[...] = (values * rms_of(values) * gm).astype(BF)
    place = (4 * x + y) * 128
    lane = lax.broadcasted_iota(jnp.int32, (1, 128), 1) + place
    row = lax.broadcasted_iota(jnp.int32, (128, 128), 0) + place
    masks = [jnp.where(lane < lengths[b], 1.0, 0.0) for b in range(2)]
    for b in range(2):
        mcol[b] = jnp.where(row < lengths[b], 1.0, 0.0)
    swap_tab.wait_recv()
    own_tab.wait()

    def exps(h, carry):
        e[h] = jnp.exp(e[h].astype(F32)).astype(BF)
        return carry

    lax.fori_loop(0, HH, exps, 0)
    for i in range(4):
        g2[i].relay()
    for i in (4, 5):
        wait_recv([g1[i]])
        g2[i].start()
    g2[0].end()
    v = dot(normed[...], wv[...].reshape(D, HALF)).astype(BF).astype(F32)
    vall = flip(v) * jnp.concatenate(masks, axis=1)
    for h in range(HH):
        block = jnp.concatenate(
            [vall[64 * h : 64 * h + 64, 0:128], vall[64 * h : 64 * h + 64, 128:256]], axis=0
        )
        place = [jnp.zeros((2, 128), F32)] * (h % 3) + masks
        place = place + [jnp.zeros((14 - 2 * (h % 3), 128), F32)]
        vt[h] = jnp.concatenate([block] + place, axis=0).astype(BF)
        vals[h] = flip(block).astype(BF)

    s1x = Sum(ux, rx, "x", pool)
    s1y = Sum(uy, ry, "y", pool)
    for k in (2, 1, 3, 0):
        xx = lax.rem(x + k, 4)
        yy = lax.rem(y + k, 4)

        cols = pl.ds(pl.multiple_of(512 * xx, 512), 512)
        extra = jnp.zeros((16, 512), F32)
        for h in range(3):
            u = dot(vt[h], e[h, :, :, cols].reshape(128, 512))
            extra = extra + u[128:144]
            for j in range(4):
                ux[xx, j, 128 * h : 128 * h + 128] = u[0:128, 128 * j : 128 * j + 128].astype(BF)
        for j in range(4):
            ux[xx, j, 384:400] = extra[:, 128 * j : 128 * j + 128].astype(BF)
        if k == 2:
            start(s1x.far)
        elif k > 0:
            s1x.near[k // 2].start()
        for j in range(4):
            cols = pl.ds(pl.multiple_of(512 * j + 128 * yy, 128), 128)
            extra = jnp.zeros((16, 128), F32)
            for h in range(3):
                u = dot(vt[h + 3], e[h + 3, :, :, cols].reshape(128, 128))
                extra = extra + u[128:144]
                uy[j, yy, 128 * h : 128 * h + 128] = u[0:128].astype(BF)
            uy[j, yy, 384:400] = extra.astype(BF)
        if k == 2:
            start(s1y.far)
        elif k > 0:
            s1y.near[k // 2].start()
    for way in range(2):
        g2[2 + way].end()
        share[0][way].start()
    g2[1].end()
    swap_wo = to_sib(wo, wo)
    swap_wo.start()
    g2[4].relay()
    g2[5].relay()
    s1x.relay()
    s1y.relay()
    for way in range(2):
        g2[4 + way].end()
        share[1][way].start()
    s2x = scatter_two(mx, rx2, "x", pool)
    s2y = scatter_two(my, ry2, "y", pool)
    for pattern in g2:
        pattern.sent()
    wait_send(g1)
    wait_send([swap_a, swap_b, swap_tok, swap_tab, swap_og])
    s1x.end(mx)
    start([s2x])
    s1y.end(my)
    start([s2y])
    for half, (copies, mid, rcv, first) in enumerate(((s2x, mx, rx2, "x"), (s2y, my, ry2, "y"))):
        wait_recv([copies])
        total = scatter_end(mid, rcv, first)
        for hh in range(3):
            h = half * 3 + hh
            for b in range(2):
                r = masks[b] / total[384 + 2 * hh + b : 385 + 2 * hh + b]
                rr[b, h : h + 1] = r
                mt[b, 64 * h : 64 * h + 64] = total[128 * hh + 64 * b : 128 * hh + 64 * b + 64] * r
    for b in range(2):
        mix[c, b] = flip(mt[b]).astype(BF)
    swap_mix = to_sib(mix.at[c], mix.at[c])
    swap_mix.start()
    swap_wo.wait_recv()
    swap_mix.wait_recv()
    mixed = [mix[i].reshape(256, HALF) for i in range(2)]
    for cc in range(2):
        w = wo_all[cc].reshape(D, HALF)
        cols = slice(HALF * cc, HALF * cc + HALF)
        middle[:, cols] = (
            tok[...].reshape(256, D)[:, cols].astype(F32)
            + dot(mixed[0], w[0:HALF])
            + dot(mixed[1], w[HALF:D])
        )
    mid_v = middle[...]
    rms = rms_of(mid_v)
    nf[...] = (mid_v * rms * gf).astype(BF)
    swap_og.wait_recv()
    grad = og[...].reshape(256, D)
    wait_recv(share[0])

    def up_rows(hf):
        return jnp.concatenate([wz[2 * hf + i].reshape(D, HALF) for i in range(2)], axis=1)

    for hf in range(2):
        hp = dot(nf[...], up_rows(hf))
        t = jnp.tanh(GELU_C * (hp + GELU_A * hp * hp * hp))
        hid[hf] = (0.5 * hp * (1.0 + t)).astype(BF)
        act[hf] = 0.5 * (1.0 + t) + 0.5 * hp * (1.0 - t * t) * (
            GELU_C * (1.0 + 3.0 * GELU_A * hp * hp)
        )

    def down_rows(m, b):
        return jnp.concatenate([wz[4 + b, m].reshape(192, HALF), wz[6 + b, m].reshape(192, HALF)], axis=0)

    lots = (
        (dwda, rd.at[0], md.at[0], rd2.at[0], "x"),
        (dwdb, rd.at[1], md.at[1], rd2.at[1], "y"),
        (dws, rl.at[0], ml.at[0], rl2.at[0], "x"),
        (dwo, rl.at[1], ml.at[1], rl2.at[1], "y"),
        (
            dwv.at[:, :, pl.ds(0, 32)], rl.at[2, :, :, pl.ds(0, 32)], ml.at[2, :, pl.ds(0, 32)],
            rl2.at[2, :, pl.ds(0, 32)], "x",
        ),
        (
            dwv.at[:, :, pl.ds(32, 16)], rl.at[2, :, :, pl.ds(32, 16)], ml.at[2, :, pl.ds(32, 16)],
            rl2.at[2, :, pl.ds(32, 16)], "y",
        ),
    )
    def middle_sum(i):
        w1[i].end(lots[i][2])
        start([w2[i]])

    def last_sum(i):
        wait_recv([w2[i]])
        _, _, mid, rcv, first = lots[i]
        return scatter_end(mid, rcv, first)

    def z_at(k):
        return at(lax.rem(z + k, 8), x, y, c)

    def down_part(d):
        return down_sum.at[lax.rem(d, 4)]

    def rest_part(d):
        return rest.at[pl.ds(pl.multiple_of(16 * lax.rem(d, 4), 16), 16)]

    def z_first(part, buf, ks):
        return Batch(pool, [(part(z + k), buf.at[j], z_at(k)) for j, k in enumerate(ks)], buf, buf)

    def z_half(part, buf, res):
        total = part(z)[...].astype(F32)
        for j in range(3):
            total = total + buf[j].astype(F32)
        res[...] = total.astype(BF)

    def z_swap(half, other):
        return remote(half, other, pool.take(), pool.take(), z_at(4))

    def z_last(half, other, full, ks):
        full[q] = (half[...].astype(F32) + other[...].astype(F32)).astype(BF)
        three = full.at[pl.ds(0, 3)]
        return Batch(pool, [(full.at[q], full.at[q], z_at(k)) for k in ks], three, three)

    w1 = [Sum(lot[0], lot[1], lot[4], pool) for lot in lots]
    w2 = [scatter_two(lot[2], lot[3], lot[4], pool) for lot in lots]

    def dw_part(shift, h):
        return dwu.at[lax.rem(z + 8 + shift, 4), pl.ds(2 * h, 2)]

    ways = (up, down)
    far = [remote(dw_part(2 - 4 * h, h), dfar.at[h], pool.take(), pool.take(), ways[h]) for h in range(2)]
    near = [remote(dw_part(2 * h - 1, h), dnear.at[h], pool.take(), pool.take(), ways[1 - h]) for h in range(2)]
    last = [remote(dsum.at[h], dlast.at[h], pool.take(), pool.take(), ways[h]) for h in range(2)]
    wait_recv(share[1])
    s1x.sent()
    s1y.sent()
    wait_send([s2x, s2y] + share[0] + [swap_wo, swap_mix])
    def down_cols(hf):
        pair = [jnp.concatenate([down_rows(2 * hf + i, b) for b in range(2)], axis=1) for i in range(2)]
        return jnp.concatenate(pair, axis=0)

    for hf in range(2):
        pgr[hf] = (act[hf] * dot_nt(grad, down_cols(hf))).astype(BF)
        more = dot_nt(pgr[hf], up_rows(hf)).reshape(2, 2, 64, D)
        fng[...] = more if hf == 0 else fng[...] + more
    fng_b[...] = fng[...].astype(BF)
    swap_fng = to_sib(fng_b, fng_r)
    swap_fng.start()
    for hf in range(2):
        grad_w = dot(flip(nf[...]), pgr[hf]).astype(BF)
        for i in range(2):
            dwu[2 * hf + i] = grad_w[:, HALF * i : HALF * i + HALF].reshape(4, 4, 48, HALF)
    start(far)
    swap_fng.wait_recv()
    full = (fng_b[...].astype(F32) + fng_r[...].astype(F32)).reshape(256, D)
    mid_v = middle[...]
    rms = rms_of(mid_v)
    gain_f = jnp.sum(full * mid_v * rms, axis=0, keepdims=True)
    weighted = full * gf
    inner = jnp.mean(weighted * mid_v, axis=-1, keepdims=True)
    mg = grad.astype(F32) + rms * weighted - mid_v * (rms * rms * rms) * inner
    mgrad[...] = mg.reshape(2, 2, 64, D)
    bg = mg.astype(BF)
    bgs[...] = bg
    xg = jnp.zeros((256, HALF), F32)
    for cc in range(2):
        w = wo_all[cc, pl.ds(2 * c, 2)].reshape(HALF, HALF)
        xg = xg + dot_nt(bg[:, HALF * cc : HALF * cc + HALF], w)
    deltas = []
    for b in range(2):
        xgt = flip(xg[128 * b : 128 * b + 128])
        for h in range(HH):
            rows = xgt[64 * h : 64 * h + 64]
            r = rr[b, h : h + 1]
            deltas.append(jnp.sum(rows * mt[b, 64 * h : 64 * h + 64], axis=0, keepdims=True) * r)
            own = gx if h < 3 else gy
            base = 128 * (h % 3) + 64 * b
            own[x, y, base : base + 64] = (rows * r).astype(BF)
    for own, first in ((gx, 0), (gy, 3)):
        rows = []
        for h in range(first, first + 3):
            d0, d1 = deltas[h], deltas[HH + h]
            h0 = d0.astype(BF).astype(F32)
            h1 = d1.astype(BF).astype(F32)
            rows = rows + [h0, h1, d0 - h0, d1 - h1]
        own[x, y, 384:400] = jnp.concatenate(rows + [jnp.zeros((4, 128), F32)], axis=0).astype(BF)
    parts_g = [
        (buf.at[:, :, pl.ds(base, size)], first)
        for buf in (gx, gy)
        for base, size, first in ((0, 208, "x"), (208, 192, "y"))
    ]
    a1 = [gather_one(buf, first, pool) for buf, first in parts_g]
    a2 = [Spread(buf, first, pool) for buf, first in parts_g]
    start(a1)
    start(near)
    for hf in range(2):
        grad_w = dot(flip(hid[hf]), grad).astype(BF)
        for i in range(2):
            for a in range(2):
                for k in range(4):
                    base = HALF * i + 192 * a + 48 * k
                    dwda[2 * hf + i, k, 48 * a : 48 * a + 48] = grad_w[base : base + 48, 0:HALF]
                    dwdb[2 * hf + i, k, 48 * a : 48 * a + 48] = grad_w[base : base + 48, HALF:D]
    for i in range(2):
        wait_recv([a1[i]])
        a2[i].start()
    bg_c = bgs[:, pl.ds(pl.multiple_of(HALF * c, 128), HALF)]
    for i in range(2):
        dwo[pl.ds(2 * i, 2)] = dot(flip(mixed[i]), bg_c).astype(BF).reshape(2, 4, 48, HALF)
    for hf in range(2):
        more = dot(hid[hf], down_cols(hf)).reshape(2, 2, 64, D)
        part[...] = more if hf == 0 else part[...] + more
    swap_part = to_sib(part.at[:, 1 - c], part_r)
    swap_part.start()
    for i in range(2):
        a2[i].relay()
    for h in range(2):
        far[h].wait_recv()
        dsum[h] = (dw_part(1 - 2 * h, h)[...].astype(F32) + dfar[h].astype(F32)).astype(BF)
        last[h].start()
    for i in range(2, 4):
        wait_recv([a1[i]])
        a2[i].start()
    swap_fng.wait_send()
    fng[...] = middle[...].reshape(2, 2, 64, D)
    swap_part.wait_recv()
    out_s[...] = (fng[:, c] + (part[:, c] + part_r[...])).astype(BF)
    save(out_s, out)
    wait_send(a1)
    wait_send(far + share[1])
    for i in range(2):
        a2[i].end()

    def table_part(d, hf):
        buf = gx if hf == 0 else gy
        result = []
        for hh in range(3):
            h = 3 * hf + hh
            pair = []
            for i in range(2):
                k = 2 * d + i
                g = buf[k // 4, lax.rem(k, 4), 128 * hh : 128 * hh + 128]
                cols = pl.ds(pl.multiple_of(256 * d + 128 * i, 128), 128)
                extra = buf[k // 4, lax.rem(k, 4), 384:400].astype(F32)[4 * hh : 4 * hh + 4]
                s = dot(vals[h], g)
                s = s - mcol[0] * (extra[0:1] + extra[2:3])
                s = s - mcol[1] * (extra[1:2] + extra[3:4])
                pair.append(s * e[h, :, :, cols].reshape(128, 128).astype(F32))
            result.append(jnp.concatenate(pair, axis=1))
        return result

    def ring(send, recv, count, hf, device):
        sent = pool.take()
        return [
            remote(send.at[hf, t], recv.at[hf, t], sent, pool.take(), device) for t in range(count)
        ], Bytes(send.at[hf, pl.ds(0, count)], sent)

    ups, up_sent = zip(*[ring(up_s, up_r, 4 - hf, hf, up) for hf in range(2)])
    dns, dn_sent = zip(*[ring(dn_s, dn_r, 3 + hf, hf, down) for hf in range(2)])

    def step(t, hf):
        for copies, send, recv, d in (
            (ups[hf], up_s, up_r, lax.rem(z + 12 - hf - t, 8)),
            (dns[hf], dn_s, dn_r, lax.rem(z + 5 - hf + t, 8)),
        ):
            if t >= len(copies):
                continue
            parts = table_part(d, hf)
            if t > 0:
                copies[t - 1].wait_recv()
            for hh in range(3):
                p = parts[hh]
                if t > 0:
                    p = p + recv[hf, t - 1, hh].astype(F32)
                send[hf, t, hh] = p.astype(BF)
            copies[t].start()

    def value_part(hf):
        buf = (gx, gy)[hf]
        for hh in range(3):
            total = jnp.zeros((128, 128), F32)
            rows = slice(128 * hh, 128 * hh + 128)
            for k in range(0, 16, 4):
                g = jnp.concatenate([buf[k // 4, i, rows] for i in range(4)], axis=1)
                cols = slice(128 * k, 128 * k + 512)
                total = total + dot_nt(g, e[3 * hf + hh, :, :, cols].reshape(128, 512))
            rows = slice(64 * (3 * hf + hh), 64 * (3 * hf + hh) + 64)
            for b in range(2):
                vgt[b, rows] = total[64 * b : 64 * b + 64] * masks[b]

    step(0, 0)
    for i in range(2, 4):
        a2[i].relay()
    w1[0].start()
    w1[1].start()
    value_part(0)
    for h in range(2):
        near[h].wait_recv()
        last[h].wait_recv()
        total = dw_part(0, h)[...].astype(F32) + dnear[h].astype(F32) + dlast[h].astype(F32)
        dws[pl.ds(2 * h, 2)] = total.astype(BF)
    w1[2].start()
    w1[3].start()
    step(1, 0)
    for i in range(2, 4):
        a2[i].end()
    w1[0].relay()
    w1[1].relay()
    step(0, 1)
    value_part(1)
    vg = jnp.concatenate([flip(vgt[b]) for b in range(2)], axis=0).astype(BF)
    dwv[...] = dot(flip(normed[...]), vg).astype(BF).reshape(4, 4, 48, HALF)
    w1[4].start()
    w1[5].start()
    swap_part.wait_send()
    part[...] = dot_nt(vg, wv[...].reshape(D, HALF)).reshape(2, 2, 64, D)
    swap_ng = to_sib(part, ng_r)
    swap_ng.start()
    xv = tok[...].reshape(256, D).astype(F32)
    rms = rms_of(xv)
    gain_m = jnp.sum(part[...].reshape(256, D) * xv * rms, axis=0, keepdims=True)

    def packed(gains):
        high = gains.astype(BF).astype(F32)
        rows = [high, gains - high]
        rows = [r[:, HALF * i : HALF * i + HALF] for i in range(2) for r in rows]
        return jnp.concatenate(rows + [jnp.zeros((8, HALF), F32)], axis=0).astype(BF)

    def unpacked(rows):
        return jnp.concatenate([rows[0:2] + rows[2:4], rows[4:6] + rows[6:8]], axis=1)

    gs[...] = packed(jnp.concatenate([gain_m, 0.5 * gain_f], axis=0))
    gr[x, y] = gs[...]
    gain1 = gather_one(gr, "x", pool)
    gain2 = gather_two(gr, "x", pool)
    start([gain1])
    for pattern in a2:
        pattern.sent()
    step(2, 0)
    w1[2].relay()
    w1[3].relay()
    w1[4].relay()
    w1[5].relay()
    wait_recv([gain1])
    start([gain2])
    step(1, 1)
    for i in (0, 1, 3, 4, 5, 2):
        middle_sum(i)
    step(3, 0)
    swap_ng.wait_recv()
    full = (part[...] + ng_r[...]).reshape(256, D)
    weighted = full * gm
    inner = jnp.mean(weighted * xv, axis=-1, keepdims=True)
    fng[...] = (rms * weighted - xv * (rms * rms * rms) * inner).reshape(2, 2, 64, D)
    ig_s[...] = mgrad[:, c] + fng[:, c]
    save(ig_s, input_grad)
    for i in range(2):
        total = last_sum(i).astype(BF)
        for a in range(2):
            down_sum[2 * a + i, 0:48] = total[48 * a : 48 * a + 48]
    total = last_sum(3).astype(BF)
    for r in range(3):
        down_sum[r, 48:64] = total[16 * r : 16 * r + 16]
    down_sum[3, 48:64] = jnp.zeros((16, HALF), BF)
    z_down1 = z_first(down_part, zr_down, (1, 2, 7))
    start([z_down1])
    rest[0:32] = last_sum(4).astype(BF)
    rest[32:48] = last_sum(5).astype(BF)
    wait_recv([gain2])
    rest[48:64] = packed(unpacked(jnp.sum(gr[...].reshape(16, 16, HALF).astype(F32), axis=0)))
    z_rest1 = z_first(rest_part, zr_rest, (7, 6, 1))
    start([z_rest1])
    half_up[...] = last_sum(2).astype(BF)
    z_up2 = z_swap(half_up, other_up)
    z_up2.start()
    step(2, 1)
    for pattern in w1[:3]:
        pattern.sent()
    wait_send(near + last)
    wait_recv([z_down1])
    z_half(down_part, zr_down, half_down)
    z_down2 = z_swap(half_down, other_down)
    z_down2.start()
    wait_recv([z_rest1])
    z_half(rest_part, zr_rest, half_rest)
    z_rest2 = z_swap(half_rest, other_rest)
    z_rest2.start()
    step(3, 1)

    def rows_of(src, base, cc):
        return src[0, pl.ds(pl.multiple_of(base + 24 * cc, 8), 24)]

    def finish_ring(hf):
        own = table_part(z, hf)
        ups[hf][-1].wait_recv()
        dns[hf][-1].wait_recv()
        for hh in range(3):
            h = 3 * hf + hh
            p = own[hh] + (up_r[hf, 3 - hf, hh].astype(F32) + dn_r[hf, 2 + hf, hh].astype(F32))
            act[1, 0:128, 0:256] = p
            tgo[h] = act[1, pl.ds(pl.multiple_of(64 * c, 64), 64), 0:256]
            tgs[h] = act[1, pl.ds(pl.multiple_of(64 * (1 - c), 64), 64), 0:256]
        swap_tg[hf].start()
        save(tgo.at[pl.ds(3 * hf, 3)], tg.at[c, pl.ds(3 * hf, 3)])

    swap_tg = [
        to_sib(tgs.at[pl.ds(3 * hf, 3)], tg_r.at[pl.ds(3 * hf, 3)]) for hf in range(2)
    ]
    z_up2.wait_recv()
    z_up3 = z_last(half_up, other_up, zs_up, (1, 7, 2))
    start([z_up3])
    z_down2.wait_recv()
    z_down3 = z_last(half_down, other_down, zs_down, (1, 7, 6))
    start([z_down3])
    z_rest2.wait_recv()
    z_rest3 = z_last(half_rest, other_rest, zs_rest, (1, 7, 6))
    start([z_rest3])
    finish_ring(0)
    finish_ring(1)
    wait_recv([z_up3])
    for m in range(4):
        act[0, 48 * (m // 2) : 48 * (m // 2) + 48, HALF * (m % 2) : HALF * (m % 2) + HALF] = zs_up[m].astype(F32)
    for cc, ref in ((c, post_up.at[0]), (1 - c, post_up.at[1])):
        ref[:, 0:D] = rows_of(act, 0, cc)
        ref[:, D : 2 * D] = rows_of(act, 48, cc)
    swap_up = to_sib(post_up.at[1], post_up.at[2])
    swap_up.start()
    for pattern in w1[3:]:
        pattern.sent()
    wait_send(w2 + [z_down1, z_rest1, gain1, gain2])
    first_core = (c == 0).astype(F32)

    def by_core(ref):
        own, got = ref[0], ref[2]
        return own * first_core + got * (1.0 - first_core), got * first_core + own * (1.0 - first_core)

    wait_recv([z_rest3])
    for r in range(3):
        act[0, 96 + 16 * r : 112 + 16 * r, HALF:D] = zs_rest[r].astype(F32)
    gains = unpacked(zs_rest[3].astype(F32))
    wait_recv([z_down3])
    for r in range(3):
        act[0, 96 + 16 * r : 112 + 16 * r, 0:HALF] = zs_down[r, 48:64].astype(F32)
    for i, cc in enumerate((c, 1 - c)):
        post_rest[i, 0:24] = rows_of(act, 96, cc)
        post_rest[i, 24:32] = jnp.concatenate([gains, jnp.zeros((6, D), F32)], axis=0)
    swap_rest = to_sib(post_rest.at[1], post_rest.at[2])
    swap_rest.start()
    for m in range(4):
        rows, cols = slice(48 * (m // 2), 48 * (m // 2) + 48), slice(HALF * (m % 2), HALF * (m % 2) + HALF)
        down_s[rows, cols] = zs_down[m, 0:48].astype(F32)
    save(down_s, d_down)
    for hf in range(2):
        swap_tg[hf].wait_recv()
        save(tg_r.at[pl.ds(3 * hf, 3)], tg.at[1 - c, pl.ds(3 * hf, 3)])
    swap_up.wait_recv()
    pair = by_core(post_up)
    for m in range(4):
        block = jnp.concatenate([p[:, HALF * m : HALF * m + HALF] for p in pair], axis=1).astype(BF)
        up_s_out[:, D * m : D * m + D] = dot_nt(block, perm[...])
    save(up_s_out, d_up)
    swap_rest.wait_recv()
    gsum_s[...] = post_rest[0, 24:32] + post_rest[2, 24:32]
    save(gsum_s, gsum)
    pair = by_core(post_rest)
    for cc in range(2):
        cols = slice(HALF * cc, HALF * cc + HALF)
        two_s[0, :, cols] = pair[cc][0:24, 0:HALF]
        two_s[1, :, cols] = pair[cc][0:24, HALF:D]
    save(two_s.at[0], d_out)
    save(two_s.at[1], d_value)
    for copy in saved:
        copy.wait()
    wait_send(list(up_sent + dn_sent) + swap_tg + [z_up3, z_down3, z_rest3])
    assert pool.used == SEMS, pool.used
    wait_send([swap_ng, swap_up, swap_rest, z_up2, z_down2, z_rest2])


def finish(out, input_grad, d_value, d_out, d_up, d_down, gsum, tg, *outs):
    for src, dst in zip((out, input_grad, d_value, d_out, d_up, d_down, tg), outs):
        dst[...] = src[...]
    s = lax.axis_index("seq")
    row = lax.broadcasted_iota(jnp.int32, (D, 128), 0)
    lane = lax.broadcasted_iota(jnp.int32, (D, 128), 1)
    pick = jnp.where(row == lane + 24 * s, 1.0, 0.0)
    for i in range(2):
        got = jnp.dot(gsum[...], pick, precision=lax.Precision.HIGHEST, preferred_element_type=F32)
        outs[7 + i][...] = got[i, 0:24]


def vmem(*shape, kind=BF):
    return pltpu.VMEM(shape, kind)


IN_VMEM = pl.BlockSpec(memory_space=pltpu.VMEM)
ANY = pl.BlockSpec(memory_space=pl.ANY)


def per_device(tokens, lengths, w_value, w_out, w_up, w_down, gain_mix, gain_ffn, mix_table, out_grad):
    sd = jax.ShapeDtypeStruct
    shapes = [
        sd((2, 64, D), BF), sd((2, 64, D), F32), sd((24, D), F32), sd((24, D), F32), sd((24, 4 * D), F32),
        sd((96, D), F32), sd((8, D), F32), sd((2, HH, 64, 256), F32),
    ]
    raw = pl.pallas_call(
        layer,
        name="layer",
        out_shape=shapes,
        in_specs=[pl.BlockSpec(memory_space=pltpu.SMEM)] + [IN_VMEM] * 8 + [pl.BlockSpec(memory_space=pl.ANY)],
        out_specs=[ANY] * 8,
        scratch_shapes=[
            vmem(D, D), vmem(2, 24, D, kind=F32), vmem(2, 24, D, kind=F32), vmem(2, 24, D, kind=F32), vmem(2, 24, D, kind=F32),
            vmem(2, 2, 64, D), vmem(2, 2, 64, D), vmem(HH, 2, 64, 2048),
            vmem(4, 4, 48, HALF), vmem(2, 4, 4, 48, HALF), vmem(8, 4, 4, 48, HALF),
            vmem(4, 4, ROWS, 128), vmem(4, 4, ROWS, 128), vmem(3, 4, ROWS, 128), vmem(3, 4, ROWS, 128),
            vmem(4, ROWS, 128), vmem(4, ROWS, 128), vmem(3, ROWS, 128), vmem(3, ROWS, 128),
            vmem(2, HALF, 128, kind=F32), vmem(2, 8, 128, kind=F32), vmem(2, 2, 128, HALF), vmem(HH, 144, 128),
            vmem(HH, 128, 128), vmem(2, 128, 128, kind=F32), vmem(256, D), vmem(256, D, kind=F32), vmem(256, D),
            vmem(256, D), vmem(2, 256, D), vmem(2, 256, D), vmem(2, 256, D, kind=F32),
            vmem(2, 2, 64, D, kind=F32), vmem(2, 64, D, kind=F32), vmem(2, 2, 64, D, kind=F32),
            vmem(2, 2, 64, D), vmem(2, 2, 64, D), vmem(2, 2, 64, D, kind=F32),
            vmem(4, 4, 4, 48, HALF), vmem(4, 4, 96, HALF), vmem(4, 4, 96, HALF), vmem(4, 4, 48, HALF), vmem(4, 4, 48, HALF),
            vmem(4, 4, 48, HALF), vmem(4, 4, ROWS, 128), vmem(4, 4, ROWS, 128),
            vmem(2, 3, 4, 96, HALF), vmem(3, 3, 4, 48, HALF), vmem(2, 4, 96, HALF), vmem(3, 4, 48, HALF),
            vmem(2, 3, 96, HALF), vmem(3, 3, 48, HALF),
            vmem(2, 2, 4, 48, HALF), vmem(2, 2, 4, 48, HALF), vmem(2, 2, 4, 48, HALF), vmem(2, 2, 4, 48, HALF),
            vmem(16, HALF), vmem(4, 4, 16, HALF),
            vmem(2, 4, 3, 128, 256), vmem(2, 4, 3, 128, 256), vmem(2, 4, 3, 128, 256), vmem(2, 4, 3, 128, 256),
            vmem(HH, 64, 256, kind=F32), vmem(HH, 64, 256, kind=F32), vmem(2, HALF, 128, kind=F32),
            vmem(2, 2, 64, D, kind=F32), vmem(4, 64, HALF), vmem(64, HALF), vmem(3, 64, HALF), vmem(3, 16, HALF),
            vmem(48, HALF), vmem(64, HALF), vmem(16, HALF), vmem(48, HALF), vmem(64, HALF), vmem(16, HALF),
            vmem(4, 48, HALF), vmem(4, 64, HALF), vmem(4, 16, HALF),
            vmem(3, 24, 2 * D, kind=F32), vmem(3, 32, D, kind=F32), vmem(2, 64, D), vmem(2, 64, D, kind=F32),
            vmem(96, D, kind=F32), vmem(24, 4 * D, kind=F32), vmem(HH, 64, 256, kind=F32),
            vmem(8, D, kind=F32), vmem(2, 24, D, kind=F32),
            pltpu.SemaphoreType.DMA((SEMS,)),
        ],
        compiler_params=pltpu.CompilerParams(
            collective_id=0, has_side_effects=True, vmem_limit_bytes=63 << 20
        ),
    )(lengths, tokens, out_grad, w_value, w_out, w_up, w_down, gain_mix, gain_ffn, mix_table)
    out, input_grad, d_value, d_out, d_up, d_down, tg, mix_gain, ffn_gain = pl.pallas_call(
        finish,
        name="finish",
        out_shape=shapes[:6] + [shapes[7], sd((24,), F32), sd((24,), F32)],
        in_specs=[IN_VMEM] * 8,
        out_specs=[IN_VMEM] * 9,
    )(*raw)
    return (
        out, input_grad, d_value, d_out, d_up, d_down, mix_gain, ffn_gain, tg.reshape(HEADS, 64, 256),
    )


def solution(mesh):
    return jax.shard_map(
        per_device,
        mesh=mesh,
        in_specs=(
            P("dp", "seq", None),
            P("dp"),
            P("seq", None),
            P("seq", None),
            P("seq", None),
            P("seq", None),
            P(),
            P(),
            P(None, "seq", None),
            P("dp", "seq", None),
        ),
        out_specs=(
            P("dp", "seq", None),
            P("dp", "seq", None),
            P("seq", None),
            P("seq", None),
            P("seq", None),
            P("seq", None),
            P("seq"),
            P("seq"),
            P(None, "seq", "dp"),
        ),
        check_vma=False,
    )
```
